32 devices in a mesh: dp: 8 (over y, x, core), tensor: 4 (over z).
Axes of the slice: x: 2, y: 2, z: 4, core: 2. Of those that a mesh axis runs over, the one named last changes fastest.
Arguments:
- stream_in: bfloat16 [16384, 1024], P(('dp', 'tensor')), may hold values from -6 to 6
- timestep: int32 [16], P('dp'), may hold values from 0 to 999
- lengths: int32 [16], P('dp'), may hold values from 1 to 1024, 12288 in all
- time_weight: bfloat16 [1024, 1024], replicated, may hold values from -0.1875 to 0.1875
- time_bias: float32 [1024], replicated, may hold values from -3 to 3
- triple_weight: bfloat16 [1024, 3, 1024], P(None, None, 'tensor'), may hold values from -0.1875 to 0.1875
- query_value_bias: float32 [2, 1024], P(None, 'tensor'), may hold values from -3 to 3
- output_weight: bfloat16 [1024, 1024], P('tensor'), may hold values from -0.75 to 0.75
- output_bias: float32 [1024], replicated, may hold values from -2 to 2
- first_gain: float32 [1024], replicated, may hold values from 0.5 to 1.5
- first_shift: float32 [1024], replicated, may hold values from -2 to 2
- up_weight: bfloat16 [1024, 4096], P(None, 'tensor'), may hold values from -0.1875 to 0.1875
- up_bias: float32 [4096], P('tensor'), may hold values from -3 to 3
- down_weight: bfloat16 [4096, 1024], P('tensor'), may hold values from -0.09375 to 0.09375
- down_bias: float32 [1024], replicated, may hold values from -2 to 2
- second_gain: float32 [1024], replicated, may hold values from 0.5 to 1.5
- second_shift: float32 [1024], replicated, may hold values from -2 to 2
- cotangent: bfloat16 [16384, 1024], P(('dp', 'tensor')), may hold values from -6 to 6
Outputs:
- block_output: bfloat16 [16384, 1024], P(('dp', 'tensor'))
- input_gradient: bfloat16 [16384, 1024], P(('dp', 'tensor'))
- root_squares: float32 [16, 3], P('dp')
- time_weight_gradient: float32 [1024, 1024], replicated
- time_bias_gradient: float32 [1024], replicated
- triple_weight_gradient: float32 [1024, 3, 1024], P(None, None, 'tensor')
- query_value_bias_gradient: float32 [2, 1024], P(None, 'tensor')
- output_weight_gradient: float32 [1024, 1024], P('tensor')
- output_bias_gradient: float32 [1024], replicated
- first_gain_gradient: float32 [1024], replicated
- first_shift_gradient: float32 [1024], replicated
- up_weight_gradient: float32 [1024, 4096], P(None, 'tensor')
- up_bias_gradient: float32 [4096], P('tensor')
- down_weight_gradient: float32 [4096, 1024], P('tensor')
- down_bias_gradient: float32 [1024], replicated
- second_gain_gradient: float32 [1024], replicated
- second_shift_gradient: float32 [1024], replicated
The draws below stay inside these ranges and needn't reach their ends.
Inputs may be any that keep to these rules, and one draw needn't show every extreme that they name: lengths[s] valid tokens stand at the start of sequence s; some sequence has all 1024 valid.
All inputs are finite; a program needn't handle non-finite values. No bound on the sum of `lengths` on one device may be relied on, other than what follows from the above.
Results may differ from the reference program's by a relative error of at most 0.025.
Values may be sent and summed in bfloat16 or wider, within the bound.
A program may use at most 128 MiB of HBM per device.

```python
import math
import jax
import jax.numpy as jnp
import numpy as np
from jax import lax

D = 1024
H = 16
HD = 64
FF = 4096
LEN = 1024
SEQS = 16
TOKENS = 16384


def touch_ends(values, rng, smallest, top_value):
    longest = values.shape.index(max(values.shape))
    spots = []
    for shift in (0, 1):
        where = [jax.random.randint(jax.random.fold_in(rng, axis), (), 0, length) for axis, length in enumerate(values.shape)]
        where[longest] = (where[longest] + shift) % values.shape[longest]
        spots.append(tuple(where))
    return values.at[spots[0]].set(smallest).at[spots[1]].set(top_value)


def levels(rng, extent, shards, low, high):
    factor_of, own = 1.0, jax.random.fold_in(rng, 6)
    for dim, blocks in shards:
        heights = jnp.exp(jax.random.uniform(jax.random.fold_in(own, dim), (blocks,), jnp.float32, low / len(shards), high / len(shards)))
        factor_of = factor_of * jnp.repeat(heights, extent[dim] // blocks).reshape([-1 if axis == dim else 1 for axis in range(len(extent))])
    return factor_of


def split_up(amount, total, reach, slope):
    loads = [(1 << 20) // math.isqrt(rank ** slope) + 1 for rank in range(2, amount + 1)]
    surplus, given = total - reach - (amount - 1), [1] * (amount - 1)
    while surplus > 0:
        free = [i for i in range(amount - 1) if given[i] < reach]
        pool, left = sum([loads[i] for i in free]), surplus
        for i in free:
            extra = min(reach - given[i], max(1, left * loads[i] // pool), surplus)
            given[i] = given[i] + extra
            surplus = surplus - extra
    return np.array([reach] + given)


def uneven(stream_key, count, total, most, skew):
    if count == 2:
        one = jax.random.randint(stream_key, (), max(1, total - most), min(most, total - 1) + 1)
        return jnp.stack([one, total - one])
    sizes = jnp.asarray(split_up(count, total, most, skew), jnp.int32)
    twos = (count - 1) // 2
    source_of, receiver = sizes[1:1 + 2 * twos:2], sizes[2:2 + 2 * twos:2]
    margin = jnp.minimum(source_of - 1, most - receiver)
    passed = jax.random.randint(jax.random.fold_in(stream_key, 1), (twos,), 0, 1 << 20) % (margin + 1)
    sizes = sizes.at[1:1 + 2 * twos:2].set(source_of - passed).at[2:2 + 2 * twos:2].set(receiver + passed)
    return sizes[jax.random.permutation(jax.random.fold_in(stream_key, 2), count)]


def scatter_about(own_key, extent, scale, bound, split=(), dtype=jnp.bfloat16):
    level = levels(own_key, extent, split, -0.22, 0.18) if split else 1.0
    array = jax.random.normal(own_key, extent, jnp.float32) * scale * level
    return jnp.minimum(jnp.maximum(array, -bound), bound).astype(dtype)


def setup_inputs(seed: int = 0) -> dict:
    key_list = jax.random.split(jax.random.key(seed), 19)
    stream_in = scatter_about(key_list[0], (TOKENS, D), 1.0, 6.0, ((0, 32),))
    timestep = touch_ends(jax.random.randint(key_list[1], (SEQS,), 0, 1000), jax.random.fold_in(key_list[1], 1), 0, 999).astype(jnp.int32)
    lengths = uneven(key_list[2], SEQS, SEQS * LEN * 3 // 4, LEN, 2).astype(jnp.int32)
    time_weight = scatter_about(key_list[3], (D, D), D ** -0.5, 0.1875)
    time_bias = scatter_about(key_list[4], (D,), 0.5, 3.0, (), jnp.float32)
    triple_weight = scatter_about(key_list[5], (D, 3, D), D ** -0.5, 0.1875, ((2, 4),))
    query_value_bias = scatter_about(key_list[6], (2, D), 0.5, 3.0, ((1, 4),), jnp.float32)
    output_weight = scatter_about(key_list[7], (D, D), (D // 16) ** -0.5, 0.75, ((0, 4),))
    output_bias = scatter_about(key_list[8], (D,), 0.3, 2.0, (), jnp.float32)
    first_gain = jnp.clip(1.0 + 0.1 * jax.random.normal(key_list[9], (D,), jnp.float32), 0.5, 1.5)
    first_shift = scatter_about(key_list[10], (D,), 0.3, 2.0, (), jnp.float32)
    up_weight = scatter_about(key_list[11], (D, FF), D ** -0.5, 0.1875, ((1, 4),))
    up_bias = scatter_about(key_list[12], (FF,), 0.5, 3.0, ((0, 4),), jnp.float32)
    down_weight = scatter_about(key_list[13], (FF, D), FF ** -0.5, 0.09375, ((0, 4),))
    down_bias = scatter_about(key_list[14], (D,), 0.3, 2.0, (), jnp.float32)
    second_gain = jnp.clip(1.0 + 0.1 * jax.random.normal(key_list[15], (D,), jnp.float32), 0.5, 1.5)
    second_shift = scatter_about(key_list[16], (D,), 0.3, 2.0, (), jnp.float32)
    cotangent = scatter_about(key_list[17], (TOKENS, D), 1.0, 6.0, ((0, 32),))
    return dict(stream_in=stream_in, timestep=timestep, lengths=lengths, time_weight=time_weight, time_bias=time_bias, triple_weight=triple_weight, query_value_bias=query_value_bias, output_weight=output_weight, output_bias=output_bias, first_gain=first_gain, first_shift=first_shift, up_weight=up_weight, up_bias=up_bias, down_weight=down_weight, down_bias=down_bias, second_gain=second_gain, second_shift=second_shift, cotangent=cotangent)


@jax.custom_vjp
def low(v):
    return lax.optimization_barrier(v.astype(jnp.bfloat16)).astype(jnp.float32)

@jax.custom_vjp
def low_back(v):
    return v

def low_keep(v):
    return (low(v), None)

def low_pass(kept, grad):
    return (grad,)

def back_keep(v):
    return (v, None)

def back_low(kept, grad):
    return (low(grad),)
low.defvjp(low_keep, low_pass)
low_back.defvjp(back_keep, back_low)
NORM_EPS = 1e-05
STAT_EPS = 1e-06
MASKED = -1e+30

def precise(left, right):
    return jnp.dot(left, right, precision=lax.Precision.HIGHEST, preferred_element_type=jnp.float32)

def sinusoid(steps, width):
    half = width // 2
    rates = jnp.exp(-math.log(10000.0) * jnp.arange(half).astype(jnp.float32) / half)
    angles = steps.astype(jnp.float32)[:, None] * rates[None, :]
    return jnp.concatenate([jnp.sin(angles), jnp.cos(angles)], axis=1)

def layer_norm(total, gain, shift):
    middle = lax.optimization_barrier(jnp.mean(total, axis=-1, keepdims=True))
    centred = total - middle
    spread = lax.optimization_barrier(jnp.mean(centred * centred, axis=-1, keepdims=True))
    return centred * lax.rsqrt(spread + NORM_EPS) * gain + shift

def gaussian_unit(value):
    return 0.5 * value * (1.0 + jax.scipy.special.erf(value * (1.0 / math.sqrt(2.0))))

def attend(pack):
    query, keys, values, limit = pack
    scores = low_back(HD ** (-0.5) * jnp.einsum('qhd,khd->hqk', query, keys, precision=lax.Precision.HIGHEST))
    allowed = jnp.arange(LEN) < limit
    scores = jnp.where(allowed[None, None, :], scores, MASKED)
    probs = low(jax.nn.softmax(scores, axis=-1))
    return jnp.einsum('hqk,khd->qhd', probs, values, precision=lax.Precision.HIGHEST)

def forward(params, rows_in, steps, limits):
    time_weight, time_bias, triple_weight, query_value_bias, output_weight, output_bias, first_gain, first_shift, up_weight, up_bias, down_weight, down_bias, second_gain, second_shift = params
    count = steps.shape[0]
    embedded = low(sinusoid(steps, D))
    shift = precise(embedded, time_weight) + time_bias
    stream = (rows_in.reshape(count, LEN, D) + shift[:, None, :]).reshape(count * LEN, D)
    stream_low = low(stream)
    bias_full = jnp.concatenate([query_value_bias[0], jnp.zeros((D,), jnp.float32), query_value_bias[1]])
    projected = low_back(low(precise(stream_low, triple_weight.reshape(D, 3 * D)) + bias_full))
    projected = projected.reshape(count, LEN, 3, H, HD)
    context = lax.map(jax.checkpoint(attend), (projected[:, :, 0], projected[:, :, 1], projected[:, :, 2], limits))
    context = low_back(low(context.reshape(count * LEN, D)))
    branch = low_back(precise(context, output_weight) + output_bias)
    middle = layer_norm(stream + branch, first_gain, first_shift)
    before = low_back(precise(low(middle), up_weight) + up_bias)
    active = low(gaussian_unit(before))
    feed = low_back(precise(active, down_weight) + down_bias)
    result = layer_norm(middle + feed, second_gain, second_shift)
    return (result, (stream, branch, feed))

def statistics(parts, limits):
    count = limits.shape[0]
    allowed = (jnp.arange(LEN)[None, :] < limits[:, None]).astype(jnp.float32)
    sums = [lax.optimization_barrier(jnp.sum(lax.optimization_barrier(jnp.sum((part * part).reshape(count, LEN, D), axis=2)) * allowed, axis=1)) for part in parts]
    table = jnp.stack(sums, axis=1)
    return jnp.sqrt(table / (limits.astype(jnp.float32)[:, None] * D) + STAT_EPS)

def reference(stream_in, timestep, lengths, time_weight, time_bias, triple_weight, query_value_bias, output_weight, output_bias, first_gain, first_shift, up_weight, up_bias, down_weight, down_bias, second_gain, second_shift, cotangent):
    params = (time_weight.astype(jnp.float32), time_bias.astype(jnp.float32), triple_weight.astype(jnp.float32), query_value_bias.astype(jnp.float32), output_weight.astype(jnp.float32), output_bias.astype(jnp.float32), first_gain.astype(jnp.float32), first_shift.astype(jnp.float32), up_weight.astype(jnp.float32), up_bias.astype(jnp.float32), down_weight.astype(jnp.float32), down_bias.astype(jnp.float32), second_gain.astype(jnp.float32), second_shift.astype(jnp.float32))
    together = math.gcd(SEQS, max(1, 4096 // LEN))
    groups = SEQS // together
    rows_in = stream_in.astype(jnp.float32).reshape(groups, together * LEN, D)
    incoming = cotangent.astype(jnp.float32).reshape(groups, together * LEN, D)

    def one_group(totals, pack):
        rows_group, steps_group, limits_group, incoming_group = pack

        def local(weights, rows_value):
            return forward(weights, rows_value, steps_group, limits_group)
        result, pull, parts = jax.vjp(local, params, rows_group, has_aux=True)
        weight_grads, row_grads = pull(incoming_group)
        totals = jax.tree.map(jnp.add, totals, weight_grads)
        return (totals, (result.astype(jnp.bfloat16), row_grads.astype(jnp.bfloat16), statistics(parts, limits_group)))
    zero = jax.tree.map(jnp.zeros_like, params)
    totals, (outputs, row_grads, table) = lax.scan(one_group, zero, (rows_in, timestep.reshape(groups, together), lengths.reshape(groups, together), incoming))
    grad_time_weight, grad_time_bias, grad_triple, grad_query_value, grad_output_weight, grad_output_bias, grad_first_gain, grad_first_shift, grad_up_weight, grad_up_bias, grad_down_weight, grad_down_bias, grad_second_gain, grad_second_shift = totals
    return (outputs.reshape(TOKENS, D), row_grads.reshape(TOKENS, D), table.reshape(SEQS, 3), grad_time_weight, grad_time_bias, grad_triple, grad_query_value, grad_output_weight, grad_output_bias, grad_first_gain, grad_first_shift, grad_up_weight, grad_up_bias, grad_down_weight, grad_down_bias, grad_second_gain, grad_second_shift)
```

```python
import functools
import math

import jax
import jax.numpy as jnp
from jax import lax
from jax.experimental import pallas as pl
from jax.experimental.pallas import tpu as pltpu
from jax.sharding import Mesh
from jax.sharding import PartitionSpec as P

HD = 64
LEN = 1024
NORM_EPS = 1e-05
STAT_EPS = 1e-06
MASKED = -1e30
LOW = jnp.bfloat16
F32 = jnp.float32
NT = (((1,), (1,)), ((), ()))
TN = (((0,), (0,)), ((), ()))


def sinusoid(steps, width):
    half = width // 2
    rates = jnp.exp(-math.log(10000.0) * jnp.arange(half).astype(F32) / half)
    angles = steps.astype(F32)[:, None] * rates[None, :]
    return jnp.concatenate([jnp.sin(angles), jnp.cos(angles)], axis=1)


def plain(left, right):
    return jnp.dot(left, right, preferred_element_type=F32)


def inner(left, right):
    return lax.dot_general(left, right, TN, preferred_element_type=F32)


def against(left, right):
    return lax.dot_general(left, right, NT, preferred_element_type=F32)


def norm_forward(total, gain, shift):
    middle = jnp.mean(total, axis=-1, keepdims=True)
    centred = total - middle
    spread = jnp.mean(centred * centred, axis=-1, keepdims=True)
    factor = lax.rsqrt(spread + NORM_EPS)
    normed = centred * factor
    return (normed * gain + shift, normed, factor)


def norm_backward(upstream, normed, factor, gain):
    pushed = upstream * gain
    first = jnp.mean(pushed, axis=-1, keepdims=True)
    second = jnp.mean(pushed * normed, axis=-1, keepdims=True)
    return (
        factor * (pushed - first - normed * second),
        jnp.sum(upstream * normed, axis=0),
        jnp.sum(upstream, axis=0),
    )


def split3(x):
    hi = x.astype(LOW)
    rest = x - hi.astype(F32)
    mid = rest.astype(LOW)
    return hi, mid, (rest - mid.astype(F32)).astype(LOW)


def extra_lanes(parts, one, count):
    lane = lax.broadcasted_iota(jnp.int32, (count, HD), 1)
    out = jnp.where(lane == len(parts), 1.0, 0.0) if one else jnp.zeros((count, HD), F32)
    for index, part in enumerate(parts):
        out = jnp.where(lane == index, jnp.broadcast_to(part.astype(F32), (count, HD)), out)
    return out.astype(LOW)


def head(x, h):
    return x[:, h * HD : (h + 1) * HD]


def attend_kernel(rows, mask_ref, q_ref, k_ref, v_ref, context_ref, log_ref):
    count = q_ref.shape[0]
    mask = mask_ref[...]
    keys = k_ref[...].astype(LOW)
    values = v_ref[...].astype(LOW)
    for start in range(0, count, rows):
        part = slice(start, start + rows)
        queries = q_ref[part].astype(LOW) * LOW(HD**-0.5)
        contexts, logs = [], []
        for h in range(2):
            scores = lax.dot_general(
                head(queries, h), head(keys, h), NT, preferred_element_type=F32
            )
            scores = scores + mask
            highest = jnp.max(scores, axis=1, keepdims=True)
            probs = jnp.exp(scores - highest)
            total = jnp.sum(probs, axis=1, keepdims=True)
            contexts.append(plain(probs.astype(LOW), head(values, h)) / total)
            logs.append(jnp.broadcast_to(highest + jnp.log(total), (rows, HD)))
        context_ref[part] = jnp.concatenate(contexts, axis=1)
        log_ref[part] = jnp.concatenate(logs, axis=1)


def attend(projected, mask_row):
    count, width = projected.shape
    local = width // 3
    pairs = local // (2 * HD)
    block = lambda which: pl.BlockSpec((count, 2 * HD), lambda p: (0, which * pairs + p))
    return pl.pallas_call(
        functools.partial(attend_kernel, 512),
        grid=(pairs,),
        in_specs=[pl.BlockSpec((1, count), lambda p: (0, 0)), block(0), block(1), block(2)],
        out_specs=[block(0)] * 2,
        out_shape=[jax.ShapeDtypeStruct((count, local), F32)] * 2,
        compiler_params=pltpu.CompilerParams(vmem_limit_bytes=40 << 20),
        cost_estimate=pl.CostEstimate(
            flops=16 * count * count * local,
            bytes_accessed=20 * count * local,
            transcendentals=count * count * local // HD,
        ),
    )(mask_row, projected, projected, projected)


def attend_back_kernel(
    rows, mask_ref, q_ref, k_ref, v_ref, context_ref, log_ref, grad_ref, dq_ref, dk_ref, dv_ref
):
    count = k_ref.shape[0]
    lane = lax.broadcasted_iota(jnp.int32, (count, HD), 1)
    three = jnp.where(lane < 3, 1.0, 0.0)
    key_extra = jnp.where(lane == 3, jnp.broadcast_to(mask_ref[...], (count, HD)), three)
    key_extra = key_extra.astype(LOW)
    value_extra = three.astype(LOW)
    queries = q_ref[...].astype(LOW) * LOW(HD**-0.5)
    keys = k_ref[...].astype(LOW)
    values = v_ref[...].astype(LOW)
    logs = log_ref[...]
    grads = grad_ref[...]
    dots = grads * context_ref[...]
    grads = grads.astype(LOW)
    kx, vx, qx, gx, dq = [], [], [], [], [None, None]
    for h in range(2):
        extra = extra_lanes(split3(-logs[:, h * HD : h * HD + 1]), True, count)
        qx.append(jnp.concatenate([head(queries, h), extra], axis=1))
        row_dot = jnp.sum(head(dots, h), axis=1, keepdims=True)
        extra = extra_lanes(split3(-row_dot), False, count)
        gx.append(jnp.concatenate([head(grads, h), extra], axis=1))
        kx.append(jnp.concatenate([head(keys, h), key_extra], axis=1))
        vx.append(jnp.concatenate([head(values, h), value_extra], axis=1))
    for start in range(0, count, rows):
        part = slice(start, start + rows)
        dk, dv = [], []
        for h in range(2):
            probs = jnp.exp(lax.dot_general(kx[h][part], qx[h], NT, preferred_element_type=F32))
            pushed = lax.dot_general(vx[h][part], gx[h], NT, preferred_element_type=F32)
            scores_grad = (probs * pushed).astype(LOW)
            dv.append(plain(probs.astype(LOW), gx[h])[:, :HD])
            dk.append(plain(scores_grad, qx[h])[:, :HD])
            more = lax.dot_general(scores_grad, kx[h][part], TN, preferred_element_type=F32)
            dq[h] = more if start == 0 else dq[h] + more
        dk_ref[part] = jnp.concatenate(dk, axis=1)
        dv_ref[part] = jnp.concatenate(dv, axis=1)
    dq_ref[...] = jnp.concatenate([x[:, :HD] for x in dq], axis=1) * HD**-0.5


def attend_back(projected, mask_column, context, log_total, grad):
    count, width = projected.shape
    local = width // 3
    pairs = local // (2 * HD)
    block = lambda which: pl.BlockSpec((count, 2 * HD), lambda p: (0, which * pairs + p))
    return pl.pallas_call(
        functools.partial(attend_back_kernel, 512),
        grid=(pairs,),
        in_specs=[pl.BlockSpec((count, 1), lambda p: (0, 0)), block(0), block(1), block(2)]
        + [block(0)] * 3,
        out_specs=[block(0)] * 3,
        out_shape=[jax.ShapeDtypeStruct((count, local), F32)] * 3,
        compiler_params=pltpu.CompilerParams(vmem_limit_bytes=50 << 20),
        cost_estimate=pl.CostEstimate(
            flops=40 * count * count * local,
            bytes_accessed=40 * count * local,
            transcendentals=count * count * local // HD,
        ),
    )(mask_column, projected, projected, projected, context, log_total, grad)


def gaussian_pair(value):
    cumulative = 0.5 * (1.0 + jax.scipy.special.erf(value * (1.0 / math.sqrt(2.0))))
    slope = cumulative + value * jnp.exp(-0.5 * value * value) * (1.0 / math.sqrt(2.0 * math.pi))
    return (value * cumulative).astype(LOW), slope.astype(LOW)


def on_device(
    plane,
    stream_in,
    timestep,
    lengths,
    time_weight,
    time_bias,
    triple_weight,
    query_value_bias,
    output_weight,
    output_bias,
    first_gain,
    first_shift,
    up_weight,
    up_bias,
    down_weight,
    down_bias,
    second_gain,
    second_shift,
    cotangent,
):
    rows, width = stream_in.shape
    seq_dev = timestep.shape[0]
    tensor = lax.axis_size("tensor")
    subs = tensor // seq_dev
    local = triple_weight.shape[2]
    units = up_weight.shape[1]
    half_units = units // 2
    quarters = 2 ** len(plane)
    piece_units = half_units // quarters
    me = lax.axis_index("tensor")
    core = lax.axis_index("core")
    spot = lax.axis_index(plane)
    sub = me % subs
    which = me // subs
    offsets = [(k, j) for k in range(subs) for j in range(seq_dev)]
    others = offsets[1:]

    def member(i, k, j):
        return ((i // subs + j) % seq_dev) * subs + (i % subs + k) % subs

    def fetch(x, k, j):
        return lax.ppermute(x, "tensor", [(member(i, k, j), i) for i in range(tensor)])

    def send(x, k, j):
        return lax.ppermute(x, "tensor", [(i, member(i, k, j)) for i in range(tensor)])

    def swap(x, axis):
        return lax.ppermute(x, axis, [(0, 1), (1, 0)])

    def across(x, mask):
        return lax.ppermute(x, plane, [(i, i ^ mask) for i in range(quarters)])

    def pick(x, index, axis=0):
        return lax.dynamic_index_in_dim(x, index, axis, keepdims=False)

    def ordered(parts, index):
        parts = jnp.stack(parts) if isinstance(parts, (list, tuple)) else parts
        return jnp.stack([pick(parts, index ^ m) for m in range(parts.shape[0])])

    small = jnp.concatenate([up_bias, query_value_bias.reshape(-1)])
    small_of = {(0, 0): small}
    for k, j in others:
        small_of[(k, j)] = fetch(small, k, j)

    raw = [stream_in] + [fetch(stream_in, k, 0) for k in range(1, subs)]
    seq_in = jnp.concatenate(raw, axis=0)
    embedded_own = sinusoid(timestep, width).astype(LOW)
    shift_own = plain(embedded_own, time_weight) + time_bias
    shift_row = pick(shift_own, which)
    limit = pick(lengths, which)
    stream = stream_in.astype(F32) + shift_row
    stream_low = (seq_in.astype(F32) + shift_row).astype(LOW)
    place = (jnp.arange(LEN, dtype=jnp.int32) + sub * rows) % LEN
    mask = jnp.where(place < limit, 0.0, MASKED).astype(F32)
    mask_row, mask_column = mask[None, :], mask[:, None]
    valid = (place[:rows] < limit).astype(F32)

    triple_own = triple_weight.reshape(width, 3 * local)
    part = width // (2 * quarters)

    def whole(piece):
        got = jnp.stack([piece] + [across(piece, mask) for mask in range(1, quarters)])
        other = swap(got, "core")
        first = jnp.where(core == 0, got, other)
        second = jnp.where(core == 0, other, got)
        return ordered(jnp.stack([first, second], axis=1), spot)

    triples = [triple_own]
    for j in range(1, seq_dev):
        share = lax.dynamic_slice_in_dim(triple_own, (2 * spot + core) * part, part, 0)
        share = fetch(share, 0, j)
        triples.append(whole(share).reshape(width, 3 * local))

    up_half = lax.dynamic_slice_in_dim(up_weight, core * half_units, half_units, 1).T
    down_half = lax.dynamic_slice_in_dim(down_weight, core * half_units, half_units, 0)

    def spread_units(x, straight):
        mine = ordered(x.reshape((quarters, piece_units) + x.shape[1:]), spot)
        got = jnp.stack([fetch(mine[0], k, j) for k, j in others])[None]
        names = list(enumerate(reversed(plane)))
        if straight:
            for _, name in names:
                got = jnp.concatenate([got, swap(got, name)], axis=0)
        else:
            for _, name in reversed(names):
                got = jnp.concatenate([got, swap(got, name)], axis=0)
            shape = got.shape
            got = got.reshape((2,) * len(plane) + shape[1:])
            got = got.transpose(tuple(reversed(range(len(plane)))) + tuple(range(len(plane), got.ndim)))
            got = got.reshape(shape)
        return jnp.concatenate([mine[:, None], got], axis=1)

    out_part = local // (2 * quarters)
    out_share = lax.dynamic_slice_in_dim(
        output_weight, (2 * spot + core) * out_part, out_part, 0
    )
    out_got = jnp.stack([fetch(out_share, k, j) for k, j in others])
    out_all = whole(out_got)
    out_all = out_all.transpose(2, 0, 1, 3, 4).reshape(tensor - 1, local, width)
    out_full = jnp.concatenate([output_weight[None], out_all]).reshape(tensor * local, width)

    qv = [small_of[(0, j)][units:].reshape(2, local) for j in range(seq_dev)]
    projected, context, log_total = [], [], []
    for j in range(seq_dev):
        bias = jnp.concatenate([qv[j][0], jnp.zeros((local,), F32), qv[j][1]])
        projected.append(plain(stream_low, triples[j]) + bias)
        here = attend(projected[j], mask_row)
        context.append(here[0])
        log_total.append(here[1])
    block = lambda x, k: x[k * rows : (k + 1) * rows]
    columns = []
    for k in range(subs):
        back = (subs - k) % subs
        for j in range(seq_dev):
            mine = block(context[j], back).astype(LOW)
            columns.append(mine if k == 0 else send(mine, back, 0))
    context_own = jnp.concatenate(columns, axis=1)
    branch = plain(context_own, out_full) + output_bias
    middle, normed_first, factor_first = norm_forward(stream + branch, first_gain, first_shift)
    middle_low = middle.astype(LOW)

    up_rows = spread_units(up_half, True).reshape(quarters * tensor * piece_units, width)
    down_rows = spread_units(down_half, False).reshape(quarters * tensor * piece_units, width)
    bias_all = jnp.stack([small_of[o][:units] for o in offsets])
    bias_half = lax.dynamic_slice_in_dim(bias_all, core * half_units, half_units, 1)
    bias_rel = ordered(
        bias_half.reshape(tensor, quarters, piece_units).transpose(1, 0, 2), spot
    ).reshape(-1)
    both = jnp.concatenate([middle_low, swap(middle_low, "core")], axis=0)
    active, slope = gaussian_pair(against(both, up_rows) + bias_rel)
    feed_other = plain(active[rows:], down_rows).astype(LOW)
    feed = plain(active[:rows], down_rows) + swap(feed_other, "core").astype(F32) + down_bias
    result, normed_second, factor_second = norm_forward(middle + feed, second_gain, second_shift)
    block_output = result.astype(LOW)

    to_second, grad_second_gain, grad_second_shift = norm_backward(
        cotangent.astype(F32), normed_second, factor_second, second_gain
    )
    feed_grad = to_second.astype(LOW)
    grad_down_bias = jnp.sum(feed_grad.astype(F32), axis=0)
    feed_grad_both = jnp.concatenate([feed_grad, swap(feed_grad, "core")], axis=0)

    def reduce_units(total, straight):
        total = total.reshape((2,) * len(plane) + (tensor, piece_units, width))
        axes = list(range(len(plane)))
        left = len(plane)
        order = axes if straight else axes[::-1]
        for axis in order:
            name = plane[axis]
            at = axis if not straight else 0
            keep = lax.index_in_dim(total, 0, at, keepdims=False)
            away = lax.index_in_dim(total, 1, at, keepdims=False)
            total = (keep.astype(F32) + swap(away, name).astype(F32)).astype(LOW)
            left -= 1
        summed = total[0].astype(F32)
        for index, (k, j) in enumerate(offsets):
            if index:
                summed = summed + send(total[index], k, j).astype(F32)
        got = summed.astype(LOW)[None]
        names = list(reversed(plane))
        if straight:
            for name in names:
                got = jnp.concatenate([got, swap(got, name)], axis=0)
        else:
            for name in reversed(names):
                got = jnp.concatenate([got, swap(got, name)], axis=0)
            shape = got.shape
            got = got.reshape((2,) * len(plane) + shape[1:])
            got = got.transpose(tuple(reversed(range(len(plane)))) + tuple(range(len(plane), got.ndim)))
            got = got.reshape(shape)
        got = ordered(got, spot)
        other = swap(got, "core")
        first = jnp.where(core == 0, got, other)
        second = jnp.where(core == 0, other, got)
        return jnp.stack([first, second]).reshape(units, width)

    down_total = inner(active, feed_grad_both).astype(LOW)
    grad_down_weight = reduce_units(down_total, False).astype(F32)
    before_grad = (against(feed_grad_both, down_rows) * slope.astype(F32)).astype(LOW)
    up_total = inner(before_grad, both).astype(LOW)
    grad_up_weight = reduce_units(up_total, True).T.astype(F32)
    grad_up_rel = jnp.sum(before_grad.astype(F32), axis=0)
    middle_other = plain(before_grad[rows:], up_rows).astype(LOW)
    middle_grad = (
        to_second + plain(before_grad[:rows], up_rows) + swap(middle_other, "core").astype(F32)
    )

    to_first, grad_first_gain, grad_first_shift = norm_backward(
        middle_grad, normed_first, factor_first, first_gain
    )
    branch_grad = to_first.astype(LOW)
    grad_output_bias = jnp.sum(branch_grad.astype(F32), axis=0)
    context_grad = against(branch_grad, out_full).astype(LOW)

    def reduce_rows(total, sends):
        count, deep, wide = total.shape
        fine = deep // (2 * quarters)
        shaped = total.reshape(count, quarters, 2, fine, wide)
        keep = pick(shaped, core, 2)
        away = pick(shaped, 1 - core, 2)
        total = (keep.astype(F32) + swap(away, "core").astype(F32)).astype(LOW)
        summed = pick(total, spot, 1).astype(F32)
        for mask in range(1, quarters):
            summed = summed + across(pick(total, spot ^ mask, 1), mask).astype(F32)
        total = summed.astype(LOW)
        summed = total[0].astype(F32)
        for index, (k, j) in enumerate(sends):
            if index:
                summed = summed + send(total[index], k, j).astype(F32)
        return whole(summed.astype(LOW)).reshape(deep, wide)

    out_total = inner(context_own, branch_grad).astype(LOW).reshape(tensor, local, width)
    grad_output_weight = reduce_rows(out_total, offsets).astype(F32)

    wide = subs * seq_dev
    shaped = context_grad.reshape(rows, subs, seq_dev, local)
    triple_total, grads = [], []
    for j in range(seq_dev):
        parts = []
        for k in range(subs):
            back = (subs - k) % subs
            mine = shaped[:, back, j]
            parts.append(mine if k == 0 else send(mine, back, 0))
        incoming = jnp.concatenate(parts, axis=0).astype(F32)
        here = attend_back(projected[j], mask_column, context[j], log_total[j], incoming)
        grads.append(jnp.concatenate(here, axis=1).astype(LOW))
    stream_grad = to_first
    for k in range(1, subs):
        away = sum(against(block(grads[j], k), triples[j]) for j in range(seq_dev))
        stream_grad = stream_grad + send(away.astype(LOW), k, 0).astype(F32)
    stream_grad = stream_grad + sum(
        against(block(grads[j], 0), triples[j]) for j in range(seq_dev)
    )
    input_gradient = stream_grad.astype(LOW)
    triple_total = jnp.stack([inner(stream_low, grads[j]).astype(LOW) for j in range(seq_dev)])
    grad_triple = reduce_rows(triple_total, [(0, j) for j in range(seq_dev)])
    grad_triple = grad_triple.astype(F32).reshape(width, 3, local)

    dp_index = spot * 2 + core
    seqs = quarters * 2 * seq_dev
    column_sums = [jnp.sum(grads[j].astype(F32), axis=0) for j in range(seq_dev)]
    shift_part = jnp.sum(to_first, axis=0) + sum(
        against(column_sums[j][None].astype(F32), triples[j].astype(F32))[0]
        for j in range(seq_dev)
    )
    hot = (jnp.arange(seqs) == dp_index * seq_dev + which).astype(F32)
    shift_rows = hot[:, None] * shift_part[None, :]
    squares = jnp.stack([jnp.sum(jnp.sum(x * x, axis=1) * valid) for x in (stream, branch, feed)])
    table = hot[:, None] * squares[None, :]
    steps_hot = (
        jnp.arange(seqs)[:, None] == dp_index * seq_dev + jnp.arange(seq_dev)[None, :]
    ).astype(F32)
    steps = jnp.sum(steps_hot * timestep.astype(F32)[None, :], axis=1) * (me == 0)
    up_canonical = ordered(grad_up_rel.reshape(quarters, tensor, piece_units), spot)
    up_canonical = up_canonical.transpose(1, 0, 2).reshape(tensor, half_units)
    full_up = jnp.zeros((tensor, 2, half_units), F32)
    full_qv = jnp.zeros((tensor, 2, local), F32)
    for index, (k, j) in enumerate(offsets):
        at = ((which + j) % seq_dev) * subs + (sub + k) % subs
        row = jnp.where(jnp.arange(2)[:, None] == core, up_canonical[index][None], 0.0)
        full_up = lax.dynamic_update_slice_in_dim(full_up, row[None], at, 0)
        if k == 0:
            value = column_sums[j].reshape(3, local)
            value = jnp.stack([value[0], value[2]])
            full_qv = lax.dynamic_update_slice_in_dim(full_qv, value[None], at, 0)

    def everywhere(x):
        x = x + swap(x, "core")
        x = x + sum(across(x, mask) for mask in range(1, quarters))
        return x + sum(fetch(x, k, j) for k, j in others)

    early = jnp.concatenate(
        [
            grad_first_gain,
            grad_first_shift,
            grad_output_bias,
            grad_down_bias,
            grad_second_gain,
            grad_second_shift,
            full_up.reshape(-1),
            table.reshape(-1),
            steps,
        ]
    )
    size = early.shape[0]
    early = jnp.pad(early, (0, -size % width)).reshape(-1, width)
    early = everywhere(early).reshape(-1)
    cut = [width] * 6 + [2 * tensor * half_units, 3 * seqs, seqs]
    got, at = [], 0
    for length in cut:
        got.append(early[at : at + length])
        at += length
    full_up = pick(got[6].reshape(tensor, units), me)
    table, steps = got[7].reshape(seqs, 3), got[8]
    late = everywhere(jnp.concatenate([shift_rows.reshape(-1), full_qv.reshape(-1)]).reshape(-1, width))
    late = late.reshape(-1)
    shift_grad = late[: seqs * width].reshape(seqs, width)
    grad_query_value = pick(late[seqs * width :].reshape(tensor, 2, local), me)
    grad_time_bias = jnp.sum(shift_grad, axis=0)
    embedded_all = sinusoid(steps, width).astype(LOW).astype(F32)
    grad_time_weight = lax.dot_general(
        embedded_all, shift_grad, TN, precision=lax.Precision.HIGHEST, preferred_element_type=F32
    )
    own_table = lax.dynamic_slice_in_dim(table, dp_index * seq_dev, seq_dev, 0)
    root_squares = jnp.sqrt(own_table / (lengths.astype(F32)[:, None] * width) + STAT_EPS)
    return (
        block_output,
        input_gradient,
        root_squares,
        grad_time_weight,
        grad_time_bias,
        grad_triple,
        grad_query_value,
        grad_output_weight,
        got[2],
        got[0],
        got[1],
        grad_up_weight,
        full_up,
        grad_down_weight,
        got[3],
        got[4],
        got[5],
    )


def solution(mesh):
    tensor = mesh.shape["tensor"]
    spots = mesh.shape["dp"] // 2
    plane = tuple(f"plane{i}" for i in range(spots.bit_length() - 1))
    fine = Mesh(
        mesh.devices.reshape((2,) * len(plane) + (2, tensor)), plane + ("core", "tensor")
    )
    dp = plane + ("core",)
    row = P(dp + ("tensor",), None)
    in_specs = (
        row,
        P(dp),
        P(dp),
        P(),
        P(),
        P(None, None, "tensor"),
        P(None, "tensor"),
        P("tensor", None),
        P(),
        P(),
        P(),
        P(None, "tensor"),
        P("tensor"),
        P("tensor", None),
        P(),
        P(),
        P(),
        row,
    )
    out_specs = (
        row,
        row,
        P(dp, None),
        P(),
        P(),
        P(None, None, "tensor"),
        P(None, "tensor"),
        P("tensor", None),
        P(),
        P(),
        P(),
        P(None, "tensor"),
        P("tensor"),
        P("tensor", None),
        P(),
        P(),
        P(),
    )
    return jax.shard_map(
        functools.partial(on_device, plane),
        mesh=fine,
        in_specs=in_specs,
        out_specs=out_specs,
        check_vma=False,
    )
```

```python
import functools
import math

import jax
import jax.numpy as jnp
from jax import lax
from jax.experimental import pallas as pl
from jax.experimental.pallas import tpu as pltpu
from jax.sharding import Mesh
from jax.sharding import PartitionSpec as P

HD = 64
LEN = 1024
NORM_EPS = 1e-05
STAT_EPS = 1e-06
MASKED = -1e30
LOW = jnp.bfloat16
F32 = jnp.float32
NT = (((1,), (1,)), ((), ()))
TN = (((0,), (0,)), ((), ()))


def sinusoid(steps, width):
    half = width // 2
    rates = jnp.exp(-math.log(10000.0) * jnp.arange(half).astype(F32) / half)
    angles = steps.astype(F32)[:, None] * rates[None, :]
    return jnp.concatenate([jnp.sin(angles), jnp.cos(angles)], axis=1)


def plain(left, right):
    return jnp.dot(left, right, preferred_element_type=F32)


def inner(left, right):
    return lax.dot_general(left, right, TN, preferred_element_type=F32)


def against(left, right):
    return lax.dot_general(left, right, NT, preferred_element_type=F32)


def norm_forward(total, gain, shift):
    middle = jnp.mean(total, axis=-1, keepdims=True)
    centred = total - middle
    spread = jnp.mean(centred * centred, axis=-1, keepdims=True)
    factor = lax.rsqrt(spread + NORM_EPS)
    normed = centred * factor
    return (normed * gain + shift, normed, factor)


def norm_backward(upstream, normed, factor, gain):
    pushed = upstream * gain
    first = jnp.mean(pushed, axis=-1, keepdims=True)
    second = jnp.mean(pushed * normed, axis=-1, keepdims=True)
    return (
        factor * (pushed - first - normed * second),
        jnp.sum(upstream * normed, axis=0),
        jnp.sum(upstream, axis=0),
    )


def split3(x):
    hi = x.astype(LOW)
    rest = x - hi.astype(F32)
    mid = rest.astype(LOW)
    return hi, mid, (rest - mid.astype(F32)).astype(LOW)


def extra_lanes(parts, one, count):
    lane = lax.broadcasted_iota(jnp.int32, (count, HD), 1)
    out = jnp.where(lane == len(parts), 1.0, 0.0) if one else jnp.zeros((count, HD), F32)
    for index, part in enumerate(parts):
        out = jnp.where(lane == index, jnp.broadcast_to(part.astype(F32), (count, HD)), out)
    return out.astype(LOW)


def head(x, h):
    return x[:, h * HD : (h + 1) * HD]


def attend_kernel(rows, mask_ref, q_ref, k_ref, v_ref, context_ref, log_ref):
    count = q_ref.shape[0]
    mask = mask_ref[...]
    keys = k_ref[...].astype(LOW)
    values = v_ref[...].astype(LOW)
    for start in range(0, count, rows):
        part = slice(start, start + rows)
        queries = q_ref[part].astype(LOW) * LOW(HD**-0.5)
        contexts, logs = [], []
        for h in range(2):
            scores = lax.dot_general(
                head(queries, h), head(keys, h), NT, preferred_element_type=F32
            )
            scores = scores + mask
            highest = jnp.max(scores, axis=1, keepdims=True)
            probs = jnp.exp(scores - highest)
            total = jnp.sum(probs, axis=1, keepdims=True)
            contexts.append(plain(probs.astype(LOW), head(values, h)) / total)
            logs.append(jnp.broadcast_to(highest + jnp.log(total), (rows, HD)))
        context_ref[part] = jnp.concatenate(contexts, axis=1)
        log_ref[part] = jnp.concatenate(logs, axis=1)


def attend(projected, mask_row, pair):
    count, width = projected.shape
    local = width // 3
    pairs = local // (2 * HD)
    block = lambda which: pl.BlockSpec((count, 2 * HD), lambda p: (0, which * pairs + pair))
    whole = pl.BlockSpec((count, 2 * HD), lambda p: (0, 0))
    return pl.pallas_call(
        functools.partial(attend_kernel, 512),
        grid=(1,),
        in_specs=[pl.BlockSpec((1, count), lambda p: (0, 0)), block(0), block(1), block(2)],
        out_specs=[whole] * 2,
        out_shape=[jax.ShapeDtypeStruct((count, 2 * HD), F32)] * 2,
        compiler_params=pltpu.CompilerParams(vmem_limit_bytes=40 << 20),
        cost_estimate=pl.CostEstimate(
            flops=16 * count * count * 2 * HD,
            bytes_accessed=40 * count * HD,
            transcendentals=2 * count * count,
        ),
    )(mask_row, projected, projected, projected)


def attend_back_kernel(
    rows, mask_ref, q_ref, k_ref, v_ref, context_ref, log_ref, grad_ref, *refs
):
    dq_ref, dk_ref, dv_ref = refs[-3:]
    count = k_ref.shape[0]
    lane = lax.broadcasted_iota(jnp.int32, (count, HD), 1)
    three = jnp.where(lane < 3, 1.0, 0.0)
    key_extra = jnp.where(lane == 3, jnp.broadcast_to(mask_ref[...], (count, HD)), three)
    key_extra = key_extra.astype(LOW)
    value_extra = three.astype(LOW)
    queries = q_ref[...].astype(LOW) * LOW(HD**-0.5)
    keys = k_ref[...].astype(LOW)
    values = v_ref[...].astype(LOW)
    logs = log_ref[...]
    grads = grad_ref[...]
    dots = grads * context_ref[...]
    grads = grads.astype(LOW)
    kx, vx, qx, gx, dq = [], [], [], [], [None, None]
    for h in range(2):
        extra = extra_lanes(split3(-logs[:, h * HD : h * HD + 1]), True, count)
        qx.append(jnp.concatenate([head(queries, h), extra], axis=1))
        row_dot = jnp.sum(head(dots, h), axis=1, keepdims=True)
        extra = extra_lanes(split3(-row_dot), False, count)
        gx.append(jnp.concatenate([head(grads, h), extra], axis=1))
        kx.append(jnp.concatenate([head(keys, h), key_extra], axis=1))
        vx.append(jnp.concatenate([head(values, h), value_extra], axis=1))
    for start in range(0, count, rows):
        part = slice(start, start + rows)
        dk, dv = [], []
        for h in range(2):
            probs = jnp.exp(lax.dot_general(kx[h][part], qx[h], NT, preferred_element_type=F32))
            pushed = lax.dot_general(vx[h][part], gx[h], NT, preferred_element_type=F32)
            scores_grad = (probs * pushed).astype(LOW)
            dv.append(plain(probs.astype(LOW), gx[h])[:, :HD])
            dk.append(plain(scores_grad, qx[h])[:, :HD])
            more = lax.dot_general(scores_grad, kx[h][part], TN, preferred_element_type=F32)
            dq[h] = more if start == 0 else dq[h] + more
        dk_ref[part] = jnp.concatenate(dk, axis=1)
        dv_ref[part] = jnp.concatenate(dv, axis=1)
    dq_ref[...] = jnp.concatenate([x[:, :HD] for x in dq], axis=1) * HD**-0.5


def attend_back(projected, mask_column, context, log_total, grad, pair, before):
    count, width = projected.shape
    local = width // 3
    pairs = local // (2 * HD)
    block = lambda which: pl.BlockSpec((count, 2 * HD), lambda p: (0, which * pairs + pair))
    whole = pl.BlockSpec((count, 2 * HD), lambda p: (0, 0))
    return pl.pallas_call(
        functools.partial(attend_back_kernel, 512),
        grid=(1,),
        in_specs=[pl.BlockSpec((count, 1), lambda p: (0, 0)), block(0), block(1), block(2)]
        + [whole, whole, block(0)]
        + [pl.BlockSpec(memory_space=pl.ANY)] * len(before),
        out_specs=[whole] * 3,
        out_shape=[jax.ShapeDtypeStruct((count, 2 * HD), F32)] * 3,
        compiler_params=pltpu.CompilerParams(vmem_limit_bytes=50 << 20),
        cost_estimate=pl.CostEstimate(
            flops=40 * count * count * 2 * HD,
            bytes_accessed=80 * count * HD,
            transcendentals=2 * count * count,
        ),
    )(mask_column, projected, projected, projected, context, log_total, grad, *before)


class Wires:
    def __init__(self, plane, subs, seq_dev, send_sems, recv_sems):
        self.plane, self.subs, self.seq_dev = plane, subs, seq_dev
        self.send_sems, self.recv_sems, self.sent = send_sems, recv_sems, []
        self.bits = [lax.axis_index(name) for name in plane]
        self.core = lax.axis_index("core")
        me = lax.axis_index("tensor")
        self.sub, self.which = lax.rem(me, subs), lax.div(me, subs)
        self.quarters = 2 ** len(plane)

    def spot(self, mask=0):
        total, count = 0, len(self.plane)
        for i, bit in enumerate(self.bits):
            flip = (mask >> (count - 1 - i)) & 1
            total = total + (1 - bit if flip else bit) * 2 ** (count - 1 - i)
        return total

    def at_plane(self, mask):
        count = len(self.plane)
        return {
            name: 1 - bit
            for i, (name, bit) in enumerate(zip(self.plane, self.bits))
            if (mask >> (count - 1 - i)) & 1
        }

    def at_core(self):
        return {"core": 1 - self.core}

    def at_member(self, k, j):
        return {
            "tensor": lax.rem(self.which + j + self.seq_dev, self.seq_dev) * self.subs
            + lax.rem(self.sub + k + self.subs, self.subs)
        }

    def greet(self, targets):
        barrier = pltpu.get_barrier_semaphore()
        for target in targets:
            pl.semaphore_signal(barrier, inc=1, device_id=target, device_id_type=pl.DeviceIdType.MESH)
        pl.semaphore_wait(barrier, len(targets))

    def send(self, src, dst, target):
        index = len(self.sent)
        copy = pltpu.make_async_remote_copy(
            src_ref=src,
            dst_ref=dst,
            send_sem=self.send_sems.at[index],
            recv_sem=self.recv_sems.at[index],
            device_id=target,
            device_id_type=pl.DeviceIdType.MESH,
        )
        copy.start()
        self.sent.append(copy)
        return copy

    def finish(self):
        for copy in self.sent:
            copy.wait_send()


def wide(x):
    return x.astype(F32)


def sum_kernel(
    plane, subs, seq_dev, units, later, now, output, vectors, away,
    units_out, triple_out, output_out, vectors_out, away_out,
    units_z, later_core, now_core, output_core, later_half, now_half, output_half,
    later_plane, now_plane, output_plane, triple_z, output_z, triple_mine, output_mine,
    vectors_core, vectors_plane, vectors_z, vectors_one, vectors_two, send_sems, recv_sems,
):
    wires = Wires(plane, subs, seq_dev, send_sems, recv_sems)
    quarters, core = wires.quarters, wires.core
    spot = wires.spot()
    offsets = [(k, j) for k in range(subs) for j in range(seq_dev)]
    ahead = range(1, len(offsets))
    masks = range(1, quarters)
    wires.greet(
        [wires.at_core()]
        + [wires.at_plane(mask) for mask in masks]
        + [wires.at_member(k, j) for k, j in offsets[1:]]
    )
    core_got = []
    for source, target in ((later, later_core), (output, output_core), (now, now_core)):
        core_got.append(
            [
                wires.send(source.at[place, 1 - core], target.at[place], wires.at_core())
                for place in range(quarters)
            ]
        )
    vectors_got = wires.send(vectors, vectors_core, wires.at_core())
    units_got = [
        [wires.send(units.at[which, z], units_z.at[which, z - 1], wires.at_member(*offsets[z])) for z in ahead]
        for which in range(2)
    ]
    away_got = [wires.send(away.at[k - 1], away_out.at[k - 1], wires.at_member(k, 0)) for k in range(1, subs)]
    plane_got = []
    for got, source, received, half, target in (
        (core_got[0], later, later_core, later_half, later_plane),
        (core_got[1], output, output_core, output_half, output_plane),
        (core_got[2], now, now_core, now_half, now_plane),
    ):
        for copy in got:
            copy.wait_recv()
        for place in range(quarters):
            half[place] = (wide(source[place, core]) + wide(received[place])).astype(LOW)
        plane_got.append(
            [
                wires.send(half.at[wires.spot(mask)], target.at[mask - 1], wires.at_plane(mask))
                for mask in masks
            ]
        )
    vectors_got.wait_recv()
    vectors_one[...] = vectors[...] + vectors_core[...]
    vectors_got = [
        wires.send(vectors_one, vectors_plane.at[mask - 1], wires.at_plane(mask)) for mask in masks
    ]
    for copy in plane_got[0]:
        copy.wait_recv()
    total = wide(later_half[spot])
    for mask in masks:
        total = total + wide(later_plane[mask - 1])
    triple_mine[...] = total.astype(LOW)
    triple_got = [wires.send(triple_mine, triple_z, wires.at_member(0, 1))]
    for copy in plane_got[1]:
        copy.wait_recv()
    total = wide(output_half[spot])
    for mask in masks:
        total = total + wide(output_plane[mask - 1])
    output_mine[...] = total.astype(LOW)
    output_got = [
        wires.send(output_mine.at[z], output_z.at[z - 1], wires.at_member(*offsets[z])) for z in ahead
    ]
    for copy in vectors_got:
        copy.wait_recv()
    total = vectors_one[...]
    for mask in masks:
        total = total + vectors_plane[mask - 1]
    vectors_two[...] = total
    vectors_got = [
        wires.send(vectors_two, vectors_z.at[z - 1], wires.at_member(*offsets[z])) for z in ahead
    ]
    for copy in plane_got[2]:
        copy.wait_recv()
    last, passed = [], []

    def hand_round(slot):
        for mask in masks:
            passed.append((slot, mask, wires.send(slot(spot), slot(spot), wires.at_plane(mask))))
        last.append(wires.send(slot(spot), slot(spot), wires.at_core()))

    def hand_over():
        while passed:
            slot, mask, copy = passed.pop(0)
            copy.wait_recv()
            ref = slot(wires.spot(mask))
            last.append(wires.send(ref, ref, wires.at_core()))

    for copy in triple_got:
        copy.wait_recv()
    total = wide(now_half[spot]) + wide(triple_z[...])
    for mask in masks:
        total = total + wide(now_plane[mask - 1])
    triple_out[spot, core] = total.astype(LOW)
    hand_round(lambda place: triple_out.at[place, core])
    for copy in output_got:
        copy.wait_recv()
    total = wide(output_mine[0])
    for z in ahead:
        total = total + wide(output_z[z - 1])
    output_out[spot, core] = total.astype(LOW)
    hand_round(lambda place: output_out.at[place, core])
    for which in range(2):
        for copy in units_got[which]:
            copy.wait_recv()
        total = wide(units[which, 0])
        for z in ahead:
            total = total + wide(units_z[which, z - 1])
        units_out[which, core, spot] = total.astype(LOW)
        hand_over()
        hand_round(functools.partial(lambda which, place: units_out.at[which, core, place], which))
    hand_over()
    for copy in vectors_got:
        copy.wait_recv()
    total = vectors_two[...]
    for z in ahead:
        total = total + vectors_z[z - 1]
    vectors_out[...] = total
    for copy in away_got + last:
        copy.wait_recv()
    wires.finish()


def sum_all(plane, seq_dev, units, later, now, output, vectors, away):
    tensor, quarters = lax.axis_size("tensor"), 2 ** len(plane)
    subs, masks = tensor // seq_dev, quarters - 1
    piece, share, out_share = units.shape[2:], later.shape[2:], output.shape[3:]
    low = lambda *shape: pltpu.VMEM(shape, LOW)
    full = lambda *shape: pltpu.VMEM(shape + vectors.shape, F32)
    copies = (
        3 * quarters + 1 + 2 * (tensor - 1) + subs - 1 + 3 * masks + masks + 1 + 2 * (tensor - 1)
        + 4 * (masks + 1 + masks)
    )
    return pl.pallas_call(
        functools.partial(sum_kernel, plane, subs, seq_dev),
        in_specs=[pl.BlockSpec(memory_space=pltpu.VMEM)] * 6,
        out_specs=[pl.BlockSpec(memory_space=pltpu.VMEM)] * 5,
        out_shape=[
            jax.ShapeDtypeStruct((2, 2, quarters) + piece, LOW),
            jax.ShapeDtypeStruct((quarters, 2) + share, LOW),
            jax.ShapeDtypeStruct((quarters, 2) + out_share, LOW),
            jax.ShapeDtypeStruct(vectors.shape, F32),
            jax.ShapeDtypeStruct(away.shape, LOW),
        ],
        scratch_shapes=[
            low(2, tensor - 1, *piece),
            low(quarters, *share),
            low(quarters, *share),
            low(quarters, tensor, *out_share),
            low(quarters, *share),
            low(quarters, *share),
            low(quarters, tensor, *out_share),
            low(masks, *share),
            low(masks, *share),
            low(masks, tensor, *out_share),
            low(*share),
            low(tensor - 1, *out_share),
            low(*share),
            low(tensor, *out_share),
            full(),
            full(masks),
            full(tensor - 1),
            full(),
            full(),
            pltpu.SemaphoreType.DMA((copies,)),
            pltpu.SemaphoreType.DMA((copies,)),
        ],
        compiler_params=pltpu.CompilerParams(
            collective_id=1, has_side_effects=True, vmem_limit_bytes=48 << 20
        ),
        cost_estimate=pl.CostEstimate(flops=1 << 24, bytes_accessed=1 << 27, transcendentals=0),
    )(units, later, now, output, vectors, away)


def gaussian_pair(value):
    cumulative = 0.5 * (1.0 + jax.scipy.special.erf(value * (1.0 / math.sqrt(2.0))))
    slope = cumulative + value * jnp.exp(-0.5 * value * value) * (1.0 / math.sqrt(2.0 * math.pi))
    return (value * cumulative).astype(LOW), slope.astype(LOW)


def on_device(
    plane,
    stream_in,
    timestep,
    lengths,
    time_weight,
    time_bias,
    triple_weight,
    query_value_bias,
    output_weight,
    output_bias,
    first_gain,
    first_shift,
    up_weight,
    up_bias,
    down_weight,
    down_bias,
    second_gain,
    second_shift,
    cotangent,
):
    rows, width = stream_in.shape
    seq_dev = timestep.shape[0]
    tensor = lax.axis_size("tensor")
    subs = tensor // seq_dev
    local = triple_weight.shape[2]
    units = up_weight.shape[1]
    half_units = units // 2
    quarters = 2 ** len(plane)
    piece_units = half_units // quarters
    me = lax.axis_index("tensor")
    core = lax.axis_index("core")
    spot = lax.axis_index(plane)
    sub = me % subs
    which = me // subs
    offsets = [(k, j) for k in range(subs) for j in range(seq_dev)]
    others = offsets[1:]

    def member(i, k, j):
        return ((i // subs + j) % seq_dev) * subs + (i % subs + k) % subs

    def fetch(x, k, j):
        return lax.ppermute(x, "tensor", [(member(i, k, j), i) for i in range(tensor)])

    def send(x, k, j):
        return lax.ppermute(x, "tensor", [(i, member(i, k, j)) for i in range(tensor)])

    def swap(x, axis):
        return lax.ppermute(x, axis, [(0, 1), (1, 0)])

    def across(x, mask):
        return lax.ppermute(x, plane, [(i, i ^ mask) for i in range(quarters)])

    def pick(x, index, axis=0):
        return lax.dynamic_index_in_dim(x, index, axis, keepdims=False)

    def tie(x, *before):
        return lax.optimization_barrier((x,) + before)[0]

    def ordered(parts, index):
        parts = jnp.stack(parts) if isinstance(parts, (list, tuple)) else parts
        return jnp.stack([pick(parts, index ^ m) for m in range(parts.shape[0])])

    raw = [stream_in] + [fetch(stream_in, k, 0) for k in range(1, subs)]
    triple_own = triple_weight.reshape(width, 3 * local)
    part = width // (2 * quarters)

    def whole(piece):
        got = jnp.stack([piece] + [across(piece, mask) for mask in range(1, quarters)])
        other = swap(got, "core")
        first = jnp.where(core == 0, got, other)
        second = jnp.where(core == 0, other, got)
        return ordered(jnp.stack([first, second], axis=1), spot)

    triples = [triple_own]
    for j in range(1, seq_dev):
        share = lax.dynamic_slice_in_dim(triple_own, (2 * spot + core) * part, part, 0)
        share = fetch(share, 0, j)
        triples.append(whole(share).reshape(width, 3 * local))

    small = tie(jnp.concatenate([up_bias, query_value_bias.reshape(-1)]), share)
    small_of = {(0, 0): small}
    for k, j in others:
        small_of[(k, j)] = fetch(small, k, j)

    up_half = lax.dynamic_slice_in_dim(up_weight, core * half_units, half_units, 1).T
    down_half = lax.dynamic_slice_in_dim(down_weight, core * half_units, half_units, 0)
    units_mine = [
        ordered(x.reshape(quarters, piece_units, width), spot) for x in (up_half, down_half)
    ]
    units_share = tie(jnp.stack([units_mine[0][0], units_mine[1][0]]), share)
    units_got = [fetch(units_share, k, j) for k, j in others]

    out_part = local // (2 * quarters)
    out_share = lax.dynamic_slice_in_dim(
        output_weight, (2 * spot + core) * out_part, out_part, 0
    )
    out_share = tie(out_share, share)
    out_got = jnp.stack([fetch(out_share, k, j) for k, j in others])
    out_all = whole(tie(out_got, triples[-1]))
    out_all = out_all.transpose(2, 0, 1, 3, 4).reshape(tensor - 1, local, width)
    out_full = jnp.concatenate([output_weight[None], out_all]).reshape(tensor * local, width)

    embedded_own = sinusoid(timestep, width).astype(LOW)
    shift_own = plain(embedded_own, time_weight) + time_bias
    shift_row = pick(shift_own, which)
    limit = pick(lengths, which)
    stream = stream_in.astype(F32) + shift_row
    stream_low = (jnp.concatenate(raw, axis=0).astype(F32) + shift_row).astype(LOW)
    place = (jnp.arange(LEN, dtype=jnp.int32) + sub * rows) % LEN
    mask = jnp.where(place < limit, 0.0, MASKED).astype(F32)
    mask_row, mask_column = mask[None, :], mask[:, None]
    valid = (place[:rows] < limit).astype(F32)

    pairs = local // (2 * HD)
    qv = [small_of[(0, j)][units:].reshape(2, local) for j in range(seq_dev)]
    projected, context, log_total = [], [], []
    for j in range(seq_dev):
        bias = jnp.concatenate([qv[j][0], jnp.zeros((local,), F32), qv[j][1]])
        projected.append(plain(stream_low, triples[j]) + bias)
        here = [attend(projected[j], mask_row, pair) for pair in range(pairs)]
        context.append([x[0] for x in here])
        log_total.append([x[1] for x in here])
    block = lambda x, k: x[k * rows : (k + 1) * rows]
    columns = []
    for k in range(subs):
        back = (subs - k) % subs
        for j in range(seq_dev):
            mine = jnp.concatenate([block(x, back) for x in context[j]], axis=1).astype(LOW)
            columns.append(mine if k == 0 else send(mine, back, 0))
    context_own = jnp.concatenate(columns, axis=1)

    units_got = jnp.stack(units_got, axis=1)
    units_got = tie(units_got, context[0][-1])
    bits = [(1 << (len(plane) - 1 - i), name) for i, name in enumerate(plane)]

    def over_plane(x, order):
        got, masks = x[None], [0]
        for step, (bit, name) in enumerate(order):
            got = jnp.concatenate([got, swap(got, name)], axis=0)
            masks = masks + [m | bit for m in masks]
            if step == 0:
                got = tie(got, context[-1][-1])
        return {m: got[i] for i, m in enumerate(masks)}

    def all_rows(mine, got):
        full = [x for m in range(quarters) for x in (mine[m][None], got[m])]
        return jnp.concatenate(full, axis=0).reshape(quarters * tensor * piece_units, width)

    up_rows = all_rows(units_mine[0], over_plane(units_got[0], bits[::-1]))
    down_rows = all_rows(units_mine[1], over_plane(units_got[1], bits))

    branch = plain(context_own, out_full) + output_bias
    middle, normed_first, factor_first = norm_forward(stream + branch, first_gain, first_shift)
    middle_low = middle.astype(LOW)

    bias_all = jnp.stack([small_of[o][:units] for o in offsets])
    bias_half = lax.dynamic_slice_in_dim(bias_all, core * half_units, half_units, 1)
    bias_rel = ordered(
        bias_half.reshape(tensor, quarters, piece_units).transpose(1, 0, 2), spot
    ).reshape(-1)
    both = jnp.concatenate([middle_low, swap(middle_low, "core")], axis=0)
    active, slope = gaussian_pair(against(both, up_rows) + bias_rel)
    feed_other = plain(active[rows:], down_rows).astype(LOW)
    feed = plain(active[:rows], down_rows) + swap(feed_other, "core").astype(F32) + down_bias
    result, normed_second, factor_second = norm_forward(middle + feed, second_gain, second_shift)
    block_output = result.astype(LOW)

    to_second, grad_second_gain, grad_second_shift = norm_backward(
        cotangent.astype(F32), normed_second, factor_second, second_gain
    )
    feed_grad = to_second.astype(LOW)
    grad_down_bias = jnp.sum(feed_grad.astype(F32), axis=0)
    feed_grad_both = jnp.concatenate([feed_grad, swap(feed_grad, "core")], axis=0)

    def by_mask(total):
        shaped = total.reshape(quarters, tensor, piece_units, width)
        return {m: shaped[m] for m in range(quarters)}

    down_total = by_mask(inner(active, feed_grad_both).astype(LOW))
    before_grad = (against(feed_grad_both, down_rows) * slope.astype(F32)).astype(LOW)
    up_total = by_mask(inner(before_grad, both).astype(LOW))
    units_sum = wide(jnp.stack([up_total[0], down_total[0]]))
    for m in range(1, quarters):
        units_sum = units_sum + wide(across(jnp.stack([up_total[m], down_total[m]]), m))
    units_sum = units_sum.astype(LOW)
    grad_up_rel = jnp.sum(before_grad.astype(F32), axis=0)
    middle_other = plain(before_grad[rows:], up_rows).astype(LOW)
    middle_grad = (
        to_second + plain(before_grad[:rows], up_rows) + swap(middle_other, "core").astype(F32)
    )

    to_first, grad_first_gain, grad_first_shift = norm_backward(
        middle_grad, normed_first, factor_first, first_gain
    )
    branch_grad = to_first.astype(LOW)
    grad_output_bias = jnp.sum(branch_grad.astype(F32), axis=0)
    context_grad = against(branch_grad, out_full).astype(LOW)
    shaped = context_grad.reshape(rows, subs, seq_dev, local)
    incoming = []
    for j in range(seq_dev):
        parts = []
        for k in range(subs):
            back = (subs - k) % subs
            mine = shaped[:, back, j]
            parts.append(mine if k == 0 else send(mine, back, 0))
        incoming.append(jnp.concatenate(parts, axis=0).astype(F32))

    def backward(j, pair, before):
        return attend_back(
            projected[j], mask_column, context[j][pair], log_total[j][pair], incoming[j], pair, before
        )

    def together(parts):
        return jnp.concatenate([x[i] for i in range(3) for x in parts], axis=1).astype(LOW)

    grads = [None] * seq_dev
    for j in reversed(range(seq_dev)):
        grads[j] = together([backward(j, pair, []) for pair in range(pairs)])
    triple_parts = [
        inner(stream_low, grads[j]).astype(LOW).reshape(quarters, 2, part, 3 * local)
        for j in range(seq_dev)
    ]
    out_total = inner(context_own, branch_grad).astype(LOW)
    out_total = out_total.reshape(tensor, quarters, 2, out_part, width).transpose(1, 2, 0, 3, 4)
    away = jnp.stack(
        [
            sum(against(block(grads[j], k), triples[j]) for j in range(seq_dev)).astype(LOW)
            for k in range(1, subs)
        ]
    )
    stream_own = to_first + sum(
        against(block(grads[j], 0), triples[j]) for j in range(seq_dev)
    )

    dp_index = spot * 2 + core
    seqs = quarters * 2 * seq_dev
    column_sums = [jnp.sum(grads[j].astype(F32), axis=0) for j in range(seq_dev)]
    shift_part = jnp.sum(to_first, axis=0) + sum(
        against(column_sums[j][None].astype(F32), triples[j].astype(F32))[0]
        for j in range(seq_dev)
    )
    hot = (jnp.arange(seqs) == dp_index * seq_dev + which).astype(F32)
    shift_rows = hot[:, None] * shift_part[None, :]
    squares = jnp.stack([jnp.sum(jnp.sum(x * x, axis=1) * valid) for x in (stream, branch, feed)])
    table = hot[:, None] * squares[None, :]
    steps_hot = (
        jnp.arange(seqs)[:, None] == dp_index * seq_dev + jnp.arange(seq_dev)[None, :]
    ).astype(F32)
    steps_all = jnp.sum(steps_hot * timestep.astype(F32)[None, :], axis=1) * (me == 0)
    up_canonical = ordered(grad_up_rel.reshape(quarters, tensor, piece_units), spot)
    up_canonical = up_canonical.transpose(1, 0, 2).reshape(tensor, half_units)
    full_up = jnp.zeros((tensor, 2, half_units), F32)
    full_qv = jnp.zeros((tensor, 2, local), F32)
    for index, (k, j) in enumerate(offsets):
        at = ((which + j) % seq_dev) * subs + (sub + k) % subs
        row = jnp.where(jnp.arange(2)[:, None] == core, up_canonical[index][None], 0.0)
        full_up = lax.dynamic_update_slice_in_dim(full_up, row[None], at, 0)
        if k == 0:
            value = column_sums[j].reshape(3, local)
            value = jnp.stack([value[0], value[2]])
            full_qv = lax.dynamic_update_slice_in_dim(full_qv, value[None], at, 0)

    vectors = [
        grad_first_gain,
        grad_first_shift,
        grad_output_bias,
        grad_down_bias,
        grad_second_gain,
        grad_second_shift,
        full_up.reshape(-1),
        shift_rows.reshape(-1),
        full_qv.reshape(-1),
        table.reshape(-1),
        steps_all,
    ]
    packed = jnp.concatenate(vectors)
    packed = jnp.pad(packed, (0, -packed.shape[0] % width)).reshape(-1, width)
    units_all, triple_all, out_all, packed, away = sum_all(
        plane, seq_dev, units_sum, triple_parts[1], triple_parts[0], out_total, packed, away
    )
    units_all = units_all.reshape(2, units, width)
    grad_up_weight = units_all[0].T.astype(F32)
    grad_down_weight = units_all[1].astype(F32)
    grad_output_weight = out_all.reshape(local, width).astype(F32)
    grad_triple = triple_all.astype(F32).reshape(width, 3, local)
    input_gradient = (stream_own + sum(wide(away[k]) for k in range(subs - 1))).astype(LOW)
    packed = packed.reshape(-1)
    got, at = [], 0
    for vector in vectors:
        got.append(packed[at : at + vector.shape[0]])
        at += vector.shape[0]
    full_up = pick(got[6].reshape(tensor, units), me)
    shift_grad = got[7].reshape(seqs, width)
    grad_query_value = pick(got[8].reshape(tensor, 2, local), me)
    table, steps_all = got[9].reshape(seqs, 3), got[10]
    grad_time_bias = jnp.sum(shift_grad, axis=0)
    embedded_all = sinusoid(steps_all, width).astype(LOW).astype(F32)
    grad_time_weight = lax.dot_general(
        embedded_all, shift_grad, TN, precision=lax.Precision.HIGHEST, preferred_element_type=F32
    )
    own_table = lax.dynamic_slice_in_dim(table, dp_index * seq_dev, seq_dev, 0)
    root_squares = jnp.sqrt(own_table / (lengths.astype(F32)[:, None] * width) + STAT_EPS)
    return (
        block_output,
        input_gradient,
        root_squares,
        grad_time_weight,
        grad_time_bias,
        grad_triple,
        grad_query_value,
        grad_output_weight,
        got[2],
        got[0],
        got[1],
        grad_up_weight,
        full_up,
        grad_down_weight,
        got[3],
        got[4],
        got[5],
    )


def solution(mesh):
    tensor = mesh.shape["tensor"]
    spots = mesh.shape["dp"] // 2
    plane = tuple(f"plane{i}" for i in range(spots.bit_length() - 1))
    fine = Mesh(
        mesh.devices.reshape((2,) * len(plane) + (2, tensor)), plane + ("core", "tensor")
    )
    dp = plane + ("core",)
    row = P(dp + ("tensor",), None)
    in_specs = (
        row,
        P(dp),
        P(dp),
        P(),
        P(),
        P(None, None, "tensor"),
        P(None, "tensor"),
        P("tensor", None),
        P(),
        P(),
        P(),
        P(None, "tensor"),
        P("tensor"),
        P("tensor", None),
        P(),
        P(),
        P(),
        row,
    )
    out_specs = (
        row,
        row,
        P(dp, None),
        P(),
        P(),
        P(None, None, "tensor"),
        P(None, "tensor"),
        P("tensor", None),
        P(),
        P(),
        P(),
        P(None, "tensor"),
        P("tensor"),
        P("tensor", None),
        P(),
        P(),
        P(),
    )
    return jax.shard_map(
        functools.partial(on_device, plane),
        mesh=fine,
        in_specs=in_specs,
        out_specs=out_specs,
        check_vma=False,
    )
```

```python
import functools
import math

import jax
import jax.numpy as jnp
from jax import lax
from jax.experimental import pallas as pl
from jax.experimental.pallas import tpu as pltpu
from jax.sharding import Mesh
from jax.sharding import PartitionSpec as P

HD = 64
LEN = 1024
NORM_EPS = 1e-05
STAT_EPS = 1e-06
MASKED = -1e30
LOW = jnp.bfloat16
F32 = jnp.float32
NT = (((1,), (1,)), ((), ()))
TN = (((0,), (0,)), ((), ()))


def sinusoid(steps, width):
    half = width // 2
    rates = jnp.exp(-math.log(10000.0) * jnp.arange(half).astype(F32) / half)
    angles = steps.astype(F32)[:, None] * rates[None, :]
    return jnp.concatenate([jnp.sin(angles), jnp.cos(angles)], axis=1)


def plain(left, right):
    return jnp.dot(left, right, preferred_element_type=F32)


def inner(left, right):
    return lax.dot_general(left, right, TN, preferred_element_type=F32)


def against(left, right):
    return lax.dot_general(left, right, NT, preferred_element_type=F32)


def norm_forward(total, gain, shift):
    middle = jnp.mean(total, axis=-1, keepdims=True)
    centred = total - middle
    spread = jnp.mean(centred * centred, axis=-1, keepdims=True)
    factor = lax.rsqrt(spread + NORM_EPS)
    normed = centred * factor
    return (normed * gain + shift, normed, factor)


def norm_backward(upstream, normed, factor, gain):
    pushed = upstream * gain
    first = jnp.mean(pushed, axis=-1, keepdims=True)
    second = jnp.mean(pushed * normed, axis=-1, keepdims=True)
    return (
        factor * (pushed - first - normed * second),
        jnp.sum(upstream * normed, axis=0),
        jnp.sum(upstream, axis=0),
    )


def split3(x):
    hi = x.astype(LOW)
    rest = x - hi.astype(F32)
    mid = rest.astype(LOW)
    return hi, mid, (rest - mid.astype(F32)).astype(LOW)


def extra_lanes(parts, one, count):
    lane = lax.broadcasted_iota(jnp.int32, (count, HD), 1)
    out = jnp.where(lane == len(parts), 1.0, 0.0) if one else jnp.zeros((count, HD), F32)
    for index, part in enumerate(parts):
        out = jnp.where(lane == index, jnp.broadcast_to(part.astype(F32), (count, HD)), out)
    return out.astype(LOW)


def head(x, h):
    return x[:, h * HD : (h + 1) * HD]


def attend_kernel(rows, mask_ref, q_ref, k_ref, v_ref, context_ref, log_ref):
    count = q_ref.shape[0]
    mask = mask_ref[...]
    keys = k_ref[...].astype(LOW)
    values = v_ref[...].astype(LOW)
    for start in range(0, count, rows):
        part = slice(start, start + rows)
        queries = q_ref[part].astype(LOW) * LOW(HD**-0.5)
        contexts, logs = [], []
        for h in range(2):
            scores = lax.dot_general(
                head(queries, h), head(keys, h), NT, preferred_element_type=F32
            )
            scores = scores + mask
            highest = jnp.max(scores, axis=1, keepdims=True)
            probs = jnp.exp(scores - highest)
            total = jnp.sum(probs, axis=1, keepdims=True)
            contexts.append(plain(probs.astype(LOW), head(values, h)) / total)
            logs.append(jnp.broadcast_to(highest + jnp.log(total), (rows, HD)))
        context_ref[part] = jnp.concatenate(contexts, axis=1)
        log_ref[part] = jnp.concatenate(logs, axis=1)


def attend(projected, mask_row, pair):
    count, width = projected.shape
    local = width // 3
    pairs = local // (2 * HD)
    block = lambda which: pl.BlockSpec((count, 2 * HD), lambda p: (0, which * pairs + pair))
    whole = pl.BlockSpec((count, 2 * HD), lambda p: (0, 0))
    return pl.pallas_call(
        functools.partial(attend_kernel, 512),
        grid=(1,),
        in_specs=[pl.BlockSpec((1, count), lambda p: (0, 0)), block(0), block(1), block(2)],
        out_specs=[whole] * 2,
        out_shape=[jax.ShapeDtypeStruct((count, 2 * HD), F32)] * 2,
        compiler_params=pltpu.CompilerParams(vmem_limit_bytes=40 << 20),
        cost_estimate=pl.CostEstimate(
            flops=16 * count * count * 2 * HD,
            bytes_accessed=40 * count * HD,
            transcendentals=2 * count * count,
        ),
    )(mask_row, projected, projected, projected)


def attend_back_kernel(
    rows, mask_ref, q_ref, k_ref, v_ref, context_ref, log_ref, grad_ref, *refs
):
    dq_ref, dk_ref, dv_ref = refs[-3:]
    count = k_ref.shape[0]
    lane = lax.broadcasted_iota(jnp.int32, (count, HD), 1)
    three = jnp.where(lane < 3, 1.0, 0.0)
    key_extra = jnp.where(lane == 3, jnp.broadcast_to(mask_ref[...], (count, HD)), three)
    key_extra = key_extra.astype(LOW)
    value_extra = three.astype(LOW)
    queries = q_ref[...].astype(LOW) * LOW(HD**-0.5)
    keys = k_ref[...].astype(LOW)
    values = v_ref[...].astype(LOW)
    logs = log_ref[...]
    grads = grad_ref[...]
    dots = grads * context_ref[...]
    grads = grads.astype(LOW)
    kx, vx, qx, gx, dq = [], [], [], [], [None, None]
    for h in range(2):
        extra = extra_lanes(split3(-logs[:, h * HD : h * HD + 1]), True, count)
        qx.append(jnp.concatenate([head(queries, h), extra], axis=1))
        row_dot = jnp.sum(head(dots, h), axis=1, keepdims=True)
        extra = extra_lanes(split3(-row_dot), False, count)
        gx.append(jnp.concatenate([head(grads, h), extra], axis=1))
        kx.append(jnp.concatenate([head(keys, h), key_extra], axis=1))
        vx.append(jnp.concatenate([head(values, h), value_extra], axis=1))
    for start in range(0, count, rows):
        part = slice(start, start + rows)
        dk, dv = [], []
        for h in range(2):
            probs = jnp.exp(lax.dot_general(kx[h][part], qx[h], NT, preferred_element_type=F32))
            pushed = lax.dot_general(vx[h][part], gx[h], NT, preferred_element_type=F32)
            scores_grad = (probs * pushed).astype(LOW)
            dv.append(plain(probs.astype(LOW), gx[h])[:, :HD])
            dk.append(plain(scores_grad, qx[h])[:, :HD])
            more = lax.dot_general(scores_grad, kx[h][part], TN, preferred_element_type=F32)
            dq[h] = more if start == 0 else dq[h] + more
        dk_ref[part] = jnp.concatenate(dk, axis=1)
        dv_ref[part] = jnp.concatenate(dv, axis=1)
    dq_ref[...] = jnp.concatenate([x[:, :HD] for x in dq], axis=1) * HD**-0.5


def attend_back(projected, mask_column, context, log_total, grad, pair, before):
    count, width = projected.shape
    local = width // 3
    pairs = local // (2 * HD)
    block = lambda which: pl.BlockSpec((count, 2 * HD), lambda p: (0, which * pairs + pair))
    whole = pl.BlockSpec((count, 2 * HD), lambda p: (0, 0))
    return pl.pallas_call(
        functools.partial(attend_back_kernel, 512),
        grid=(1,),
        in_specs=[pl.BlockSpec((count, 1), lambda p: (0, 0)), block(0), block(1), block(2)]
        + [whole, whole, block(0)]
        + [pl.BlockSpec(memory_space=pl.ANY)] * len(before),
        out_specs=[whole] * 3,
        out_shape=[jax.ShapeDtypeStruct((count, 2 * HD), F32)] * 3,
        compiler_params=pltpu.CompilerParams(vmem_limit_bytes=50 << 20),
        cost_estimate=pl.CostEstimate(
            flops=40 * count * count * 2 * HD,
            bytes_accessed=80 * count * HD,
            transcendentals=2 * count * count,
        ),
    )(mask_column, projected, projected, projected, context, log_total, grad, *before)


class Wires:
    def __init__(self, plane, subs, seq_dev, send_sems, recv_sems):
        self.plane, self.subs, self.seq_dev = plane, subs, seq_dev
        self.send_sems, self.recv_sems, self.sent = send_sems, recv_sems, []
        self.bits = [lax.axis_index(name) for name in plane]
        self.core = lax.axis_index("core")
        me = lax.axis_index("tensor")
        self.sub, self.which = lax.rem(me, subs), lax.div(me, subs)
        self.quarters = 2 ** len(plane)

    def spot(self, mask=0):
        total, count = 0, len(self.plane)
        for i, bit in enumerate(self.bits):
            flip = (mask >> (count - 1 - i)) & 1
            total = total + (1 - bit if flip else bit) * 2 ** (count - 1 - i)
        return total

    def at_plane(self, mask):
        count = len(self.plane)
        return {
            name: 1 - bit
            for i, (name, bit) in enumerate(zip(self.plane, self.bits))
            if (mask >> (count - 1 - i)) & 1
        }

    def at_core(self):
        return {"core": 1 - self.core}

    def at_member(self, k, j):
        return {
            "tensor": lax.rem(self.which + j + self.seq_dev, self.seq_dev) * self.subs
            + lax.rem(self.sub + k + self.subs, self.subs)
        }

    def greet(self, targets):
        barrier = pltpu.get_barrier_semaphore()
        for target in targets:
            pl.semaphore_signal(barrier, inc=1, device_id=target, device_id_type=pl.DeviceIdType.MESH)
        pl.semaphore_wait(barrier, len(targets))

    def send(self, src, dst, target):
        index = len(self.sent)
        copy = pltpu.make_async_remote_copy(
            src_ref=src,
            dst_ref=dst,
            send_sem=self.send_sems.at[index],
            recv_sem=self.recv_sems.at[index],
            device_id=target,
            device_id_type=pl.DeviceIdType.MESH,
        )
        copy.start()
        self.sent.append(copy)
        return copy

    def finish(self):
        for copy in self.sent:
            copy.wait_send()


def wide(x):
    return x.astype(F32)


def sum_kernel(
    plane, subs, seq_dev, ordering, units, later, now, output, vectors, *refs
):
    (
    units_out, triple_out, output_out, vectors_out,
    units_z, later_core, now_core, output_core, later_half, now_half, output_half,
    later_plane, now_plane, output_plane, triple_z, output_z, triple_mine, output_mine,
    vectors_core, vectors_plane, vectors_z, vectors_one, vectors_two, send_sems, recv_sems,
    ) = refs[ordering:]
    wires = Wires(plane, subs, seq_dev, send_sems, recv_sems)
    quarters, core = wires.quarters, wires.core
    spot = wires.spot()
    offsets = [(k, j) for k in range(subs) for j in range(seq_dev)]
    ahead = range(1, len(offsets))
    masks = range(1, quarters)
    wires.greet(
        [wires.at_core()]
        + [wires.at_plane(mask) for mask in masks]
        + [wires.at_member(k, j) for k, j in offsets[1:]]
    )
    core_got = []
    for source, target in ((later, later_core), (output, output_core), (now, now_core)):
        core_got.append(
            [
                wires.send(source.at[place, 1 - core], target.at[place], wires.at_core())
                for place in range(quarters)
            ]
        )
    vectors_got = wires.send(vectors, vectors_core, wires.at_core())

    def units_along(which):
        return [
            wires.send(units.at[which, z], units_z.at[which, z - 1], wires.at_member(*offsets[z]))
            for z in ahead
        ]

    units_got = [units_along(0)]
    plane_got = []
    for got, source, received, half, target in (
        (core_got[0], later, later_core, later_half, later_plane),
        (core_got[1], output, output_core, output_half, output_plane),
        (core_got[2], now, now_core, now_half, now_plane),
    ):
        for copy in got:
            copy.wait_recv()
        for place in range(quarters):
            half[place] = (wide(source[place, core]) + wide(received[place])).astype(LOW)
        plane_got.append(
            [
                wires.send(half.at[wires.spot(mask)], target.at[mask - 1], wires.at_plane(mask))
                for mask in masks
            ]
        )
    vectors_got.wait_recv()
    vectors_one[...] = vectors[...] + vectors_core[...]
    vectors_got = [
        wires.send(vectors_one, vectors_plane.at[mask - 1], wires.at_plane(mask)) for mask in masks
    ]
    last, passed = [], []

    def hand_round(slot):
        for mask in masks:
            passed.append((slot, mask, wires.send(slot(spot), slot(spot), wires.at_plane(mask))))
        last.append(wires.send(slot(spot), slot(spot), wires.at_core()))

    def hand_over():
        while passed:
            slot, mask, copy = passed.pop(0)
            copy.wait_recv()
            ref = slot(wires.spot(mask))
            last.append(wires.send(ref, ref, wires.at_core()))

    def units_whole(which):
        for copy in units_got[which]:
            copy.wait_recv()
        total = wide(units[which, 0])
        for z in ahead:
            total = total + wide(units_z[which, z - 1])
        units_out[which, core, spot] = total.astype(LOW)
        hand_round(lambda place: units_out.at[which, core, place])

    for copy in plane_got[0]:
        copy.wait_recv()
    total = wide(later_half[spot])
    for mask in masks:
        total = total + wide(later_plane[mask - 1])
    triple_mine[...] = total.astype(LOW)
    triple_got = [wires.send(triple_mine, triple_z, wires.at_member(0, 1))]
    for copy in plane_got[1]:
        copy.wait_recv()
    total = wide(output_half[spot])
    for mask in masks:
        total = total + wide(output_plane[mask - 1])
    output_mine[...] = total.astype(LOW)
    output_got = [
        wires.send(output_mine.at[z], output_z.at[z - 1], wires.at_member(*offsets[z])) for z in ahead
    ]
    units_got.append(units_along(1))
    for copy in vectors_got:
        copy.wait_recv()
    total = vectors_one[...]
    for mask in masks:
        total = total + vectors_plane[mask - 1]
    vectors_two[...] = total
    vectors_got = [
        wires.send(vectors_two, vectors_z.at[z - 1], wires.at_member(*offsets[z])) for z in ahead
    ]
    units_whole(0)
    for copy in plane_got[2]:
        copy.wait_recv()
    for copy in triple_got:
        copy.wait_recv()
    total = wide(now_half[spot]) + wide(triple_z[...])
    for mask in masks:
        total = total + wide(now_plane[mask - 1])
    triple_out[spot, core] = total.astype(LOW)
    hand_round(lambda place: triple_out.at[place, core])
    for copy in output_got:
        copy.wait_recv()
    total = wide(output_mine[0])
    for z in ahead:
        total = total + wide(output_z[z - 1])
    output_out[spot, core] = total.astype(LOW)
    hand_round(lambda place: output_out.at[place, core])
    hand_over()
    units_whole(1)
    for copy in vectors_got:
        copy.wait_recv()
    total = vectors_two[...]
    for z in ahead:
        total = total + vectors_z[z - 1]
    vectors_out[...] = total
    hand_over()
    for copy in last:
        copy.wait_recv()
    wires.finish()


def sum_all(plane, seq_dev, units, later, now, output, vectors, before):
    tensor, quarters = lax.axis_size("tensor"), 2 ** len(plane)
    subs, masks = tensor // seq_dev, quarters - 1
    piece, share, out_share = units.shape[2:], later.shape[2:], output.shape[3:]
    low = lambda *shape: pltpu.VMEM(shape, LOW)
    full = lambda *shape: pltpu.VMEM(shape + vectors.shape, F32)
    copies = (
        3 * quarters + 1 + 2 * (tensor - 1) + 3 * masks + masks + 1 + 2 * (tensor - 1)
        + 4 * (masks + 1 + masks)
    )
    return pl.pallas_call(
        functools.partial(sum_kernel, plane, subs, seq_dev, len(before)),
        in_specs=[pl.BlockSpec(memory_space=pltpu.VMEM)] * 5
        + [pl.BlockSpec(memory_space=pl.ANY)] * len(before),
        out_specs=[pl.BlockSpec(memory_space=pltpu.VMEM)] * 4,
        out_shape=[
            jax.ShapeDtypeStruct((2, 2, quarters) + piece, LOW),
            jax.ShapeDtypeStruct((quarters, 2) + share, LOW),
            jax.ShapeDtypeStruct((quarters, 2) + out_share, LOW),
            jax.ShapeDtypeStruct(vectors.shape, F32),
        ],
        scratch_shapes=[
            low(2, tensor - 1, *piece),
            low(quarters, *share),
            low(quarters, *share),
            low(quarters, tensor, *out_share),
            low(quarters, *share),
            low(quarters, *share),
            low(quarters, tensor, *out_share),
            low(masks, *share),
            low(masks, *share),
            low(masks, tensor, *out_share),
            low(*share),
            low(tensor - 1, *out_share),
            low(*share),
            low(tensor, *out_share),
            full(),
            full(masks),
            full(tensor - 1),
            full(),
            full(),
            pltpu.SemaphoreType.DMA((copies,)),
            pltpu.SemaphoreType.DMA((copies,)),
        ],
        compiler_params=pltpu.CompilerParams(
            collective_id=1, has_side_effects=True, vmem_limit_bytes=48 << 20
        ),
        cost_estimate=pl.CostEstimate(flops=1 << 24, bytes_accessed=1 << 27, transcendentals=0),
    )(units, later, now, output, vectors, *before)


def gather_kernel(
    plane, subs, seq_dev, stream, triple, output, units, small,
    stream_out, triple_out, output_out, early_out, rest_out, small_out, send_sems, recv_sems,
):
    wires = Wires(plane, subs, seq_dev, send_sems, recv_sems)
    quarters, core = wires.quarters, wires.core
    offsets = [(k, j) for k in range(subs) for j in range(seq_dev)]
    ahead = range(1, len(offsets))
    masks = range(1, quarters)
    wires.greet(
        [wires.at_core()]
        + [wires.at_plane(mask) for mask in masks]
        + [wires.at_member(k, j) for k, j in offsets[1:]]
    )
    mine = 2 * wires.spot() + core
    share, out_share = triple_out.shape[1:], output_out.shape[2:]
    back = lambda z: wires.at_member(-offsets[z][0], -offsets[z][1])
    triple_got = wires.send(triple.at[mine], triple_out.at[mine], back(1))
    stream_got = [wires.send(stream, stream_out.at[k - 1], wires.at_member(-k, 0)) for k in range(1, subs)]
    output_got = [wires.send(output.at[mine], output_out.at[z - 1, mine], back(z)) for z in ahead]
    small_got = [wires.send(small, small_out.at[z - 1], back(z)) for z in ahead]
    early_got = wires.send(units, early_out.at[0], back(1))
    triple_got.wait_recv()
    last, passed = [], []
    ref = triple_out.at[mine]
    for mask in masks:
        passed.append((triple_out, mask, wires.send(ref, ref, wires.at_plane(mask))))
    last.append(wires.send(ref, ref, wires.at_core()))
    for copy in output_got:
        copy.wait_recv()
    rest_got = [wires.send(units, rest_out.at[z - 2], back(z)) for z in ahead if z > 1]
    output_passed = []
    for mask in masks:
        for z in ahead:
            ref = output_out.at[z - 1, mine]
            output_passed.append((z, mask, wires.send(ref, ref, wires.at_plane(mask))))
    for z in ahead:
        ref = output_out.at[z - 1, mine]
        last.append(wires.send(ref, ref, wires.at_core()))
    for _, mask, copy in passed:
        copy.wait_recv()
        ref = triple_out.at[2 * wires.spot(mask) + core]
        last.append(wires.send(ref, ref, wires.at_core()))
    early_got.wait_recv()
    for mask in masks:
        last.append(wires.send(early_out.at[0], early_out.at[mask], wires.at_plane(mask)))
    for z, mask, copy in output_passed:
        copy.wait_recv()
        ref = output_out.at[z - 1, 2 * wires.spot(mask) + core]
        last.append(wires.send(ref, ref, wires.at_core()))
    for copy in small_got + stream_got + rest_got + last:
        copy.wait_recv()
    wires.finish()


def gather_all(plane, seq_dev, stream, triple, output, units, small):
    tensor, quarters = lax.axis_size("tensor"), 2 ** len(plane)
    subs, masks = tensor // seq_dev, quarters - 1
    others = tensor - 1
    copies = 2 + subs - 1 + 2 * others + 2 * quarters - 1 + 2 * others * quarters + others + masks
    return pl.pallas_call(
        functools.partial(gather_kernel, plane, subs, seq_dev),
        in_specs=[pl.BlockSpec(memory_space=pltpu.VMEM)] * 5,
        out_specs=[pl.BlockSpec(memory_space=pltpu.VMEM)] * 6,
        out_shape=[
            jax.ShapeDtypeStruct((subs - 1,) + stream.shape, LOW),
            jax.ShapeDtypeStruct(triple.shape, LOW),
            jax.ShapeDtypeStruct((others,) + output.shape, LOW),
            jax.ShapeDtypeStruct((quarters,) + units.shape, LOW),
            jax.ShapeDtypeStruct((others - 1,) + units.shape, LOW),
            jax.ShapeDtypeStruct((others,) + small.shape, F32),
        ],
        scratch_shapes=[
            pltpu.SemaphoreType.DMA((copies,)),
            pltpu.SemaphoreType.DMA((copies,)),
        ],
        compiler_params=pltpu.CompilerParams(
            collective_id=2, has_side_effects=True, vmem_limit_bytes=32 << 20
        ),
        cost_estimate=pl.CostEstimate(flops=1 << 20, bytes_accessed=1 << 27, transcendentals=0),
    )(stream, triple, output, units, small)


def gaussian_pair(value):
    cumulative = 0.5 * (1.0 + jax.scipy.special.erf(value * (1.0 / math.sqrt(2.0))))
    slope = cumulative + value * jnp.exp(-0.5 * value * value) * (1.0 / math.sqrt(2.0 * math.pi))
    return (value * cumulative).astype(LOW), slope.astype(LOW)


def on_device(
    plane,
    stream_in,
    timestep,
    lengths,
    time_weight,
    time_bias,
    triple_weight,
    query_value_bias,
    output_weight,
    output_bias,
    first_gain,
    first_shift,
    up_weight,
    up_bias,
    down_weight,
    down_bias,
    second_gain,
    second_shift,
    cotangent,
):
    rows, width = stream_in.shape
    seq_dev = timestep.shape[0]
    tensor = lax.axis_size("tensor")
    subs = tensor // seq_dev
    local = triple_weight.shape[2]
    units = up_weight.shape[1]
    half_units = units // 2
    quarters = 2 ** len(plane)
    piece_units = half_units // quarters
    me = lax.axis_index("tensor")
    core = lax.axis_index("core")
    spot = lax.axis_index(plane)
    sub = me % subs
    which = me // subs
    offsets = [(k, j) for k in range(subs) for j in range(seq_dev)]
    others = offsets[1:]

    def member(i, k, j):
        return ((i // subs + j) % seq_dev) * subs + (i % subs + k) % subs

    def fetch(x, k, j):
        return lax.ppermute(x, "tensor", [(member(i, k, j), i) for i in range(tensor)])

    def send(x, k, j):
        return lax.ppermute(x, "tensor", [(i, member(i, k, j)) for i in range(tensor)])

    def swap(x, axis):
        return lax.ppermute(x, axis, [(0, 1), (1, 0)])

    def across(x, mask):
        return lax.ppermute(x, plane, [(i, i ^ mask) for i in range(quarters)])

    def pick(x, index, axis=0):
        return lax.dynamic_index_in_dim(x, index, axis, keepdims=False)

    def tie(x, *before):
        return lax.optimization_barrier((x,) + before)[0]

    def ordered(parts, index):
        parts = jnp.stack(parts) if isinstance(parts, (list, tuple)) else parts
        return jnp.stack([pick(parts, index ^ m) for m in range(parts.shape[0])])

    triple_own = triple_weight.reshape(width, 3 * local)
    part = width // (2 * quarters)
    out_part = local // (2 * quarters)
    up_half = lax.dynamic_slice_in_dim(up_weight, core * half_units, half_units, 1).T
    down_half = lax.dynamic_slice_in_dim(down_weight, core * half_units, half_units, 0)
    units_mine = [
        ordered(x.reshape(quarters, piece_units, width), spot) for x in (up_half, down_half)
    ]
    small = jnp.concatenate([up_bias, query_value_bias.reshape(-1)])
    pad = -small.shape[0] % 1024
    raw, triple_got, out_got, early, rest, small_got = gather_all(
        plane,
        seq_dev,
        stream_in,
        triple_own.reshape(2 * quarters, part, 3 * local),
        output_weight.reshape(2 * quarters, out_part, width),
        jnp.stack([units_mine[0][0], units_mine[1][0]]),
        jnp.pad(small, (0, pad)).reshape(-1, 128),
    )
    raw = [stream_in] + [raw[k] for k in range(subs - 1)]
    triples = [triple_own, triple_got.reshape(width, 3 * local)]
    out_got = out_got.reshape(tensor - 1, local, width)
    out_full = jnp.concatenate([output_weight[None], out_got]).reshape(tensor * local, width)
    small_of = {(0, 0): small}
    for z, (k, j) in enumerate(others):
        small_of[(k, j)] = small_got[z].reshape(-1)[: small.shape[0]]
    rest_of = [rest] + [across(rest, m) for m in range(1, quarters)]

    def all_rows(which):
        full = []
        for m in range(quarters):
            full += [units_mine[which][m][None], early[m, which][None], rest_of[m][:, which]]
        return jnp.concatenate(full, axis=0).reshape(-1, width)

    up_rows, down_rows = all_rows(0), all_rows(1)

    embedded_own = sinusoid(timestep, width).astype(LOW)
    shift_own = plain(embedded_own, time_weight) + time_bias
    shift_row = pick(shift_own, which)
    limit = pick(lengths, which)
    stream = stream_in.astype(F32) + shift_row
    stream_low = (jnp.concatenate(raw, axis=0).astype(F32) + shift_row).astype(LOW)
    place = (jnp.arange(LEN, dtype=jnp.int32) + sub * rows) % LEN
    mask = jnp.where(place < limit, 0.0, MASKED).astype(F32)
    mask_row, mask_column = mask[None, :], mask[:, None]
    valid = (place[:rows] < limit).astype(F32)

    pairs = local // (2 * HD)
    qv = [small_of[(0, j)][units:].reshape(2, local) for j in range(seq_dev)]
    projected, context, log_total = [], [], []
    for j in range(seq_dev):
        bias = jnp.concatenate([qv[j][0], jnp.zeros((local,), F32), qv[j][1]])
        projected.append(plain(stream_low, triples[j]) + bias)
        here = [attend(projected[j], mask_row, pair) for pair in range(pairs)]
        context.append([x[0] for x in here])
        log_total.append([x[1] for x in here])
    block = lambda x, k: x[k * rows : (k + 1) * rows]
    columns = []
    for k in range(subs):
        back = (subs - k) % subs
        for j in range(seq_dev):
            mine = jnp.concatenate([block(x, back) for x in context[j]], axis=1).astype(LOW)
            columns.append(mine if k == 0 else send(mine, back, 0))
    context_own = jnp.concatenate(columns, axis=1)

    branch = plain(context_own, out_full) + output_bias
    middle, normed_first, factor_first = norm_forward(stream + branch, first_gain, first_shift)
    middle_low = middle.astype(LOW)

    bias_all = jnp.stack([small_of[o][:units] for o in offsets])
    bias_half = lax.dynamic_slice_in_dim(bias_all, core * half_units, half_units, 1)
    bias_rel = ordered(
        bias_half.reshape(tensor, quarters, piece_units).transpose(1, 0, 2), spot
    ).reshape(-1)
    both = jnp.concatenate([middle_low, swap(middle_low, "core")], axis=0)
    active, slope = gaussian_pair(against(both, up_rows) + bias_rel)
    feed_other = plain(active[rows:], down_rows).astype(LOW)
    feed = plain(active[:rows], down_rows) + swap(feed_other, "core").astype(F32) + down_bias
    result, normed_second, factor_second = norm_forward(middle + feed, second_gain, second_shift)
    block_output = result.astype(LOW)

    to_second, grad_second_gain, grad_second_shift = norm_backward(
        cotangent.astype(F32), normed_second, factor_second, second_gain
    )
    feed_grad = to_second.astype(LOW)
    grad_down_bias = jnp.sum(feed_grad.astype(F32), axis=0)
    feed_grad_both = jnp.concatenate([feed_grad, swap(feed_grad, "core")], axis=0)

    def by_mask(total):
        shaped = total.reshape(quarters, tensor, piece_units, width)
        return {m: shaped[m] for m in range(quarters)}

    down_total = by_mask(inner(active, feed_grad_both).astype(LOW))
    before_grad = (against(feed_grad_both, down_rows) * slope.astype(F32)).astype(LOW)
    up_total = by_mask(inner(before_grad, both).astype(LOW))
    units_sum = wide(jnp.stack([up_total[0], down_total[0]]))
    for m in range(1, quarters):
        units_sum = units_sum + wide(across(jnp.stack([up_total[m], down_total[m]]), m))
    units_sum = units_sum.astype(LOW)
    grad_up_rel = jnp.sum(before_grad.astype(F32), axis=0)
    middle_other = plain(before_grad[rows:], up_rows).astype(LOW)
    middle_grad = (
        to_second + plain(before_grad[:rows], up_rows) + swap(middle_other, "core").astype(F32)
    )

    to_first, grad_first_gain, grad_first_shift = norm_backward(
        middle_grad, normed_first, factor_first, first_gain
    )
    branch_grad = to_first.astype(LOW)
    grad_output_bias = jnp.sum(branch_grad.astype(F32), axis=0)
    context_grad = against(branch_grad, out_full).astype(LOW)
    shaped = context_grad.reshape(rows, subs, seq_dev, local)
    incoming = []
    for j in range(seq_dev):
        parts = []
        for k in range(subs):
            back = (subs - k) % subs
            mine = shaped[:, back, j]
            parts.append(mine if k == 0 else send(mine, back, 0))
        incoming.append(jnp.concatenate(parts, axis=0).astype(F32))

    def backward(j, pair, before):
        return attend_back(
            projected[j], mask_column, context[j][pair], log_total[j][pair], incoming[j], pair, before
        )

    def together(parts):
        return jnp.concatenate([x[i] for i in range(3) for x in parts], axis=1).astype(LOW)

    grads = [None] * seq_dev
    for j in reversed(range(seq_dev)):
        grads[j] = together([backward(j, pair, []) for pair in range(pairs)])
    triple_parts = [
        inner(stream_low, grads[j]).astype(LOW).reshape(quarters, 2, part, 3 * local)
        for j in range(seq_dev)
    ]
    out_total = inner(context_own, branch_grad).astype(LOW)
    out_total = out_total.reshape(tensor, quarters, 2, out_part, width).transpose(1, 2, 0, 3, 4)
    away = [
        send(
            sum(against(block(grads[j], k), triples[j]) for j in range(seq_dev)).astype(LOW), k, 0
        )
        for k in range(1, subs)
    ]
    stream_own = to_first + sum(
        against(block(grads[j], 0), triples[j]) for j in range(seq_dev)
    )

    dp_index = spot * 2 + core
    seqs = quarters * 2 * seq_dev
    column_sums = [jnp.sum(grads[j].astype(F32), axis=0) for j in range(seq_dev)]
    shift_part = jnp.sum(to_first, axis=0) + sum(
        against(column_sums[j][None].astype(F32), triples[j].astype(F32))[0]
        for j in range(seq_dev)
    )
    hot = (jnp.arange(seqs) == dp_index * seq_dev + which).astype(F32)
    shift_rows = hot[:, None] * shift_part[None, :]
    squares = jnp.stack([jnp.sum(jnp.sum(x * x, axis=1) * valid) for x in (stream, branch, feed)])
    table = hot[:, None] * squares[None, :]
    steps_hot = (
        jnp.arange(seqs)[:, None] == dp_index * seq_dev + jnp.arange(seq_dev)[None, :]
    ).astype(F32)
    steps_all = jnp.sum(steps_hot * timestep.astype(F32)[None, :], axis=1) * (me == 0)
    up_canonical = ordered(grad_up_rel.reshape(quarters, tensor, piece_units), spot)
    up_canonical = up_canonical.transpose(1, 0, 2).reshape(tensor, half_units)
    full_up = jnp.zeros((tensor, 2, half_units), F32)
    full_qv = jnp.zeros((tensor, 2, local), F32)
    for index, (k, j) in enumerate(offsets):
        at = ((which + j) % seq_dev) * subs + (sub + k) % subs
        row = jnp.where(jnp.arange(2)[:, None] == core, up_canonical[index][None], 0.0)
        full_up = lax.dynamic_update_slice_in_dim(full_up, row[None], at, 0)
        if k == 0:
            value = column_sums[j].reshape(3, local)
            value = jnp.stack([value[0], value[2]])
            full_qv = lax.dynamic_update_slice_in_dim(full_qv, value[None], at, 0)

    vectors = [
        grad_first_gain,
        grad_first_shift,
        grad_output_bias,
        grad_down_bias,
        grad_second_gain,
        grad_second_shift,
        full_up.reshape(-1),
        shift_rows.reshape(-1),
        full_qv.reshape(-1),
        table.reshape(-1),
        steps_all,
    ]
    packed = jnp.concatenate(vectors)
    packed = jnp.pad(packed, (0, -packed.shape[0] % width)).reshape(-1, width)
    units_all, triple_all, out_all, packed = sum_all(
        plane, seq_dev, units_sum, triple_parts[1], triple_parts[0], out_total, packed, away
    )
    units_all = units_all.reshape(2, units, width)
    grad_up_weight = units_all[0].T.astype(F32)
    grad_down_weight = units_all[1].astype(F32)
    grad_output_weight = out_all.reshape(local, width).astype(F32)
    grad_triple = triple_all.astype(F32).reshape(width, 3, local)
    input_gradient = (stream_own + sum(wide(x) for x in away)).astype(LOW)
    packed = packed.reshape(-1)
    got, at = [], 0
    for vector in vectors:
        got.append(packed[at : at + vector.shape[0]])
        at += vector.shape[0]
    full_up = pick(got[6].reshape(tensor, units), me)
    shift_grad = got[7].reshape(seqs, width)
    grad_query_value = pick(got[8].reshape(tensor, 2, local), me)
    table, steps_all = got[9].reshape(seqs, 3), got[10]
    grad_time_bias = jnp.sum(shift_grad, axis=0)
    embedded_all = sinusoid(steps_all, width).astype(LOW).astype(F32)
    grad_time_weight = lax.dot_general(
        embedded_all, shift_grad, TN, precision=lax.Precision.HIGHEST, preferred_element_type=F32
    )
    own_table = lax.dynamic_slice_in_dim(table, dp_index * seq_dev, seq_dev, 0)
    root_squares = jnp.sqrt(own_table / (lengths.astype(F32)[:, None] * width) + STAT_EPS)
    return (
        block_output,
        input_gradient,
        root_squares,
        grad_time_weight,
        grad_time_bias,
        grad_triple,
        grad_query_value,
        grad_output_weight,
        got[2],
        got[0],
        got[1],
        grad_up_weight,
        full_up,
        grad_down_weight,
        got[3],
        got[4],
        got[5],
    )


def solution(mesh):
    tensor = mesh.shape["tensor"]
    spots = mesh.shape["dp"] // 2
    plane = tuple(f"plane{i}" for i in range(spots.bit_length() - 1))
    fine = Mesh(
        mesh.devices.reshape((2,) * len(plane) + (2, tensor)), plane + ("core", "tensor")
    )
    dp = plane + ("core",)
    row = P(dp + ("tensor",), None)
    in_specs = (
        row,
        P(dp),
        P(dp),
        P(),
        P(),
        P(None, None, "tensor"),
        P(None, "tensor"),
        P("tensor", None),
        P(),
        P(),
        P(),
        P(None, "tensor"),
        P("tensor"),
        P("tensor", None),
        P(),
        P(),
        P(),
        row,
    )
    out_specs = (
        row,
        row,
        P(dp, None),
        P(),
        P(),
        P(None, None, "tensor"),
        P(None, "tensor"),
        P("tensor", None),
        P(),
        P(),
        P(),
        P(None, "tensor"),
        P("tensor"),
        P("tensor", None),
        P(),
        P(),
        P(),
    )
    return jax.shard_map(
        functools.partial(on_device, plane),
        mesh=fine,
        in_specs=in_specs,
        out_specs=out_specs,
        check_vma=False,
    )
```

```python
import functools
import math

import jax
import jax.numpy as jnp
from jax import lax
from jax.experimental import pallas as pl
from jax.experimental.pallas import tpu as pltpu
from jax.sharding import Mesh
from jax.sharding import PartitionSpec as P

HD = 64
LEN = 1024
NORM_EPS = 1e-05
STAT_EPS = 1e-06
MASKED = -1e30
LOW = jnp.bfloat16
F32 = jnp.float32
NT = (((1,), (1,)), ((), ()))
TN = (((0,), (0,)), ((), ()))


def sinusoid(steps, width):
    half = width // 2
    rates = jnp.exp(-math.log(10000.0) * jnp.arange(half).astype(F32) / half)
    angles = steps.astype(F32)[:, None] * rates[None, :]
    return jnp.concatenate([jnp.sin(angles), jnp.cos(angles)], axis=1)


def plain(left, right):
    return jnp.dot(left, right, preferred_element_type=F32)


def inner(left, right):
    return lax.dot_general(left, right, TN, preferred_element_type=F32)


def against(left, right):
    return lax.dot_general(left, right, NT, preferred_element_type=F32)


def norm_forward(total, gain, shift):
    middle = jnp.mean(total, axis=-1, keepdims=True)
    centred = total - middle
    spread = jnp.mean(centred * centred, axis=-1, keepdims=True)
    factor = lax.rsqrt(spread + NORM_EPS)
    normed = centred * factor
    return (normed * gain + shift, normed, factor)


def norm_backward(upstream, normed, factor, gain):
    pushed = upstream * gain
    first = jnp.mean(pushed, axis=-1, keepdims=True)
    second = jnp.mean(pushed * normed, axis=-1, keepdims=True)
    return (
        factor * (pushed - first - normed * second),
        jnp.sum(upstream * normed, axis=0),
        jnp.sum(upstream, axis=0),
    )


def split3(x):
    hi = x.astype(LOW)
    rest = x - hi.astype(F32)
    mid = rest.astype(LOW)
    return hi, mid, (rest - mid.astype(F32)).astype(LOW)


def extra_lanes(parts, one, count):
    lane = lax.broadcasted_iota(jnp.int32, (count, HD), 1)
    out = jnp.where(lane == len(parts), 1.0, 0.0) if one else jnp.zeros((count, HD), F32)
    for index, part in enumerate(parts):
        out = jnp.where(lane == index, jnp.broadcast_to(part.astype(F32), (count, HD)), out)
    return out.astype(LOW)


def head(x, h):
    return x[:, h * HD : (h + 1) * HD]


def attend_kernel(rows, mask_ref, q_ref, k_ref, v_ref, context_ref, log_ref):
    count = q_ref.shape[0]
    mask = mask_ref[...]
    keys = k_ref[...].astype(LOW)
    values = v_ref[...].astype(LOW)
    for start in range(0, count, rows):
        part = slice(start, start + rows)
        queries = q_ref[part].astype(LOW) * LOW(HD**-0.5)
        contexts, logs = [], []
        for h in range(2):
            scores = lax.dot_general(
                head(queries, h), head(keys, h), NT, preferred_element_type=F32
            )
            scores = scores + mask
            highest = jnp.max(scores, axis=1, keepdims=True)
            probs = jnp.exp(scores - highest)
            total = jnp.sum(probs, axis=1, keepdims=True)
            contexts.append(plain(probs.astype(LOW), head(values, h)) / total)
            logs.append(jnp.broadcast_to(highest + jnp.log(total), (rows, HD)))
        context_ref[part] = jnp.concatenate(contexts, axis=1)
        log_ref[part] = jnp.concatenate(logs, axis=1)


def attend(projected, mask_row, pair):
    count, width = projected.shape
    local = width // 3
    pairs = local // (2 * HD)
    block = lambda which: pl.BlockSpec((count, 2 * HD), lambda p: (0, which * pairs + pair))
    whole = pl.BlockSpec((count, 2 * HD), lambda p: (0, 0))
    return pl.pallas_call(
        functools.partial(attend_kernel, 512),
        grid=(1,),
        in_specs=[pl.BlockSpec((1, count), lambda p: (0, 0)), block(0), block(1), block(2)],
        out_specs=[whole] * 2,
        out_shape=[jax.ShapeDtypeStruct((count, 2 * HD), F32)] * 2,
        compiler_params=pltpu.CompilerParams(vmem_limit_bytes=40 << 20),
        cost_estimate=pl.CostEstimate(
            flops=16 * count * count * 2 * HD,
            bytes_accessed=40 * count * HD,
            transcendentals=2 * count * count,
        ),
    )(mask_row, projected, projected, projected)


def attend_back_kernel(
    rows, mask_ref, q_ref, k_ref, v_ref, context_ref, log_ref, grad_ref, *refs
):
    dq_ref, dk_ref, dv_ref = refs[-3:]
    count = k_ref.shape[0]
    lane = lax.broadcasted_iota(jnp.int32, (count, HD), 1)
    three = jnp.where(lane < 3, 1.0, 0.0)
    key_extra = jnp.where(lane == 3, jnp.broadcast_to(mask_ref[...], (count, HD)), three)
    key_extra = key_extra.astype(LOW)
    value_extra = three.astype(LOW)
    queries = q_ref[...].astype(LOW) * LOW(HD**-0.5)
    keys = k_ref[...].astype(LOW)
    values = v_ref[...].astype(LOW)
    logs = log_ref[...]
    grads = grad_ref[...]
    dots = grads * context_ref[...]
    grads = grads.astype(LOW)
    kx, vx, qx, gx, dq = [], [], [], [], [None, None]
    for h in range(2):
        extra = extra_lanes(split3(-logs[:, h * HD : h * HD + 1]), True, count)
        qx.append(jnp.concatenate([head(queries, h), extra], axis=1))
        row_dot = jnp.sum(head(dots, h), axis=1, keepdims=True)
        extra = extra_lanes(split3(-row_dot), False, count)
        gx.append(jnp.concatenate([head(grads, h), extra], axis=1))
        kx.append(jnp.concatenate([head(keys, h), key_extra], axis=1))
        vx.append(jnp.concatenate([head(values, h), value_extra], axis=1))
    for start in range(0, count, rows):
        part = slice(start, start + rows)
        dk, dv = [], []
        for h in range(2):
            probs = jnp.exp(lax.dot_general(kx[h][part], qx[h], NT, preferred_element_type=F32))
            pushed = lax.dot_general(vx[h][part], gx[h], NT, preferred_element_type=F32)
            scores_grad = (probs * pushed).astype(LOW)
            dv.append(plain(probs.astype(LOW), gx[h])[:, :HD])
            dk.append(plain(scores_grad, qx[h])[:, :HD])
            more = lax.dot_general(scores_grad, kx[h][part], TN, preferred_element_type=F32)
            dq[h] = more if start == 0 else dq[h] + more
        dk_ref[part] = jnp.concatenate(dk, axis=1)
        dv_ref[part] = jnp.concatenate(dv, axis=1)
    dq_ref[...] = jnp.concatenate([x[:, :HD] for x in dq], axis=1) * HD**-0.5


def attend_back(projected, mask_column, context, log_total, grad, pair, before):
    count, width = projected.shape
    local = width // 3
    pairs = local // (2 * HD)
    block = lambda which: pl.BlockSpec((count, 2 * HD), lambda p: (0, which * pairs + pair))
    whole = pl.BlockSpec((count, 2 * HD), lambda p: (0, 0))
    return pl.pallas_call(
        functools.partial(attend_back_kernel, 512),
        grid=(1,),
        in_specs=[pl.BlockSpec((count, 1), lambda p: (0, 0)), block(0), block(1), block(2)]
        + [whole, whole, block(0)]
        + [pl.BlockSpec(memory_space=pl.ANY)] * len(before),
        out_specs=[whole] * 3,
        out_shape=[jax.ShapeDtypeStruct((count, 2 * HD), F32)] * 3,
        compiler_params=pltpu.CompilerParams(vmem_limit_bytes=50 << 20),
        cost_estimate=pl.CostEstimate(
            flops=40 * count * count * 2 * HD,
            bytes_accessed=80 * count * HD,
            transcendentals=2 * count * count,
        ),
    )(mask_column, projected, projected, projected, context, log_total, grad, *before)


class Wires:
    def __init__(self, plane, subs, seq_dev, send_sems, recv_sems):
        self.plane, self.subs, self.seq_dev = plane, subs, seq_dev
        self.send_sems, self.recv_sems, self.sent = send_sems, recv_sems, []
        self.bits = [lax.axis_index(name) for name in plane]
        self.core = lax.axis_index("core")
        me = lax.axis_index("tensor")
        self.sub, self.which = lax.rem(me, subs), lax.div(me, subs)
        self.quarters = 2 ** len(plane)

    def spot(self, mask=0):
        total, count = 0, len(self.plane)
        for i, bit in enumerate(self.bits):
            flip = (mask >> (count - 1 - i)) & 1
            total = total + (1 - bit if flip else bit) * 2 ** (count - 1 - i)
        return total

    def at_plane(self, mask):
        count = len(self.plane)
        return {
            name: 1 - bit
            for i, (name, bit) in enumerate(zip(self.plane, self.bits))
            if (mask >> (count - 1 - i)) & 1
        }

    def at_core(self):
        return {"core": 1 - self.core}

    def at_member(self, k, j):
        return {
            "tensor": lax.rem(self.which + j + self.seq_dev, self.seq_dev) * self.subs
            + lax.rem(self.sub + k + self.subs, self.subs)
        }

    def greet(self, targets):
        barrier = pltpu.get_barrier_semaphore()
        for target in targets:
            pl.semaphore_signal(barrier, inc=1, device_id=target, device_id_type=pl.DeviceIdType.MESH)
        pl.semaphore_wait(barrier, len(targets))

    def send(self, src, dst, target):
        index = len(self.sent)
        copy = pltpu.make_async_remote_copy(
            src_ref=src,
            dst_ref=dst,
            send_sem=self.send_sems.at[index],
            recv_sem=self.recv_sems.at[index],
            device_id=target,
            device_id_type=pl.DeviceIdType.MESH,
        )
        copy.start()
        self.sent.append(copy)
        return copy

    def finish(self):
        for copy in self.sent:
            copy.wait_send()


def wide(x):
    return x.astype(F32)


def sum_kernel(
    plane, subs, seq_dev, ordering, units, later, now, output, vectors, *refs
):
    (
    units_out, triple_out, output_out, vectors_out, up_out,
    units_z, later_core, now_core, output_core, later_half, now_half, output_half,
    later_plane, now_plane, output_plane, triple_z, output_z, triple_mine, output_mine,
    vectors_core, vectors_plane, vectors_z, vectors_one, vectors_two, send_sems, recv_sems,
    ) = refs[ordering:]
    wires = Wires(plane, subs, seq_dev, send_sems, recv_sems)
    quarters, core = wires.quarters, wires.core
    spot = wires.spot()
    offsets = [(k, j) for k in range(subs) for j in range(seq_dev)]
    ahead = range(1, len(offsets))
    masks = range(1, quarters)
    wires.greet(
        [wires.at_core()]
        + [wires.at_plane(mask) for mask in masks]
        + [wires.at_member(k, j) for k, j in offsets[1:]]
    )
    core_got = []
    for source, target in ((later, later_core), (output, output_core), (now, now_core)):
        core_got.append(
            [
                wires.send(source.at[place, 1 - core], target.at[place], wires.at_core())
                for place in range(quarters)
            ]
        )
    vectors_got = wires.send(vectors, vectors_core, wires.at_core())

    def units_along(which):
        return [
            wires.send(units.at[which, z], units_z.at[which, z - 1], wires.at_member(*offsets[z]))
            for z in ahead
        ]

    units_got = [units_along(0)]
    plane_got = []
    for got, source, received, half, target in (
        (core_got[0], later, later_core, later_half, later_plane),
        (core_got[1], output, output_core, output_half, output_plane),
        (core_got[2], now, now_core, now_half, now_plane),
    ):
        for copy in got:
            copy.wait_recv()
        for place in range(quarters):
            half[place] = (wide(source[place, core]) + wide(received[place])).astype(LOW)
        plane_got.append(
            [
                wires.send(half.at[wires.spot(mask)], target.at[mask - 1], wires.at_plane(mask))
                for mask in masks
            ]
        )
    vectors_got.wait_recv()
    vectors_one[...] = vectors[...] + vectors_core[...]
    vectors_got = [
        wires.send(vectors_one, vectors_plane.at[mask - 1], wires.at_plane(mask)) for mask in masks
    ]
    last, up_crossed, passed = [], [], []

    def hand_round(slot, crossed):
        for mask in masks:
            got = wires.send(slot(spot), slot(spot), wires.at_plane(mask))
            passed.append((slot, crossed, mask, got))
        crossed.append((0, wires.send(slot(spot), slot(spot), wires.at_core())))

    def hand_over():
        while passed:
            slot, crossed, mask, copy = passed.pop(0)
            copy.wait_recv()
            ref = slot(wires.spot(mask))
            crossed.append((mask, wires.send(ref, ref, wires.at_core())))

    def units_whole(which):
        for copy in units_got[which]:
            copy.wait_recv()
        total = wide(units[which, 0])
        for z in ahead:
            total = total + wide(units_z[which, z - 1])
        units_out[which, core, spot] = total.astype(LOW)
        hand_round(lambda place: units_out.at[which, core, place], last if which else up_crossed)

    for copy in plane_got[0]:
        copy.wait_recv()
    total = wide(later_half[spot])
    for mask in masks:
        total = total + wide(later_plane[mask - 1])
    triple_mine[...] = total.astype(LOW)
    triple_got = [wires.send(triple_mine, triple_z, wires.at_member(0, 1))]
    for copy in plane_got[1]:
        copy.wait_recv()
    total = wide(output_half[spot])
    for mask in masks:
        total = total + wide(output_plane[mask - 1])
    output_mine[...] = total.astype(LOW)
    output_got = [
        wires.send(output_mine.at[z], output_z.at[z - 1], wires.at_member(*offsets[z])) for z in ahead
    ]
    units_got.append(units_along(1))
    for copy in vectors_got:
        copy.wait_recv()
    total = vectors_one[...]
    for mask in masks:
        total = total + vectors_plane[mask - 1]
    vectors_two[...] = total
    vectors_got = [
        wires.send(vectors_two, vectors_z.at[z - 1], wires.at_member(*offsets[z])) for z in ahead
    ]
    units_whole(0)
    for copy in plane_got[2]:
        copy.wait_recv()
    for copy in triple_got:
        copy.wait_recv()
    total = wide(now_half[spot]) + wide(triple_z[...])
    for mask in masks:
        total = total + wide(now_plane[mask - 1])
    triple_out[spot, core] = total.astype(LOW)
    hand_round(lambda place: triple_out.at[place, core], last)
    for copy in output_got:
        copy.wait_recv()
    total = wide(output_mine[0])
    for z in ahead:
        total = total + wide(output_z[z - 1])
    output_out[spot, core] = total.astype(LOW)
    hand_round(lambda place: output_out.at[place, core], last)
    hand_over()
    units_whole(1)

    def place_up(half, mask):
        place = wires.spot(mask)
        up_out[half, place] = wide(units_out[0, half, place]).T

    for mask, copy in up_crossed:
        place_up(core, mask)
        copy.wait_recv()
        place_up(1 - core, mask)
    for copy in vectors_got:
        copy.wait_recv()
    total = vectors_two[...]
    for z in ahead:
        total = total + vectors_z[z - 1]
    vectors_out[...] = total
    hand_over()
    for _, copy in last:
        copy.wait_recv()
    wires.finish()


def sum_all(plane, seq_dev, units, later, now, output, vectors, before):
    tensor, quarters = lax.axis_size("tensor"), 2 ** len(plane)
    subs, masks = tensor // seq_dev, quarters - 1
    piece, share, out_share = units.shape[2:], later.shape[2:], output.shape[3:]
    low = lambda *shape: pltpu.VMEM(shape, LOW)
    full = lambda *shape: pltpu.VMEM(shape + vectors.shape, F32)
    copies = (
        3 * quarters + 1 + 2 * (tensor - 1) + 3 * masks + masks + 1 + 2 * (tensor - 1)
        + 4 * (masks + 1 + masks)
    )
    return pl.pallas_call(
        functools.partial(sum_kernel, plane, subs, seq_dev, len(before)),
        in_specs=[pl.BlockSpec(memory_space=pltpu.VMEM)] * 5
        + [pl.BlockSpec(memory_space=pl.ANY)] * len(before),
        out_specs=[pl.BlockSpec(memory_space=pltpu.VMEM)] * 5,
        out_shape=[
            jax.ShapeDtypeStruct((2, 2, quarters) + piece, LOW),
            jax.ShapeDtypeStruct((quarters, 2) + share, LOW),
            jax.ShapeDtypeStruct((quarters, 2) + out_share, LOW),
            jax.ShapeDtypeStruct(vectors.shape, F32),
            jax.ShapeDtypeStruct((2, quarters, piece[1], piece[0]), F32),
        ],
        scratch_shapes=[
            low(2, tensor - 1, *piece),
            low(quarters, *share),
            low(quarters, *share),
            low(quarters, tensor, *out_share),
            low(quarters, *share),
            low(quarters, *share),
            low(quarters, tensor, *out_share),
            low(masks, *share),
            low(masks, *share),
            low(masks, tensor, *out_share),
            low(*share),
            low(tensor - 1, *out_share),
            low(*share),
            low(tensor, *out_share),
            full(),
            full(masks),
            full(tensor - 1),
            full(),
            full(),
            pltpu.SemaphoreType.DMA((copies,)),
            pltpu.SemaphoreType.DMA((copies,)),
        ],
        compiler_params=pltpu.CompilerParams(
            collective_id=1, has_side_effects=True, vmem_limit_bytes=48 << 20
        ),
        cost_estimate=pl.CostEstimate(flops=1 << 24, bytes_accessed=1 << 27, transcendentals=0),
    )(units, later, now, output, vectors, *before)


def gather_kernel(
    plane, subs, seq_dev, stream, triple, output, units, small,
    stream_out, triple_out, output_out, early_out, rest_out, small_out, send_sems, recv_sems,
):
    wires = Wires(plane, subs, seq_dev, send_sems, recv_sems)
    quarters, core = wires.quarters, wires.core
    offsets = [(k, j) for k in range(subs) for j in range(seq_dev)]
    ahead = range(1, len(offsets))
    masks = range(1, quarters)
    wires.greet(
        [wires.at_core()]
        + [wires.at_plane(mask) for mask in masks]
        + [wires.at_member(k, j) for k, j in offsets[1:]]
    )
    mine = 2 * wires.spot() + core
    share, out_share = triple_out.shape[1:], output_out.shape[2:]
    back = lambda z: wires.at_member(-offsets[z][0], -offsets[z][1])
    triple_got = wires.send(triple.at[mine], triple_out.at[mine], back(1))
    output_got = [wires.send(output.at[mine], output_out.at[z - 1, mine], back(z)) for z in ahead]
    small_got = [wires.send(small, small_out.at[z - 1], back(z)) for z in ahead]
    triple_got.wait_recv()
    stream_got = [wires.send(stream, stream_out.at[k - 1], wires.at_member(-k, 0)) for k in range(1, subs)]
    last, passed = [], []
    ref = triple_out.at[mine]
    for mask in masks:
        passed.append((mask, wires.send(ref, ref, wires.at_plane(mask))))
    last.append(wires.send(ref, ref, wires.at_core()))
    for copy in output_got:
        copy.wait_recv()
    early_got = wires.send(units, early_out.at[0], back(1))
    output_passed = []
    for mask in masks:
        for z in ahead:
            ref = output_out.at[z - 1, mine]
            output_passed.append((z, mask, wires.send(ref, ref, wires.at_plane(mask))))
    for z in ahead:
        ref = output_out.at[z - 1, mine]
        last.append(wires.send(ref, ref, wires.at_core()))
    for mask, copy in passed:
        copy.wait_recv()
        ref = triple_out.at[2 * wires.spot(mask) + core]
        last.append(wires.send(ref, ref, wires.at_core()))
    early_got.wait_recv()
    rest_got = [wires.send(units, rest_out.at[z - 2], back(z)) for z in ahead if z > 1]
    for mask in masks:
        last.append(wires.send(early_out.at[0], early_out.at[mask], wires.at_plane(mask)))
    for z, mask, copy in output_passed:
        copy.wait_recv()
        ref = output_out.at[z - 1, 2 * wires.spot(mask) + core]
        last.append(wires.send(ref, ref, wires.at_core()))
    for copy in small_got + stream_got + rest_got + last:
        copy.wait_recv()
    wires.finish()


def gather_all(plane, seq_dev, stream, triple, output, units, small):
    tensor, quarters = lax.axis_size("tensor"), 2 ** len(plane)
    subs, masks = tensor // seq_dev, quarters - 1
    others = tensor - 1
    copies = 2 + subs - 1 + 2 * others + 2 * quarters - 1 + 2 * others * quarters + others + masks
    return pl.pallas_call(
        functools.partial(gather_kernel, plane, subs, seq_dev),
        in_specs=[pl.BlockSpec(memory_space=pltpu.VMEM)] * 5,
        out_specs=[pl.BlockSpec(memory_space=pltpu.VMEM)] * 6,
        out_shape=[
            jax.ShapeDtypeStruct((subs - 1,) + stream.shape, LOW),
            jax.ShapeDtypeStruct(triple.shape, LOW),
            jax.ShapeDtypeStruct((others,) + output.shape, LOW),
            jax.ShapeDtypeStruct((quarters,) + units.shape, LOW),
            jax.ShapeDtypeStruct((others - 1,) + units.shape, LOW),
            jax.ShapeDtypeStruct((others,) + small.shape, F32),
        ],
        scratch_shapes=[
            pltpu.SemaphoreType.DMA((copies,)),
            pltpu.SemaphoreType.DMA((copies,)),
        ],
        compiler_params=pltpu.CompilerParams(
            collective_id=2, has_side_effects=True, vmem_limit_bytes=32 << 20
        ),
        cost_estimate=pl.CostEstimate(flops=1 << 20, bytes_accessed=1 << 27, transcendentals=0),
    )(stream, triple, output, units, small)


def gaussian_pair(value):
    cumulative = 0.5 * (1.0 + jax.scipy.special.erf(value * (1.0 / math.sqrt(2.0))))
    slope = cumulative + value * jnp.exp(-0.5 * value * value) * (1.0 / math.sqrt(2.0 * math.pi))
    return (value * cumulative).astype(LOW), slope.astype(LOW)


def on_device(
    plane,
    stream_in,
    timestep,
    lengths,
    time_weight,
    time_bias,
    triple_weight,
    query_value_bias,
    output_weight,
    output_bias,
    first_gain,
    first_shift,
    up_weight,
    up_bias,
    down_weight,
    down_bias,
    second_gain,
    second_shift,
    cotangent,
):
    rows, width = stream_in.shape
    seq_dev = timestep.shape[0]
    tensor = lax.axis_size("tensor")
    subs = tensor // seq_dev
    local = triple_weight.shape[2]
    units = up_weight.shape[1]
    half_units = units // 2
    quarters = 2 ** len(plane)
    piece_units = half_units // quarters
    me = lax.axis_index("tensor")
    core = lax.axis_index("core")
    spot = lax.axis_index(plane)
    sub = me % subs
    which = me // subs
    offsets = [(k, j) for k in range(subs) for j in range(seq_dev)]
    others = offsets[1:]

    def member(i, k, j):
        return ((i // subs + j) % seq_dev) * subs + (i % subs + k) % subs

    def fetch(x, k, j):
        return lax.ppermute(x, "tensor", [(member(i, k, j), i) for i in range(tensor)])

    def send(x, k, j):
        return lax.ppermute(x, "tensor", [(i, member(i, k, j)) for i in range(tensor)])

    def swap(x, axis):
        return lax.ppermute(x, axis, [(0, 1), (1, 0)])

    def across(x, mask):
        return lax.ppermute(x, plane, [(i, i ^ mask) for i in range(quarters)])

    def pick(x, index, axis=0):
        return lax.dynamic_index_in_dim(x, index, axis, keepdims=False)

    def tie(x, *before):
        return lax.optimization_barrier((x,) + before)[0]

    def ordered(parts, index):
        parts = jnp.stack(parts) if isinstance(parts, (list, tuple)) else parts
        return jnp.stack([pick(parts, index ^ m) for m in range(parts.shape[0])])

    triple_own = triple_weight.reshape(width, 3 * local)
    part = width // (2 * quarters)
    out_part = local // (2 * quarters)
    up_half = lax.dynamic_slice_in_dim(up_weight, core * half_units, half_units, 1).T
    down_half = lax.dynamic_slice_in_dim(down_weight, core * half_units, half_units, 0)
    units_mine = [
        ordered(x.reshape(quarters, piece_units, width), spot) for x in (up_half, down_half)
    ]
    small = jnp.concatenate([up_bias, query_value_bias.reshape(-1)])
    pad = -small.shape[0] % 1024
    raw, triple_got, out_got, early, rest, small_got = gather_all(
        plane,
        seq_dev,
        stream_in,
        triple_own.reshape(2 * quarters, part, 3 * local),
        output_weight.reshape(2 * quarters, out_part, width),
        jnp.stack([units_mine[0][0], units_mine[1][0]]),
        jnp.pad(small, (0, pad)).reshape(-1, 128),
    )
    raw = [stream_in] + [raw[k] for k in range(subs - 1)]
    triples = [triple_own, triple_got.reshape(width, 3 * local)]
    out_got = out_got.reshape(tensor - 1, local, width)
    out_full = jnp.concatenate([output_weight[None], out_got]).reshape(tensor * local, width)
    small_of = {(0, 0): small}
    for z, (k, j) in enumerate(others):
        small_of[(k, j)] = small_got[z].reshape(-1)[: small.shape[0]]
    rest_of = [rest] + [across(rest, m) for m in range(1, quarters)]

    def all_rows(which):
        full = []
        for m in range(quarters):
            full += [units_mine[which][m][None], early[m, which][None], rest_of[m][:, which]]
        return jnp.concatenate(full, axis=0).reshape(-1, width)

    up_rows, down_rows = all_rows(0), all_rows(1)

    embedded_own = sinusoid(timestep, width).astype(LOW)
    shift_own = plain(embedded_own, time_weight) + time_bias
    shift_row = pick(shift_own, which)
    limit = pick(lengths, which)
    stream = stream_in.astype(F32) + shift_row
    stream_low = (jnp.concatenate(raw, axis=0).astype(F32) + shift_row).astype(LOW)
    place = (jnp.arange(LEN, dtype=jnp.int32) + sub * rows) % LEN
    mask = jnp.where(place < limit, 0.0, MASKED).astype(F32)
    mask_row, mask_column = mask[None, :], mask[:, None]
    valid = (place[:rows] < limit).astype(F32)

    pairs = local // (2 * HD)
    qv = [small_of[(0, j)][units:].reshape(2, local) for j in range(seq_dev)]
    projected, context, log_total = [], [], []
    for j in range(seq_dev):
        bias = jnp.concatenate([qv[j][0], jnp.zeros((local,), F32), qv[j][1]])
        projected.append(plain(stream_low, triples[j]) + bias)
        here = [attend(projected[j], mask_row, pair) for pair in range(pairs)]
        context.append([x[0] for x in here])
        log_total.append([x[1] for x in here])
    block = lambda x, k: x[k * rows : (k + 1) * rows]
    columns = []
    for k in range(subs):
        back = (subs - k) % subs
        for j in range(seq_dev):
            mine = jnp.concatenate([block(x, back) for x in context[j]], axis=1).astype(LOW)
            columns.append(mine if k == 0 else send(mine, back, 0))
    context_own = jnp.concatenate(columns, axis=1)

    branch = plain(context_own, out_full) + output_bias
    middle, normed_first, factor_first = norm_forward(stream + branch, first_gain, first_shift)
    middle_low = middle.astype(LOW)

    bias_all = jnp.stack([small_of[o][:units] for o in offsets])
    bias_half = lax.dynamic_slice_in_dim(bias_all, core * half_units, half_units, 1)
    bias_rel = ordered(
        bias_half.reshape(tensor, quarters, piece_units).transpose(1, 0, 2), spot
    ).reshape(-1)
    both = jnp.concatenate([middle_low, swap(middle_low, "core")], axis=0)
    active, slope = lax.optimization_barrier(
        gaussian_pair(against(both, up_rows) + bias_rel)
    )
    feed_other = plain(active[rows:], down_rows).astype(LOW)
    feed = plain(active[:rows], down_rows) + swap(feed_other, "core").astype(F32) + down_bias
    result, normed_second, factor_second = norm_forward(middle + feed, second_gain, second_shift)
    block_output = result.astype(LOW)

    to_second, grad_second_gain, grad_second_shift = norm_backward(
        cotangent.astype(F32), normed_second, factor_second, second_gain
    )
    feed_grad = to_second.astype(LOW)
    grad_down_bias = jnp.sum(feed_grad.astype(F32), axis=0)
    feed_grad_both = jnp.concatenate([feed_grad, swap(feed_grad, "core")], axis=0)

    def by_mask(total):
        shaped = total.reshape(quarters, tensor, piece_units, width)
        return {m: shaped[m] for m in range(quarters)}

    down_total = by_mask(inner(active, feed_grad_both).astype(LOW))
    before_grad = (against(feed_grad_both, down_rows) * slope.astype(F32)).astype(LOW)
    up_total = by_mask(inner(before_grad, both).astype(LOW))
    units_sum = wide(jnp.stack([up_total[0], down_total[0]]))
    for m in range(1, quarters):
        units_sum = units_sum + wide(across(jnp.stack([up_total[m], down_total[m]]), m))
    units_sum = units_sum.astype(LOW)
    grad_up_rel = jnp.sum(before_grad.astype(F32), axis=0)
    middle_other = plain(before_grad[rows:], up_rows).astype(LOW)
    middle_grad = (
        to_second + plain(before_grad[:rows], up_rows) + swap(middle_other, "core").astype(F32)
    )

    to_first, grad_first_gain, grad_first_shift = norm_backward(
        middle_grad, normed_first, factor_first, first_gain
    )
    branch_grad = to_first.astype(LOW)
    grad_output_bias = jnp.sum(branch_grad.astype(F32), axis=0)
    context_grad = against(branch_grad, out_full).astype(LOW)
    shaped = context_grad.reshape(rows, subs, seq_dev, local)
    incoming = []
    for j in range(seq_dev):
        parts = []
        for k in range(subs):
            back = (subs - k) % subs
            mine = shaped[:, back, j]
            parts.append(mine if k == 0 else send(mine, back, 0))
        incoming.append(jnp.concatenate(parts, axis=0).astype(F32))

    def backward(j, pair, before):
        return attend_back(
            projected[j], mask_column, context[j][pair], log_total[j][pair], incoming[j], pair, before
        )

    def together(parts):
        return jnp.concatenate([x[i] for i in range(3) for x in parts], axis=1).astype(LOW)

    grads = [None] * seq_dev
    for j in reversed(range(seq_dev)):
        grads[j] = together([backward(j, pair, []) for pair in range(pairs)])
    triple_parts = [
        inner(stream_low, grads[j]).astype(LOW).reshape(quarters, 2, part, 3 * local)
        for j in range(seq_dev)
    ]
    out_total = inner(context_own, branch_grad).astype(LOW)
    out_total = out_total.reshape(tensor, quarters, 2, out_part, width).transpose(1, 2, 0, 3, 4)
    away = [
        send(
            sum(against(block(grads[j], k), triples[j]) for j in range(seq_dev)).astype(LOW), k, 0
        )
        for k in range(1, subs)
    ]
    stream_own = to_first + sum(
        against(block(grads[j], 0), triples[j]) for j in range(seq_dev)
    )

    dp_index = spot * 2 + core
    seqs = quarters * 2 * seq_dev
    column_sums = [jnp.sum(grads[j].astype(F32), axis=0) for j in range(seq_dev)]
    shift_part = jnp.sum(to_first, axis=0) + sum(
        against(column_sums[j][None].astype(F32), triples[j].astype(F32))[0]
        for j in range(seq_dev)
    )
    hot = (jnp.arange(seqs) == dp_index * seq_dev + which).astype(F32)
    shift_rows = hot[:, None] * shift_part[None, :]
    squares = jnp.stack([jnp.sum(jnp.sum(x * x, axis=1) * valid) for x in (stream, branch, feed)])
    table = hot[:, None] * squares[None, :]
    steps_hot = (
        jnp.arange(seqs)[:, None] == dp_index * seq_dev + jnp.arange(seq_dev)[None, :]
    ).astype(F32)
    steps_all = jnp.sum(steps_hot * timestep.astype(F32)[None, :], axis=1) * (me == 0)
    up_canonical = ordered(grad_up_rel.reshape(quarters, tensor, piece_units), spot)
    up_canonical = up_canonical.transpose(1, 0, 2).reshape(tensor, half_units)
    full_up = jnp.zeros((tensor, 2, half_units), F32)
    full_qv = jnp.zeros((tensor, 2, local), F32)
    for index, (k, j) in enumerate(offsets):
        at = ((which + j) % seq_dev) * subs + (sub + k) % subs
        row = jnp.where(jnp.arange(2)[:, None] == core, up_canonical[index][None], 0.0)
        full_up = lax.dynamic_update_slice_in_dim(full_up, row[None], at, 0)
        if k == 0:
            value = column_sums[j].reshape(3, local)
            value = jnp.stack([value[0], value[2]])
            full_qv = lax.dynamic_update_slice_in_dim(full_qv, value[None], at, 0)

    vectors = [
        grad_first_gain,
        grad_first_shift,
        grad_output_bias,
        grad_down_bias,
        grad_second_gain,
        grad_second_shift,
        full_up.reshape(-1),
        shift_rows.reshape(-1),
        full_qv.reshape(-1),
        table.reshape(-1),
        steps_all,
    ]
    packed = jnp.concatenate(vectors)
    packed = jnp.pad(packed, (0, -packed.shape[0] % width)).reshape(-1, width)
    units_all, triple_all, out_all, packed, up_all = sum_all(
        plane, seq_dev, units_sum, triple_parts[1], triple_parts[0], out_total, packed, away
    )
    grad_up_weight = up_all.transpose(2, 0, 1, 3).reshape(width, units)
    grad_down_weight = units_all[1].reshape(units, width).astype(F32)
    grad_output_weight = out_all.reshape(local, width).astype(F32)
    grad_triple = triple_all.astype(F32).reshape(width, 3, local)
    input_gradient = (stream_own + sum(wide(x) for x in away)).astype(LOW)
    packed = packed.reshape(-1)
    got, at = [], 0
    for vector in vectors:
        got.append(packed[at : at + vector.shape[0]])
        at += vector.shape[0]
    full_up = pick(got[6].reshape(tensor, units), me)
    shift_grad = got[7].reshape(seqs, width)
    grad_query_value = pick(got[8].reshape(tensor, 2, local), me)
    table, steps_all = got[9].reshape(seqs, 3), got[10]
    grad_time_bias = jnp.sum(shift_grad, axis=0)
    embedded_all = sinusoid(steps_all, width).astype(LOW).astype(F32)
    grad_time_weight = lax.dot_general(
        embedded_all, shift_grad, TN, precision=lax.Precision.HIGHEST, preferred_element_type=F32
    )
    own_table = lax.dynamic_slice_in_dim(table, dp_index * seq_dev, seq_dev, 0)
    root_squares = jnp.sqrt(own_table / (lengths.astype(F32)[:, None] * width) + STAT_EPS)
    return (
        block_output,
        input_gradient,
        root_squares,
        grad_time_weight,
        grad_time_bias,
        grad_triple,
        grad_query_value,
        grad_output_weight,
        got[2],
        got[0],
        got[1],
        grad_up_weight,
        full_up,
        grad_down_weight,
        got[3],
        got[4],
        got[5],
    )


def solution(mesh):
    tensor = mesh.shape["tensor"]
    spots = mesh.shape["dp"] // 2
    plane = tuple(f"plane{i}" for i in range(spots.bit_length() - 1))
    fine = Mesh(
        mesh.devices.reshape((2,) * len(plane) + (2, tensor)), plane + ("core", "tensor")
    )
    dp = plane + ("core",)
    row = P(dp + ("tensor",), None)
    in_specs = (
        row,
        P(dp),
        P(dp),
        P(),
        P(),
        P(None, None, "tensor"),
        P(None, "tensor"),
        P("tensor", None),
        P(),
        P(),
        P(),
        P(None, "tensor"),
        P("tensor"),
        P("tensor", None),
        P(),
        P(),
        P(),
        row,
    )
    out_specs = (
        row,
        row,
        P(dp, None),
        P(),
        P(),
        P(None, None, "tensor"),
        P(None, "tensor"),
        P("tensor", None),
        P(),
        P(),
        P(),
        P(None, "tensor"),
        P("tensor"),
        P("tensor", None),
        P(),
        P(),
        P(),
    )
    return jax.shard_map(
        functools.partial(on_device, plane),
        mesh=fine,
        in_specs=in_specs,
        out_specs=out_specs,
        check_vma=False,
    )
```

```python
import functools
import math

import jax
import jax.numpy as jnp
from jax import lax
from jax.experimental import pallas as pl
from jax.experimental.pallas import tpu as pltpu
from jax.sharding import Mesh
from jax.sharding import PartitionSpec as P

HD = 64
LEN = 1024
NORM_EPS = 1e-05
STAT_EPS = 1e-06
MASKED = -1e30
LOW = jnp.bfloat16
F32 = jnp.float32
NT = (((1,), (1,)), ((), ()))
TN = (((0,), (0,)), ((), ()))


def sinusoid(steps, width):
    half = width // 2
    rates = jnp.exp(-math.log(10000.0) * jnp.arange(half).astype(F32) / half)
    angles = steps.astype(F32)[:, None] * rates[None, :]
    return jnp.concatenate([jnp.sin(angles), jnp.cos(angles)], axis=1)


def plain(left, right):
    return jnp.dot(left, right, preferred_element_type=F32)


def inner(left, right):
    return lax.dot_general(left, right, TN, preferred_element_type=F32)


def against(left, right):
    return lax.dot_general(left, right, NT, preferred_element_type=F32)


def norm_forward(total, gain, shift):
    middle = jnp.mean(total, axis=-1, keepdims=True)
    centred = total - middle
    spread = jnp.mean(centred * centred, axis=-1, keepdims=True)
    factor = lax.rsqrt(spread + NORM_EPS)
    normed = centred * factor
    return (normed * gain + shift, normed, factor)


def norm_backward(upstream, normed, factor, gain):
    pushed = upstream * gain
    first = jnp.mean(pushed, axis=-1, keepdims=True)
    second = jnp.mean(pushed * normed, axis=-1, keepdims=True)
    return (
        factor * (pushed - first - normed * second),
        jnp.sum(upstream * normed, axis=0),
        jnp.sum(upstream, axis=0),
    )


def split3(x):
    hi = x.astype(LOW)
    rest = x - hi.astype(F32)
    mid = rest.astype(LOW)
    return hi, mid, (rest - mid.astype(F32)).astype(LOW)


def extra_lanes(parts, one, count):
    lane = lax.broadcasted_iota(jnp.int32, (count, HD), 1)
    out = jnp.where(lane == len(parts), 1.0, 0.0) if one else jnp.zeros((count, HD), F32)
    for index, part in enumerate(parts):
        out = jnp.where(lane == index, jnp.broadcast_to(part.astype(F32), (count, HD)), out)
    return out.astype(LOW)


def head(x, h):
    return x[:, h * HD : (h + 1) * HD]


def attend_kernel(rows, mask_ref, q_ref, k_ref, v_ref, context_ref, log_ref):
    count = q_ref.shape[0]
    mask = mask_ref[...]
    keys = k_ref[...].astype(LOW)
    values = v_ref[...].astype(LOW)
    for start in range(0, count, rows):
        part = slice(start, start + rows)
        queries = q_ref[part].astype(LOW) * LOW(HD**-0.5)
        contexts, logs = [], []
        for h in range(2):
            scores = lax.dot_general(
                head(queries, h), head(keys, h), NT, preferred_element_type=F32
            )
            scores = scores + mask
            highest = jnp.max(scores, axis=1, keepdims=True)
            probs = jnp.exp(scores - highest)
            total = jnp.sum(probs, axis=1, keepdims=True)
            contexts.append(plain(probs.astype(LOW), head(values, h)) / total)
            logs.append(jnp.broadcast_to(highest + jnp.log(total), (rows, HD)))
        context_ref[part] = jnp.concatenate(contexts, axis=1)
        log_ref[part] = jnp.concatenate(logs, axis=1)


def attend(projected, mask_row, pair):
    count, width = projected.shape
    local = width // 3
    pairs = local // (2 * HD)
    block = lambda which: pl.BlockSpec((count, 2 * HD), lambda p: (0, which * pairs + pair))
    whole = pl.BlockSpec((count, 2 * HD), lambda p: (0, 0))
    return pl.pallas_call(
        functools.partial(attend_kernel, 512),
        grid=(1,),
        in_specs=[pl.BlockSpec((1, count), lambda p: (0, 0)), block(0), block(1), block(2)],
        out_specs=[whole] * 2,
        out_shape=[jax.ShapeDtypeStruct((count, 2 * HD), F32)] * 2,
        compiler_params=pltpu.CompilerParams(vmem_limit_bytes=40 << 20),
        cost_estimate=pl.CostEstimate(
            flops=16 * count * count * 2 * HD,
            bytes_accessed=40 * count * HD,
            transcendentals=2 * count * count,
        ),
    )(mask_row, projected, projected, projected)


def attend_back_kernel(
    rows, mask_ref, q_ref, k_ref, v_ref, context_ref, log_ref, grad_ref, *refs
):
    dq_ref, dk_ref, dv_ref = refs[-3:]
    count = k_ref.shape[0]
    lane = lax.broadcasted_iota(jnp.int32, (count, HD), 1)
    three = jnp.where(lane < 3, 1.0, 0.0)
    key_extra = jnp.where(lane == 3, jnp.broadcast_to(mask_ref[...], (count, HD)), three)
    key_extra = key_extra.astype(LOW)
    value_extra = three.astype(LOW)
    queries = q_ref[...].astype(LOW) * LOW(HD**-0.5)
    keys = k_ref[...].astype(LOW)
    values = v_ref[...].astype(LOW)
    logs = log_ref[...]
    grads = grad_ref[...]
    dots = grads * context_ref[...]
    grads = grads.astype(LOW)
    kx, vx, qx, gx, dq = [], [], [], [], [None, None]
    for h in range(2):
        extra = extra_lanes(split3(-logs[:, h * HD : h * HD + 1]), True, count)
        qx.append(jnp.concatenate([head(queries, h), extra], axis=1))
        row_dot = jnp.sum(head(dots, h), axis=1, keepdims=True)
        extra = extra_lanes(split3(-row_dot), False, count)
        gx.append(jnp.concatenate([head(grads, h), extra], axis=1))
        kx.append(jnp.concatenate([head(keys, h), key_extra], axis=1))
        vx.append(jnp.concatenate([head(values, h), value_extra], axis=1))
    for start in range(0, count, rows):
        part = slice(start, start + rows)
        dk, dv = [], []
        for h in range(2):
            probs = jnp.exp(lax.dot_general(kx[h][part], qx[h], NT, preferred_element_type=F32))
            pushed = lax.dot_general(vx[h][part], gx[h], NT, preferred_element_type=F32)
            scores_grad = (probs * pushed).astype(LOW)
            dv.append(plain(probs.astype(LOW), gx[h])[:, :HD])
            dk.append(plain(scores_grad, qx[h])[:, :HD])
            more = lax.dot_general(scores_grad, kx[h][part], TN, preferred_element_type=F32)
            dq[h] = more if start == 0 else dq[h] + more
        dk_ref[part] = jnp.concatenate(dk, axis=1)
        dv_ref[part] = jnp.concatenate(dv, axis=1)
    dq_ref[...] = jnp.concatenate([x[:, :HD] for x in dq], axis=1) * HD**-0.5


def attend_back(projected, mask_column, context, log_total, grad, pair, before):
    count, width = projected.shape
    local = width // 3
    pairs = local // (2 * HD)
    block = lambda which: pl.BlockSpec((count, 2 * HD), lambda p: (0, which * pairs + pair))
    whole = pl.BlockSpec((count, 2 * HD), lambda p: (0, 0))
    return pl.pallas_call(
        functools.partial(attend_back_kernel, 512),
        grid=(1,),
        in_specs=[pl.BlockSpec((count, 1), lambda p: (0, 0)), block(0), block(1), block(2)]
        + [whole, whole, block(0)]
        + [pl.BlockSpec(memory_space=pl.ANY)] * len(before),
        out_specs=[whole] * 3,
        out_shape=[jax.ShapeDtypeStruct((count, 2 * HD), F32)] * 3,
        compiler_params=pltpu.CompilerParams(vmem_limit_bytes=50 << 20),
        cost_estimate=pl.CostEstimate(
            flops=40 * count * count * 2 * HD,
            bytes_accessed=80 * count * HD,
            transcendentals=2 * count * count,
        ),
    )(mask_column, projected, projected, projected, context, log_total, grad, *before)


class Wires:
    def __init__(self, plane, subs, seq_dev, send_sems, recv_sems):
        self.plane, self.subs, self.seq_dev = plane, subs, seq_dev
        self.send_sems, self.recv_sems, self.sent = send_sems, recv_sems, []
        self.bits = [lax.axis_index(name) for name in plane]
        self.core = lax.axis_index("core")
        me = lax.axis_index("tensor")
        self.sub, self.which = lax.rem(me, subs), lax.div(me, subs)
        self.quarters = 2 ** len(plane)

    def spot(self, mask=0):
        total, count = 0, len(self.plane)
        for i, bit in enumerate(self.bits):
            flip = (mask >> (count - 1 - i)) & 1
            total = total + (1 - bit if flip else bit) * 2 ** (count - 1 - i)
        return total

    def at_plane(self, mask):
        count = len(self.plane)
        return {
            name: 1 - bit
            for i, (name, bit) in enumerate(zip(self.plane, self.bits))
            if (mask >> (count - 1 - i)) & 1
        }

    def at_core(self):
        return {"core": 1 - self.core}

    def at_member(self, k, j):
        return {
            "tensor": lax.rem(self.which + j + self.seq_dev, self.seq_dev) * self.subs
            + lax.rem(self.sub + k + self.subs, self.subs)
        }

    def greet(self, targets):
        barrier = pltpu.get_barrier_semaphore()
        for target in targets:
            pl.semaphore_signal(barrier, inc=1, device_id=target, device_id_type=pl.DeviceIdType.MESH)
        pl.semaphore_wait(barrier, len(targets))

    def send(self, src, dst, target):
        index = len(self.sent)
        copy = pltpu.make_async_remote_copy(
            src_ref=src,
            dst_ref=dst,
            send_sem=self.send_sems.at[index],
            recv_sem=self.recv_sems.at[index],
            device_id=target,
            device_id_type=pl.DeviceIdType.MESH,
        )
        copy.start()
        self.sent.append(copy)
        return copy

    def finish(self):
        for copy in self.sent:
            copy.wait_send()


def wide(x):
    return x.astype(F32)


def sum_kernel(
    plane, subs, seq_dev, ordering, units, later, now, output, vectors, *refs
):
    (
    units_out, triple_out, output_out, vectors_out, up_out,
    units_z, later_core, now_core, output_core, later_half, now_half, output_half,
    later_plane, now_plane, output_plane, triple_z, output_z, triple_mine, output_mine,
    vectors_core, vectors_plane, vectors_z, vectors_one, vectors_two, send_sems, recv_sems,
    ) = refs[ordering:]
    wires = Wires(plane, subs, seq_dev, send_sems, recv_sems)
    quarters, core = wires.quarters, wires.core
    spot = wires.spot()
    offsets = [(k, j) for k in range(subs) for j in range(seq_dev)]
    ahead = range(1, len(offsets))
    masks = range(1, quarters)
    wires.greet(
        [wires.at_core()]
        + [wires.at_plane(mask) for mask in masks]
        + [wires.at_member(k, j) for k, j in offsets[1:]]
    )
    core_got = []
    for source, target in ((later, later_core), (output, output_core), (now, now_core)):
        core_got.append(
            [
                wires.send(source.at[place, 1 - core], target.at[place], wires.at_core())
                for place in range(quarters)
            ]
        )
    vectors_got = wires.send(vectors, vectors_core, wires.at_core())

    def units_along(which):
        return [
            wires.send(units.at[which, z], units_z.at[which, z - 1], wires.at_member(*offsets[z]))
            for z in ahead
        ]

    units_got = [units_along(0)]
    plane_got = []
    for got, source, received, half, target in (
        (core_got[0], later, later_core, later_half, later_plane),
        (core_got[1], output, output_core, output_half, output_plane),
        (core_got[2], now, now_core, now_half, now_plane),
    ):
        for copy in got:
            copy.wait_recv()
        for place in range(quarters):
            half[place] = (wide(source[place, core]) + wide(received[place])).astype(LOW)
        plane_got.append(
            [
                wires.send(half.at[wires.spot(mask)], target.at[mask - 1], wires.at_plane(mask))
                for mask in masks
            ]
        )
    vectors_got.wait_recv()
    vectors_one[...] = vectors[...] + vectors_core[...]
    vectors_got = [
        wires.send(vectors_one, vectors_plane.at[mask - 1], wires.at_plane(mask)) for mask in masks
    ]
    last, up_crossed, passed = [], [], []

    def hand_round(slot, crossed):
        for mask in masks:
            got = wires.send(slot(spot), slot(spot), wires.at_plane(mask))
            passed.append((slot, crossed, mask, got))
        crossed.append((0, wires.send(slot(spot), slot(spot), wires.at_core())))

    def hand_over():
        while passed:
            slot, crossed, mask, copy = passed.pop(0)
            copy.wait_recv()
            ref = slot(wires.spot(mask))
            crossed.append((mask, wires.send(ref, ref, wires.at_core())))

    def units_whole(which):
        for copy in units_got[which]:
            copy.wait_recv()
        total = wide(units[which, 0])
        for z in ahead:
            total = total + wide(units_z[which, z - 1])
        units_out[which, core, spot] = total.astype(LOW)
        hand_round(lambda place: units_out.at[which, core, place], last if which else up_crossed)

    for copy in plane_got[0]:
        copy.wait_recv()
    total = wide(later_half[spot])
    for mask in masks:
        total = total + wide(later_plane[mask - 1])
    triple_mine[...] = total.astype(LOW)
    triple_got = [wires.send(triple_mine, triple_z, wires.at_member(0, 1))]
    for copy in plane_got[1]:
        copy.wait_recv()
    total = wide(output_half[spot])
    for mask in masks:
        total = total + wide(output_plane[mask - 1])
    output_mine[...] = total.astype(LOW)
    output_got = [
        wires.send(output_mine.at[z], output_z.at[z - 1], wires.at_member(*offsets[z])) for z in ahead
    ]
    units_got.append(units_along(1))
    for copy in vectors_got:
        copy.wait_recv()
    total = vectors_one[...]
    for mask in masks:
        total = total + vectors_plane[mask - 1]
    vectors_two[...] = total
    vectors_got = [
        wires.send(vectors_two, vectors_z.at[z - 1], wires.at_member(*offsets[z])) for z in ahead
    ]
    units_whole(0)
    for copy in plane_got[2]:
        copy.wait_recv()
    for copy in triple_got:
        copy.wait_recv()
    total = wide(now_half[spot]) + wide(triple_z[...])
    for mask in masks:
        total = total + wide(now_plane[mask - 1])
    triple_out[spot, core] = total.astype(LOW)
    hand_round(lambda place: triple_out.at[place, core], last)
    for copy in output_got:
        copy.wait_recv()
    total = wide(output_mine[0])
    for z in ahead:
        total = total + wide(output_z[z - 1])
    output_out[spot, core] = total.astype(LOW)
    hand_round(lambda place: output_out.at[place, core], last)
    hand_over()
    units_whole(1)

    def place_up(half, mask):
        place = wires.spot(mask)
        up_out[half, place] = wide(units_out[0, half, place]).T

    for mask, copy in up_crossed:
        place_up(core, mask)
        copy.wait_recv()
        place_up(1 - core, mask)
    for copy in vectors_got:
        copy.wait_recv()
    total = vectors_two[...]
    for z in ahead:
        total = total + vectors_z[z - 1]
    vectors_out[...] = total
    hand_over()
    for _, copy in last:
        copy.wait_recv()
    wires.finish()


def sum_all(plane, seq_dev, units, later, now, output, vectors, before):
    tensor, quarters = lax.axis_size("tensor"), 2 ** len(plane)
    subs, masks = tensor // seq_dev, quarters - 1
    piece, share, out_share = units.shape[2:], later.shape[2:], output.shape[3:]
    low = lambda *shape: pltpu.VMEM(shape, LOW)
    full = lambda *shape: pltpu.VMEM(shape + vectors.shape, F32)
    copies = (
        3 * quarters + 1 + 2 * (tensor - 1) + 3 * masks + masks + 1 + 2 * (tensor - 1)
        + 4 * (masks + 1 + masks)
    )
    return pl.pallas_call(
        functools.partial(sum_kernel, plane, subs, seq_dev, len(before)),
        in_specs=[pl.BlockSpec(memory_space=pltpu.VMEM)] * 5
        + [pl.BlockSpec(memory_space=pl.ANY)] * len(before),
        out_specs=[pl.BlockSpec(memory_space=pltpu.VMEM)] * 5,
        out_shape=[
            jax.ShapeDtypeStruct((2, 2, quarters) + piece, LOW),
            jax.ShapeDtypeStruct((quarters, 2) + share, LOW),
            jax.ShapeDtypeStruct((quarters, 2) + out_share, LOW),
            jax.ShapeDtypeStruct(vectors.shape, F32),
            jax.ShapeDtypeStruct((2, quarters, piece[1], piece[0]), F32),
        ],
        scratch_shapes=[
            low(2, tensor - 1, *piece),
            low(quarters, *share),
            low(quarters, *share),
            low(quarters, tensor, *out_share),
            low(quarters, *share),
            low(quarters, *share),
            low(quarters, tensor, *out_share),
            low(masks, *share),
            low(masks, *share),
            low(masks, tensor, *out_share),
            low(*share),
            low(tensor - 1, *out_share),
            low(*share),
            low(tensor, *out_share),
            full(),
            full(masks),
            full(tensor - 1),
            full(),
            full(),
            pltpu.SemaphoreType.DMA((copies,)),
            pltpu.SemaphoreType.DMA((copies,)),
        ],
        compiler_params=pltpu.CompilerParams(
            collective_id=1, has_side_effects=True, vmem_limit_bytes=48 << 20
        ),
        cost_estimate=pl.CostEstimate(flops=1 << 24, bytes_accessed=1 << 27, transcendentals=0),
    )(units, later, now, output, vectors, *before)


def gather_kernel(
    plane, subs, seq_dev, stream, triple, output, units, small,
    stream_out, triple_out, output_out, early_out, rest_out, small_out, send_sems, recv_sems,
):
    wires = Wires(plane, subs, seq_dev, send_sems, recv_sems)
    quarters, core = wires.quarters, wires.core
    offsets = [(k, j) for k in range(subs) for j in range(seq_dev)]
    ahead = range(1, len(offsets))
    masks = range(1, quarters)
    wires.greet(
        [wires.at_core()]
        + [wires.at_plane(mask) for mask in masks]
        + [wires.at_member(k, j) for k, j in offsets[1:]]
    )
    mine = 2 * wires.spot() + core
    share, out_share = triple_out.shape[1:], output_out.shape[2:]
    back = lambda z: wires.at_member(-offsets[z][0], -offsets[z][1])
    triple_got = wires.send(triple.at[mine], triple_out.at[mine], back(1))
    output_got = [wires.send(output.at[mine], output_out.at[z - 1, mine], back(z)) for z in ahead]
    small_got = [wires.send(small, small_out.at[z - 1], back(z)) for z in ahead]
    triple_got.wait_recv()
    stream_got = [wires.send(stream, stream_out.at[k - 1], wires.at_member(-k, 0)) for k in range(1, subs)]
    last, passed = [], []
    ref = triple_out.at[mine]
    for mask in masks:
        passed.append((mask, wires.send(ref, ref, wires.at_plane(mask))))
    last.append(wires.send(ref, ref, wires.at_core()))
    for copy in output_got:
        copy.wait_recv()
    early_got = wires.send(units, early_out.at[0], back(1))
    output_passed = []
    for mask in masks:
        for z in ahead:
            ref = output_out.at[z - 1, mine]
            output_passed.append((z, mask, wires.send(ref, ref, wires.at_plane(mask))))
    for z in ahead:
        ref = output_out.at[z - 1, mine]
        last.append(wires.send(ref, ref, wires.at_core()))
    for mask, copy in passed:
        copy.wait_recv()
        ref = triple_out.at[2 * wires.spot(mask) + core]
        last.append(wires.send(ref, ref, wires.at_core()))
    early_got.wait_recv()
    rest_got = [wires.send(units, rest_out.at[z - 2], back(z)) for z in ahead if z > 1]
    for mask in masks:
        last.append(wires.send(early_out.at[0], early_out.at[mask], wires.at_plane(mask)))
    for z, mask, copy in output_passed:
        copy.wait_recv()
        ref = output_out.at[z - 1, 2 * wires.spot(mask) + core]
        last.append(wires.send(ref, ref, wires.at_core()))
    for copy in small_got + stream_got + rest_got + last:
        copy.wait_recv()
    wires.finish()


def gather_all(plane, seq_dev, stream, triple, output, units, small):
    tensor, quarters = lax.axis_size("tensor"), 2 ** len(plane)
    subs, masks = tensor // seq_dev, quarters - 1
    others = tensor - 1
    copies = 2 + subs - 1 + 2 * others + 2 * quarters - 1 + 2 * others * quarters + others + masks
    return pl.pallas_call(
        functools.partial(gather_kernel, plane, subs, seq_dev),
        in_specs=[pl.BlockSpec(memory_space=pltpu.VMEM)] * 5,
        out_specs=[pl.BlockSpec(memory_space=pltpu.VMEM)] * 6,
        out_shape=[
            jax.ShapeDtypeStruct((subs - 1,) + stream.shape, LOW),
            jax.ShapeDtypeStruct(triple.shape, LOW),
            jax.ShapeDtypeStruct((others,) + output.shape, LOW),
            jax.ShapeDtypeStruct((quarters,) + units.shape, LOW),
            jax.ShapeDtypeStruct((others - 1,) + units.shape, LOW),
            jax.ShapeDtypeStruct((others,) + small.shape, F32),
        ],
        scratch_shapes=[
            pltpu.SemaphoreType.DMA((copies,)),
            pltpu.SemaphoreType.DMA((copies,)),
        ],
        compiler_params=pltpu.CompilerParams(
            collective_id=2, has_side_effects=True, vmem_limit_bytes=32 << 20
        ),
        cost_estimate=pl.CostEstimate(flops=1 << 20, bytes_accessed=1 << 27, transcendentals=0),
    )(stream, triple, output, units, small)


def gaussian_pair(value):
    cumulative = 0.5 * (1.0 + jax.scipy.special.erf(value * (1.0 / math.sqrt(2.0))))
    slope = cumulative + value * jnp.exp(-0.5 * value * value) * (1.0 / math.sqrt(2.0 * math.pi))
    return (value * cumulative).astype(LOW), slope.astype(LOW)


def on_device(
    plane,
    stream_in,
    timestep,
    lengths,
    time_weight,
    time_bias,
    triple_weight,
    query_value_bias,
    output_weight,
    output_bias,
    first_gain,
    first_shift,
    up_weight,
    up_bias,
    down_weight,
    down_bias,
    second_gain,
    second_shift,
    cotangent,
):
    rows, width = stream_in.shape
    seq_dev = timestep.shape[0]
    tensor = lax.axis_size("tensor")
    subs = tensor // seq_dev
    local = triple_weight.shape[2]
    units = up_weight.shape[1]
    half_units = units // 2
    quarters = 2 ** len(plane)
    piece_units = half_units // quarters
    me = lax.axis_index("tensor")
    core = lax.axis_index("core")
    spot = lax.axis_index(plane)
    sub = me % subs
    which = me // subs
    offsets = [(k, j) for k in range(subs) for j in range(seq_dev)]
    others = offsets[1:]

    def member(i, k, j):
        return ((i // subs + j) % seq_dev) * subs + (i % subs + k) % subs

    def fetch(x, k, j):
        return lax.ppermute(x, "tensor", [(member(i, k, j), i) for i in range(tensor)])

    def send(x, k, j):
        return lax.ppermute(x, "tensor", [(i, member(i, k, j)) for i in range(tensor)])

    def swap(x, axis):
        return lax.ppermute(x, axis, [(0, 1), (1, 0)])

    def across(x, mask):
        return lax.ppermute(x, plane, [(i, i ^ mask) for i in range(quarters)])

    def pick(x, index, axis=0):
        return lax.dynamic_index_in_dim(x, index, axis, keepdims=False)

    def tie(x, *before):
        return lax.optimization_barrier((x,) + before)[0]

    def ordered(parts, index):
        parts = jnp.stack(parts) if isinstance(parts, (list, tuple)) else parts
        return jnp.stack([pick(parts, index ^ m) for m in range(parts.shape[0])])

    triple_three = triple_weight.transpose(1, 0, 2)
    triple_own = jnp.concatenate([triple_three[i] for i in range(3)], axis=1)
    part = width // (2 * quarters)
    out_part = local // (2 * quarters)
    up_half = lax.dynamic_slice_in_dim(up_weight, core * half_units, half_units, 1).T
    down_half = lax.dynamic_slice_in_dim(down_weight, core * half_units, half_units, 0)
    units_mine = [
        ordered(x.reshape(quarters, piece_units, width), spot) for x in (up_half, down_half)
    ]
    small = jnp.concatenate([up_bias, query_value_bias.reshape(-1)])
    pad = -small.shape[0] % 1024
    raw, triple_got, out_got, early, rest, small_got = gather_all(
        plane,
        seq_dev,
        stream_in,
        triple_own.reshape(2 * quarters, part, 3 * local),
        output_weight.reshape(2 * quarters, out_part, width),
        jnp.stack([units_mine[0][0], units_mine[1][0]]),
        jnp.pad(small, (0, pad)).reshape(-1, 128),
    )
    raw = [stream_in] + [raw[k] for k in range(subs - 1)]
    triples = [triple_own, triple_got.reshape(width, 3 * local)]
    out_got = out_got.reshape(tensor - 1, local, width)
    out_full = jnp.concatenate([output_weight[None], out_got]).reshape(tensor * local, width)
    small_of = {(0, 0): small}
    for z, (k, j) in enumerate(others):
        small_of[(k, j)] = small_got[z].reshape(-1)[: small.shape[0]]
    rest_of = [rest] + [across(rest, m) for m in range(1, quarters)]

    def all_rows(which):
        full = []
        for m in range(quarters):
            full += [units_mine[which][m][None], early[m, which][None], rest_of[m][:, which]]
        return jnp.concatenate(full, axis=0).reshape(-1, width)

    up_rows, down_rows = all_rows(0), all_rows(1)

    embedded_own = sinusoid(timestep, width).astype(LOW)
    shift_own = plain(embedded_own, time_weight) + time_bias
    shift_row = pick(shift_own, which)
    limit = pick(lengths, which)
    stream = stream_in.astype(F32) + shift_row
    stream_low = (jnp.concatenate(raw, axis=0).astype(F32) + shift_row).astype(LOW)
    place = (jnp.arange(LEN, dtype=jnp.int32) + sub * rows) % LEN
    mask = jnp.where(place < limit, 0.0, MASKED).astype(F32)
    mask_row, mask_column = mask[None, :], mask[:, None]
    valid = (place[:rows] < limit).astype(F32)

    pairs = local // (2 * HD)
    qv = [small_of[(0, j)][units:].reshape(2, local) for j in range(seq_dev)]
    projected, context, log_total = [], [], []
    for j in range(seq_dev):
        bias = jnp.concatenate([qv[j][0], jnp.zeros((local,), F32), qv[j][1]])
        projected.append(plain(stream_low, triples[j]) + bias)
        here = [attend(projected[j], mask_row, pair) for pair in range(pairs)]
        context.append([x[0] for x in here])
        log_total.append([x[1] for x in here])
    block = lambda x, k: x[k * rows : (k + 1) * rows]
    columns = []
    for k in range(subs):
        back = (subs - k) % subs
        for j in range(seq_dev):
            mine = jnp.concatenate([block(x, back) for x in context[j]], axis=1).astype(LOW)
            columns.append(mine if k == 0 else send(mine, back, 0))
    context_own = jnp.concatenate(columns, axis=1)

    branch = plain(context_own, out_full) + output_bias
    middle, normed_first, factor_first = norm_forward(stream + branch, first_gain, first_shift)
    middle_low = middle.astype(LOW)

    bias_all = jnp.stack([small_of[o][:units] for o in offsets])
    bias_half = lax.dynamic_slice_in_dim(bias_all, core * half_units, half_units, 1)
    bias_rel = ordered(
        bias_half.reshape(tensor, quarters, piece_units).transpose(1, 0, 2), spot
    ).reshape(-1)
    both = jnp.concatenate([middle_low, swap(middle_low, "core")], axis=0)
    active, slope = lax.optimization_barrier(
        gaussian_pair(against(both, up_rows) + bias_rel)
    )
    feed_other = plain(active[rows:], down_rows).astype(LOW)
    feed = plain(active[:rows], down_rows) + swap(feed_other, "core").astype(F32) + down_bias
    result, normed_second, factor_second = norm_forward(middle + feed, second_gain, second_shift)
    block_output = result.astype(LOW)

    to_second, grad_second_gain, grad_second_shift = norm_backward(
        cotangent.astype(F32), normed_second, factor_second, second_gain
    )
    feed_grad = to_second.astype(LOW)
    grad_down_bias = jnp.sum(feed_grad.astype(F32), axis=0)
    feed_grad_both = jnp.concatenate([feed_grad, swap(feed_grad, "core")], axis=0)

    def by_mask(total):
        shaped = total.reshape(quarters, tensor, piece_units, width)
        return {m: shaped[m] for m in range(quarters)}

    down_total = by_mask(inner(active, feed_grad_both).astype(LOW))
    before_grad = (against(feed_grad_both, down_rows) * slope.astype(F32)).astype(LOW)
    up_total = by_mask(inner(before_grad, both).astype(LOW))
    units_sum = wide(jnp.stack([up_total[0], down_total[0]]))
    for m in range(1, quarters):
        units_sum = units_sum + wide(across(jnp.stack([up_total[m], down_total[m]]), m))
    units_sum = units_sum.astype(LOW)
    grad_up_rel = jnp.sum(before_grad.astype(F32), axis=0)
    middle_other = plain(before_grad[rows:], up_rows).astype(LOW)
    middle_grad = (
        to_second + plain(before_grad[:rows], up_rows) + swap(middle_other, "core").astype(F32)
    )

    to_first, grad_first_gain, grad_first_shift = norm_backward(
        middle_grad, normed_first, factor_first, first_gain
    )
    branch_grad = to_first.astype(LOW)
    grad_output_bias = jnp.sum(branch_grad.astype(F32), axis=0)
    context_grad = against(branch_grad, out_full).astype(LOW)
    shaped = context_grad.reshape(rows, subs, seq_dev, local)
    incoming = [None] * seq_dev
    for j in reversed(range(seq_dev)):
        parts = []
        for k in range(subs):
            back = (subs - k) % subs
            mine = shaped[:, back, j]
            parts.append(mine if k == 0 else send(mine, back, 0))
        incoming[j] = jnp.concatenate(parts, axis=0).astype(F32)

    def backward(j, pair, before):
        return attend_back(
            projected[j], mask_column, context[j][pair], log_total[j][pair], incoming[j], pair, before
        )

    def together(parts):
        return jnp.concatenate([x[i] for i in range(3) for x in parts], axis=1).astype(LOW)

    grads = [None] * seq_dev
    for j in reversed(range(seq_dev)):
        grads[j] = together([backward(j, pair, []) for pair in range(pairs)])
    triple_parts = [
        inner(stream_low, grads[j]).astype(LOW).reshape(quarters, 2, part, 3 * local)
        for j in range(seq_dev)
    ]
    out_total = inner(context_own, branch_grad).astype(LOW)
    out_total = out_total.reshape(tensor, quarters, 2, out_part, width).transpose(1, 2, 0, 3, 4)
    away = [
        send(
            sum(against(block(grads[j], k), triples[j]) for j in range(seq_dev)).astype(LOW), k, 0
        )
        for k in range(1, subs)
    ]
    stream_own = to_first + sum(
        against(block(grads[j], 0), triples[j]) for j in range(seq_dev)
    )

    dp_index = spot * 2 + core
    seqs = quarters * 2 * seq_dev
    column_sums = [jnp.sum(grads[j].astype(F32), axis=0) for j in range(seq_dev)]
    shift_part = jnp.sum(to_first, axis=0) + sum(
        against(column_sums[j][None].astype(F32), triples[j].astype(F32))[0]
        for j in range(seq_dev)
    )
    hot = (jnp.arange(seqs) == dp_index * seq_dev + which).astype(F32)
    shift_rows = hot[:, None] * shift_part[None, :]
    squares = jnp.stack([jnp.sum(jnp.sum(x * x, axis=1) * valid) for x in (stream, branch, feed)])
    table = hot[:, None] * squares[None, :]
    steps_hot = (
        jnp.arange(seqs)[:, None] == dp_index * seq_dev + jnp.arange(seq_dev)[None, :]
    ).astype(F32)
    steps_all = jnp.sum(steps_hot * timestep.astype(F32)[None, :], axis=1) * (me == 0)
    up_canonical = ordered(grad_up_rel.reshape(quarters, tensor, piece_units), spot)
    up_canonical = up_canonical.transpose(1, 0, 2).reshape(tensor, half_units)
    full_up = jnp.zeros((tensor, 2, half_units), F32)
    full_qv = jnp.zeros((tensor, 2, local), F32)
    for index, (k, j) in enumerate(offsets):
        at = ((which + j) % seq_dev) * subs + (sub + k) % subs
        row = jnp.where(jnp.arange(2)[:, None] == core, up_canonical[index][None], 0.0)
        full_up = lax.dynamic_update_slice_in_dim(full_up, row[None], at, 0)
        if k == 0:
            value = column_sums[j].reshape(3, local)
            value = jnp.stack([value[0], value[2]])
            full_qv = lax.dynamic_update_slice_in_dim(full_qv, value[None], at, 0)

    vectors = [
        grad_first_gain,
        grad_first_shift,
        grad_output_bias,
        grad_down_bias,
        grad_second_gain,
        grad_second_shift,
        full_up.reshape(-1),
        shift_rows.reshape(-1),
        full_qv.reshape(-1),
        table.reshape(-1),
        steps_all,
    ]
    packed = jnp.concatenate(vectors)
    packed = jnp.pad(packed, (0, -packed.shape[0] % width)).reshape(-1, width)
    units_all, triple_all, out_all, packed, up_all = sum_all(
        plane, seq_dev, units_sum, triple_parts[1], triple_parts[0], out_total, packed, away + [stream_own]
    )
    grad_up_weight = jnp.concatenate(
        [up_all[half, place] for half in range(2) for place in range(quarters)], axis=1
    )
    grad_down_weight = units_all[1].reshape(units, width).astype(F32)
    grad_output_weight = out_all.reshape(local, width).astype(F32)
    triple_all = triple_all.reshape(width, 3 * local)
    grad_triple = jnp.stack([triple_all[:, i * local : (i + 1) * local] for i in range(3)])
    grad_triple = grad_triple.astype(F32).transpose(1, 0, 2)
    input_gradient = (stream_own + sum(wide(x) for x in away)).astype(LOW)
    packed = packed.reshape(-1)
    got, at = [], 0
    for vector in vectors:
        got.append(packed[at : at + vector.shape[0]])
        at += vector.shape[0]
    full_up = pick(got[6].reshape(tensor, units), me)
    shift_grad = got[7].reshape(seqs, width)
    grad_query_value = pick(got[8].reshape(tensor, 2, local), me)
    table, steps_all = got[9].reshape(seqs, 3), got[10]
    grad_time_bias = jnp.sum(shift_grad, axis=0)
    embedded_all = sinusoid(steps_all, width).astype(LOW).astype(F32)
    grad_time_weight = lax.dot_general(
        embedded_all, shift_grad, TN, precision=lax.Precision.HIGHEST, preferred_element_type=F32
    )
    own_table = lax.dynamic_slice_in_dim(table, dp_index * seq_dev, seq_dev, 0)
    root_squares = jnp.sqrt(own_table / (lengths.astype(F32)[:, None] * width) + STAT_EPS)
    return (
        block_output,
        input_gradient,
        root_squares,
        grad_time_weight,
        grad_time_bias,
        grad_triple,
        grad_query_value,
        grad_output_weight,
        got[2],
        got[0],
        got[1],
        grad_up_weight,
        full_up,
        grad_down_weight,
        got[3],
        got[4],
        got[5],
    )


def solution(mesh):
    tensor = mesh.shape["tensor"]
    spots = mesh.shape["dp"] // 2
    plane = tuple(f"plane{i}" for i in range(spots.bit_length() - 1))
    fine = Mesh(
        mesh.devices.reshape((2,) * len(plane) + (2, tensor)), plane + ("core", "tensor")
    )
    dp = plane + ("core",)
    row = P(dp + ("tensor",), None)
    in_specs = (
        row,
        P(dp),
        P(dp),
        P(),
        P(),
        P(None, None, "tensor"),
        P(None, "tensor"),
        P("tensor", None),
        P(),
        P(),
        P(),
        P(None, "tensor"),
        P("tensor"),
        P("tensor", None),
        P(),
        P(),
        P(),
        row,
    )
    out_specs = (
        row,
        row,
        P(dp, None),
        P(),
        P(),
        P(None, None, "tensor"),
        P(None, "tensor"),
        P("tensor", None),
        P(),
        P(),
        P(),
        P(None, "tensor"),
        P("tensor"),
        P("tensor", None),
        P(),
        P(),
        P(),
    )
    return jax.shard_map(
        functools.partial(on_device, plane),
        mesh=fine,
        in_specs=in_specs,
        out_specs=out_specs,
        check_vma=False,
    )
```

```python
import functools
import math

import jax
import jax.numpy as jnp
from jax import lax
from jax.experimental import pallas as pl
from jax.experimental.pallas import tpu as pltpu
from jax.sharding import Mesh
from jax.sharding import PartitionSpec as P

HD = 64
LEN = 1024
NORM_EPS = 1e-05
STAT_EPS = 1e-06
MASKED = -1e30
LOW = jnp.bfloat16
F32 = jnp.float32
NT = (((1,), (1,)), ((), ()))
TN = (((0,), (0,)), ((), ()))


def sinusoid(steps, width):
    half = width // 2
    rates = jnp.exp(-math.log(10000.0) * jnp.arange(half).astype(F32) / half)
    angles = steps.astype(F32)[:, None] * rates[None, :]
    return jnp.concatenate([jnp.sin(angles), jnp.cos(angles)], axis=1)


def plain(left, right):
    return jnp.dot(left, right, preferred_element_type=F32)


def inner(left, right):
    return lax.dot_general(left, right, TN, preferred_element_type=F32)


def against(left, right):
    return lax.dot_general(left, right, NT, preferred_element_type=F32)


def norm_forward(total, gain, shift):
    middle = jnp.mean(total, axis=-1, keepdims=True)
    centred = total - middle
    spread = jnp.mean(centred * centred, axis=-1, keepdims=True)
    factor = lax.rsqrt(spread + NORM_EPS)
    normed = centred * factor
    return (normed * gain + shift, normed, factor)


def norm_backward(upstream, normed, factor, gain):
    pushed = upstream * gain
    first = jnp.mean(pushed, axis=-1, keepdims=True)
    second = jnp.mean(pushed * normed, axis=-1, keepdims=True)
    return (
        factor * (pushed - first - normed * second),
        jnp.sum(upstream * normed, axis=0),
        jnp.sum(upstream, axis=0),
    )


def split3(x):
    hi = x.astype(LOW)
    rest = x - hi.astype(F32)
    mid = rest.astype(LOW)
    return hi, mid, (rest - mid.astype(F32)).astype(LOW)


def extra_lanes(parts, one, count):
    lane = lax.broadcasted_iota(jnp.int32, (count, HD), 1)
    out = jnp.where(lane == len(parts), 1.0, 0.0) if one else jnp.zeros((count, HD), F32)
    for index, part in enumerate(parts):
        out = jnp.where(lane == index, jnp.broadcast_to(part.astype(F32), (count, HD)), out)
    return out.astype(LOW)


def head(x, h):
    return x[:, h * HD : (h + 1) * HD]


def attend_kernel(rows, mask_ref, q_ref, k_ref, v_ref, context_ref, log_ref):
    count = q_ref.shape[0]
    mask = mask_ref[...]
    keys = k_ref[...].astype(LOW)
    values = v_ref[...].astype(LOW)
    for start in range(0, count, rows):
        part = slice(start, start + rows)
        queries = q_ref[part].astype(LOW) * LOW(HD**-0.5)
        contexts, logs = [], []
        for h in range(2):
            scores = lax.dot_general(
                head(queries, h), head(keys, h), NT, preferred_element_type=F32
            )
            scores = scores + mask
            highest = jnp.max(scores, axis=1, keepdims=True)
            probs = jnp.exp(scores - highest)
            total = jnp.sum(probs, axis=1, keepdims=True)
            contexts.append(plain(probs.astype(LOW), head(values, h)) / total)
            logs.append(jnp.broadcast_to(highest + jnp.log(total), (rows, HD)))
        context_ref[part] = jnp.concatenate(contexts, axis=1)
        log_ref[part] = jnp.concatenate(logs, axis=1)


def attend(projected, mask_row, pair):
    count, width = projected.shape
    local = width // 3
    pairs = local // (2 * HD)
    block = lambda which: pl.BlockSpec((count, 2 * HD), lambda p: (0, which * pairs + pair))
    whole = pl.BlockSpec((count, 2 * HD), lambda p: (0, 0))
    return pl.pallas_call(
        functools.partial(attend_kernel, 512),
        grid=(1,),
        in_specs=[pl.BlockSpec((1, count), lambda p: (0, 0)), block(0), block(1), block(2)],
        out_specs=[whole] * 2,
        out_shape=[jax.ShapeDtypeStruct((count, 2 * HD), F32)] * 2,
        compiler_params=pltpu.CompilerParams(vmem_limit_bytes=40 << 20),
        cost_estimate=pl.CostEstimate(
            flops=16 * count * count * 2 * HD,
            bytes_accessed=40 * count * HD,
            transcendentals=2 * count * count,
        ),
    )(mask_row, projected, projected, projected)


def attend_back_kernel(
    rows, mask_ref, q_ref, k_ref, v_ref, context_ref, log_ref, grad_ref, *refs
):
    dq_ref, dk_ref, dv_ref = refs[-3:]
    count = k_ref.shape[0]
    lane = lax.broadcasted_iota(jnp.int32, (count, HD), 1)
    three = jnp.where(lane < 3, 1.0, 0.0)
    key_extra = jnp.where(lane == 3, jnp.broadcast_to(mask_ref[...], (count, HD)), three)
    key_extra = key_extra.astype(LOW)
    value_extra = three.astype(LOW)
    queries = q_ref[...].astype(LOW) * LOW(HD**-0.5)
    keys = k_ref[...].astype(LOW)
    values = v_ref[...].astype(LOW)
    logs = log_ref[...]
    grads = grad_ref[...]
    dots = grads * context_ref[...]
    grads = grads.astype(LOW)
    kx, vx, qx, gx, dq = [], [], [], [], [None, None]
    for h in range(2):
        extra = extra_lanes(split3(-logs[:, h * HD : h * HD + 1]), True, count)
        qx.append(jnp.concatenate([head(queries, h), extra], axis=1))
        row_dot = jnp.sum(head(dots, h), axis=1, keepdims=True)
        extra = extra_lanes(split3(-row_dot), False, count)
        gx.append(jnp.concatenate([head(grads, h), extra], axis=1))
        kx.append(jnp.concatenate([head(keys, h), key_extra], axis=1))
        vx.append(jnp.concatenate([head(values, h), value_extra], axis=1))
    for start in range(0, count, rows):
        part = slice(start, start + rows)
        dk, dv = [], []
        for h in range(2):
            probs = jnp.exp(lax.dot_general(kx[h][part], qx[h], NT, preferred_element_type=F32))
            pushed = lax.dot_general(vx[h][part], gx[h], NT, preferred_element_type=F32)
            scores_grad = (probs * pushed).astype(LOW)
            dv.append(plain(probs.astype(LOW), gx[h])[:, :HD])
            dk.append(plain(scores_grad, qx[h])[:, :HD])
            more = lax.dot_general(scores_grad, kx[h][part], TN, preferred_element_type=F32)
            dq[h] = more if start == 0 else dq[h] + more
        dk_ref[part] = jnp.concatenate(dk, axis=1)
        dv_ref[part] = jnp.concatenate(dv, axis=1)
    dq_ref[...] = jnp.concatenate([x[:, :HD] for x in dq], axis=1) * HD**-0.5


def attend_back(projected, mask_column, context, log_total, grad, pair, before):
    count, width = projected.shape
    local = width // 3
    pairs = local // (2 * HD)
    block = lambda which: pl.BlockSpec((count, 2 * HD), lambda p: (0, which * pairs + pair))
    whole = pl.BlockSpec((count, 2 * HD), lambda p: (0, 0))
    return pl.pallas_call(
        functools.partial(attend_back_kernel, 512),
        grid=(1,),
        in_specs=[pl.BlockSpec((count, 1), lambda p: (0, 0)), block(0), block(1), block(2)]
        + [whole, whole, block(0)]
        + [pl.BlockSpec(memory_space=pl.ANY)] * len(before),
        out_specs=[whole] * 3,
        out_shape=[jax.ShapeDtypeStruct((count, 2 * HD), F32)] * 3,
        compiler_params=pltpu.CompilerParams(vmem_limit_bytes=50 << 20),
        cost_estimate=pl.CostEstimate(
            flops=40 * count * count * 2 * HD,
            bytes_accessed=80 * count * HD,
            transcendentals=2 * count * count,
        ),
    )(mask_column, projected, projected, projected, context, log_total, grad, *before)


class Wires:
    def __init__(self, plane, subs, seq_dev, send_sems, recv_sems):
        self.plane, self.subs, self.seq_dev = plane, subs, seq_dev
        self.send_sems, self.recv_sems, self.sent = send_sems, recv_sems, []
        self.bits = [lax.axis_index(name) for name in plane]
        self.core = lax.axis_index("core")
        me = lax.axis_index("tensor")
        self.sub, self.which = lax.rem(me, subs), lax.div(me, subs)
        self.quarters = 2 ** len(plane)

    def spot(self, mask=0):
        total, count = 0, len(self.plane)
        for i, bit in enumerate(self.bits):
            flip = (mask >> (count - 1 - i)) & 1
            total = total + (1 - bit if flip else bit) * 2 ** (count - 1 - i)
        return total

    def at_plane(self, mask):
        count = len(self.plane)
        return {
            name: 1 - bit
            for i, (name, bit) in enumerate(zip(self.plane, self.bits))
            if (mask >> (count - 1 - i)) & 1
        }

    def at_core(self):
        return {"core": 1 - self.core}

    def at_member(self, k, j):
        return {
            "tensor": lax.rem(self.which + j + self.seq_dev, self.seq_dev) * self.subs
            + lax.rem(self.sub + k + self.subs, self.subs)
        }

    def greet(self, targets):
        barrier = pltpu.get_barrier_semaphore()
        for target in targets:
            pl.semaphore_signal(barrier, inc=1, device_id=target, device_id_type=pl.DeviceIdType.MESH)
        pl.semaphore_wait(barrier, len(targets))

    def send(self, src, dst, target):
        index = len(self.sent)
        copy = pltpu.make_async_remote_copy(
            src_ref=src,
            dst_ref=dst,
            send_sem=self.send_sems.at[index],
            recv_sem=self.recv_sems.at[index],
            device_id=target,
            device_id_type=pl.DeviceIdType.MESH,
        )
        copy.start()
        self.sent.append(copy)
        return copy

    def finish(self):
        for copy in self.sent:
            copy.wait_send()


def wide(x):
    return x.astype(F32)


def sum_kernel(
    plane, subs, seq_dev, ordering, units, later, now, output, vectors, *refs
):
    (
    units_out, triple_out, output_out, vectors_out, up_out,
    units_z, later_core, now_core, output_core, later_half, now_half, output_half,
    later_plane, now_plane, output_plane, triple_z, output_z, triple_mine, output_mine, units_away,
    vectors_core, vectors_plane, vectors_z, vectors_one, vectors_two, send_sems, recv_sems,
    ) = refs[ordering:]
    wires = Wires(plane, subs, seq_dev, send_sems, recv_sems)
    quarters, core = wires.quarters, wires.core
    spot = wires.spot()
    offsets = [(k, j) for k in range(subs) for j in range(seq_dev)]
    ahead = range(1, len(offsets))
    masks = range(1, quarters)
    wires.greet(
        [wires.at_core()]
        + [wires.at_plane(mask) for mask in masks]
        + [wires.at_member(k, j) for k, j in offsets[1:]]
    )
    core_got = []
    for source, target in ((later, later_core), (output, output_core), (now, now_core)):
        core_got.append(
            [
                wires.send(source.at[place, 1 - core], target.at[place], wires.at_core())
                for place in range(quarters)
            ]
        )
    vectors_got = wires.send(vectors, vectors_core, wires.at_core())

    inner_count = (subs - 1) * seq_dev

    def units_inside(which):
        return [
            wires.send(
                units.at[which, pl.ds(k * seq_dev, seq_dev)],
                units_z.at[which, pl.ds((k - 1) * seq_dev, seq_dev)],
                wires.at_member(k, 0),
            )
            for k in range(1, subs)
        ]

    def units_part(which, j):
        total = wide(units[which, j])
        for k in range(1, subs):
            total = total + wide(units_z[which, (k - 1) * seq_dev + j])
        return total

    def units_across(which, got):
        for copy in got:
            copy.wait_recv()
        copies = []
        for j in range(1, seq_dev):
            units_away[which, j - 1] = units_part(which, j).astype(LOW)
            copies.append(
                wires.send(
                    units_away.at[which, j - 1],
                    units_z.at[which, inner_count + j - 1],
                    wires.at_member(0, j),
                )
            )
        return copies

    units_first = units_inside(0)
    plane_got = []
    for got, source, received, half, target in (
        (core_got[0], later, later_core, later_half, later_plane),
        (core_got[1], output, output_core, output_half, output_plane),
        (core_got[2], now, now_core, now_half, now_plane),
    ):
        for copy in got:
            copy.wait_recv()
        for place in range(quarters):
            half[place] = (wide(source[place, core]) + wide(received[place])).astype(LOW)
        plane_got.append(
            [
                wires.send(half.at[wires.spot(mask)], target.at[mask - 1], wires.at_plane(mask))
                for mask in masks
            ]
        )
    vectors_got.wait_recv()
    vectors_one[...] = vectors[...] + vectors_core[...]
    vectors_got = [
        wires.send(vectors_one, vectors_plane.at[mask - 1], wires.at_plane(mask)) for mask in masks
    ]
    last, up_crossed, passed = [], [], []

    def hand_round(slot, crossed):
        for mask in masks:
            got = wires.send(slot(spot), slot(spot), wires.at_plane(mask))
            passed.append((slot, crossed, mask, got))
        crossed.append((0, wires.send(slot(spot), slot(spot), wires.at_core())))

    def hand_over():
        while passed:
            slot, crossed, mask, copy = passed.pop(0)
            copy.wait_recv()
            ref = slot(wires.spot(mask))
            crossed.append((mask, wires.send(ref, ref, wires.at_core())))

    def units_whole(which):
        for copy in units_got[which]:
            copy.wait_recv()
        total = units_part(which, 0)
        for j in range(1, seq_dev):
            total = total + wide(units_z[which, inner_count + j - 1])
        units_out[which, core, spot] = total.astype(LOW)
        hand_round(lambda place: units_out.at[which, core, place], last if which else up_crossed)

    units_got = [units_across(0, units_first)]
    units_second = units_inside(1)
    for copy in plane_got[0]:
        copy.wait_recv()
    total = wide(later_half[spot])
    for mask in masks:
        total = total + wide(later_plane[mask - 1])
    triple_mine[...] = total.astype(LOW)
    triple_got = [wires.send(triple_mine, triple_z, wires.at_member(0, 1))]
    for copy in plane_got[1]:
        copy.wait_recv()
    total = wide(output_half[spot])
    for mask in masks:
        total = total + wide(output_plane[mask - 1])
    output_mine[...] = total.astype(LOW)
    output_got = [
        wires.send(output_mine.at[z], output_z.at[z - 1], wires.at_member(*offsets[z])) for z in ahead
    ]
    units_got.append(units_across(1, units_second))
    for copy in vectors_got:
        copy.wait_recv()
    total = vectors_one[...]
    for mask in masks:
        total = total + vectors_plane[mask - 1]
    vectors_two[...] = total
    vectors_got = [
        wires.send(vectors_two, vectors_z.at[z - 1], wires.at_member(*offsets[z])) for z in ahead
    ]
    units_whole(0)
    for copy in plane_got[2]:
        copy.wait_recv()
    for copy in triple_got:
        copy.wait_recv()
    total = wide(now_half[spot]) + wide(triple_z[...])
    for mask in masks:
        total = total + wide(now_plane[mask - 1])
    triple_out[spot, core] = total.astype(LOW)
    hand_round(lambda place: triple_out.at[place, core], last)
    for copy in output_got:
        copy.wait_recv()
    total = wide(output_mine[0])
    for z in ahead:
        total = total + wide(output_z[z - 1])
    output_out[spot, core] = total.astype(LOW)
    hand_round(lambda place: output_out.at[place, core], last)
    hand_over()
    units_whole(1)

    def place_up(half, mask):
        place = wires.spot(mask)
        block = wide(units_out[0, half, place]).T
        wide_block = block.shape[1]
        if len(up_out.shape) == 2:
            first = pl.multiple_of((half * quarters + place) * wide_block, wide_block)
            up_out[:, pl.ds(first, wide_block)] = block
        else:
            up_out[half, place] = block

    for mask, copy in up_crossed:
        place_up(core, mask)
        copy.wait_recv()
        place_up(1 - core, mask)
    for copy in vectors_got:
        copy.wait_recv()
    total = vectors_two[...]
    for z in ahead:
        total = total + vectors_z[z - 1]
    vectors_out[...] = total
    hand_over()
    for _, copy in last:
        copy.wait_recv()
    wires.finish()


def sum_all(plane, seq_dev, units, later, now, output, vectors, before):
    tensor, quarters = lax.axis_size("tensor"), 2 ** len(plane)
    subs, masks = tensor // seq_dev, quarters - 1
    piece, share, out_share = units.shape[2:], later.shape[2:], output.shape[3:]
    up_shape = (piece[1], 2 * quarters * piece[0])
    if piece[0] % 128:
        up_shape = (2, quarters, piece[1], piece[0])
    low = lambda *shape: pltpu.VMEM(shape, LOW)
    full = lambda *shape: pltpu.VMEM(shape + vectors.shape, F32)
    copies = (
        3 * quarters + 1 + 2 * (tensor - 1) + 3 * masks + masks + 1 + 2 * (tensor - 1)
        + 4 * (masks + 1 + masks)
    )
    return pl.pallas_call(
        functools.partial(sum_kernel, plane, subs, seq_dev, len(before)),
        in_specs=[pl.BlockSpec(memory_space=pltpu.VMEM)] * 5
        + [pl.BlockSpec(memory_space=pl.ANY)] * len(before),
        out_specs=[pl.BlockSpec(memory_space=pltpu.VMEM)] * 5,
        out_shape=[
            jax.ShapeDtypeStruct((2, 2, quarters) + piece, LOW),
            jax.ShapeDtypeStruct((quarters, 2) + share, LOW),
            jax.ShapeDtypeStruct((quarters, 2) + out_share, LOW),
            jax.ShapeDtypeStruct(vectors.shape, F32),
            jax.ShapeDtypeStruct(up_shape, F32),
        ],
        scratch_shapes=[
            low(2, tensor - 1, *piece),
            low(quarters, *share),
            low(quarters, *share),
            low(quarters, tensor, *out_share),
            low(quarters, *share),
            low(quarters, *share),
            low(quarters, tensor, *out_share),
            low(masks, *share),
            low(masks, *share),
            low(masks, tensor, *out_share),
            low(*share),
            low(tensor - 1, *out_share),
            low(*share),
            low(tensor, *out_share),
            low(2, seq_dev - 1, *piece),
            full(),
            full(masks),
            full(tensor - 1),
            full(),
            full(),
            pltpu.SemaphoreType.DMA((copies,)),
            pltpu.SemaphoreType.DMA((copies,)),
        ],
        compiler_params=pltpu.CompilerParams(
            collective_id=1, has_side_effects=True, vmem_limit_bytes=48 << 20
        ),
        cost_estimate=pl.CostEstimate(flops=1 << 24, bytes_accessed=1 << 27, transcendentals=0),
    )(units, later, now, output, vectors, *before)


def gather_kernel(
    plane, subs, seq_dev, stream, triple, output, units, small,
    stream_out, triple_out, output_out, early_out, rest_out, small_out, send_sems, recv_sems,
):
    wires = Wires(plane, subs, seq_dev, send_sems, recv_sems)
    quarters, core = wires.quarters, wires.core
    offsets = [(k, j) for k in range(subs) for j in range(seq_dev)]
    ahead = range(1, len(offsets))
    masks = range(1, quarters)
    wires.greet(
        [wires.at_core()]
        + [wires.at_plane(mask) for mask in masks]
        + [wires.at_member(k, j) for k, j in offsets[1:]]
    )
    mine = 2 * wires.spot() + core
    share, out_share = triple_out.shape[1:], output_out.shape[2:]
    back = lambda z: wires.at_member(-offsets[z][0], -offsets[z][1])
    triple_got = wires.send(triple.at[mine], triple_out.at[mine], back(1))
    output_got = [wires.send(output.at[mine], output_out.at[z - 1, mine], back(z)) for z in ahead]
    small_got = [wires.send(small, small_out.at[z - 1], back(z)) for z in ahead]
    triple_got.wait_recv()
    stream_got = [wires.send(stream, stream_out.at[k - 1], wires.at_member(-k, 0)) for k in range(1, subs)]
    last, passed = [], []
    ref = triple_out.at[mine]
    for mask in masks:
        passed.append((mask, wires.send(ref, ref, wires.at_plane(mask))))
    last.append(wires.send(ref, ref, wires.at_core()))
    for copy in output_got:
        copy.wait_recv()
    early_got = wires.send(units, early_out.at[0], back(1))
    output_passed = []
    for mask in masks:
        for z in ahead:
            ref = output_out.at[z - 1, mine]
            output_passed.append((z, mask, wires.send(ref, ref, wires.at_plane(mask))))
    for z in ahead:
        ref = output_out.at[z - 1, mine]
        last.append(wires.send(ref, ref, wires.at_core()))
    for mask, copy in passed:
        copy.wait_recv()
        ref = triple_out.at[2 * wires.spot(mask) + core]
        last.append(wires.send(ref, ref, wires.at_core()))
    early_got.wait_recv()
    rest_got = [wires.send(units, rest_out.at[z - 2], back(z)) for z in ahead if z > 1]
    for mask in masks:
        last.append(wires.send(early_out.at[0], early_out.at[mask], wires.at_plane(mask)))
    for z, mask, copy in output_passed:
        copy.wait_recv()
        ref = output_out.at[z - 1, 2 * wires.spot(mask) + core]
        last.append(wires.send(ref, ref, wires.at_core()))
    for copy in small_got + stream_got + rest_got + last:
        copy.wait_recv()
    wires.finish()


def gather_all(plane, seq_dev, stream, triple, output, units, small):
    tensor, quarters = lax.axis_size("tensor"), 2 ** len(plane)
    subs, masks = tensor // seq_dev, quarters - 1
    others = tensor - 1
    copies = 2 + subs - 1 + 2 * others + 2 * quarters - 1 + 2 * others * quarters + others + masks
    return pl.pallas_call(
        functools.partial(gather_kernel, plane, subs, seq_dev),
        in_specs=[pl.BlockSpec(memory_space=pltpu.VMEM)] * 5,
        out_specs=[pl.BlockSpec(memory_space=pltpu.VMEM)] * 6,
        out_shape=[
            jax.ShapeDtypeStruct((subs - 1,) + stream.shape, LOW),
            jax.ShapeDtypeStruct(triple.shape, LOW),
            jax.ShapeDtypeStruct((others,) + output.shape, LOW),
            jax.ShapeDtypeStruct((quarters,) + units.shape, LOW),
            jax.ShapeDtypeStruct((others - 1,) + units.shape, LOW),
            jax.ShapeDtypeStruct((others,) + small.shape, F32),
        ],
        scratch_shapes=[
            pltpu.SemaphoreType.DMA((copies,)),
            pltpu.SemaphoreType.DMA((copies,)),
        ],
        compiler_params=pltpu.CompilerParams(
            collective_id=2, has_side_effects=True, vmem_limit_bytes=32 << 20
        ),
        cost_estimate=pl.CostEstimate(flops=1 << 20, bytes_accessed=1 << 27, transcendentals=0),
    )(stream, triple, output, units, small)


def gaussian_pair(value):
    cumulative = 0.5 * (1.0 + jax.scipy.special.erf(value * (1.0 / math.sqrt(2.0))))
    slope = cumulative + value * jnp.exp(-0.5 * value * value) * (1.0 / math.sqrt(2.0 * math.pi))
    return (value * cumulative).astype(LOW), slope.astype(LOW)


def on_device(
    plane,
    stream_in,
    timestep,
    lengths,
    time_weight,
    time_bias,
    triple_weight,
    query_value_bias,
    output_weight,
    output_bias,
    first_gain,
    first_shift,
    up_weight,
    up_bias,
    down_weight,
    down_bias,
    second_gain,
    second_shift,
    cotangent,
):
    rows, width = stream_in.shape
    seq_dev = timestep.shape[0]
    tensor = lax.axis_size("tensor")
    subs = tensor // seq_dev
    local = triple_weight.shape[2]
    units = up_weight.shape[1]
    half_units = units // 2
    quarters = 2 ** len(plane)
    piece_units = half_units // quarters
    me = lax.axis_index("tensor")
    core = lax.axis_index("core")
    spot = lax.axis_index(plane)
    sub = me % subs
    which = me // subs
    offsets = [(k, j) for k in range(subs) for j in range(seq_dev)]
    others = offsets[1:]

    def member(i, k, j):
        return ((i // subs + j) % seq_dev) * subs + (i % subs + k) % subs

    def fetch(x, k, j):
        return lax.ppermute(x, "tensor", [(member(i, k, j), i) for i in range(tensor)])

    def send(x, k, j):
        return lax.ppermute(x, "tensor", [(i, member(i, k, j)) for i in range(tensor)])

    def swap(x, axis):
        return lax.ppermute(x, axis, [(0, 1), (1, 0)])

    def across(x, mask):
        return lax.ppermute(x, plane, [(i, i ^ mask) for i in range(quarters)])

    def pick(x, index, axis=0):
        return lax.dynamic_index_in_dim(x, index, axis, keepdims=False)

    def tie(x, *before):
        return lax.optimization_barrier((x,) + before)[0]

    def ordered(parts, index):
        parts = jnp.stack(parts) if isinstance(parts, (list, tuple)) else parts
        return jnp.stack([pick(parts, index ^ m) for m in range(parts.shape[0])])

    triple_three = triple_weight.transpose(1, 0, 2)
    triple_own = jnp.concatenate([triple_three[i] for i in range(3)], axis=1)
    part = width // (2 * quarters)
    out_part = local // (2 * quarters)
    up_half = lax.dynamic_slice_in_dim(up_weight, core * half_units, half_units, 1).T
    down_half = lax.dynamic_slice_in_dim(down_weight, core * half_units, half_units, 0)
    units_mine = [
        ordered(x.reshape(quarters, piece_units, width), spot) for x in (up_half, down_half)
    ]
    small = jnp.concatenate([up_bias, query_value_bias.reshape(-1)])
    pad = -small.shape[0] % 1024
    raw, triple_got, out_got, early, rest, small_got = gather_all(
        plane,
        seq_dev,
        stream_in,
        triple_own.reshape(2 * quarters, part, 3 * local),
        output_weight.reshape(2 * quarters, out_part, width),
        jnp.stack([units_mine[0][0], units_mine[1][0]]),
        jnp.pad(small, (0, pad)).reshape(-1, 128),
    )
    raw = [stream_in] + [raw[k] for k in range(subs - 1)]
    triples = [triple_own, triple_got.reshape(width, 3 * local)]
    out_got = out_got.reshape(tensor - 1, local, width)
    out_full = jnp.concatenate([output_weight[None], out_got]).reshape(tensor * local, width)
    small_of = {(0, 0): small}
    for z, (k, j) in enumerate(others):
        small_of[(k, j)] = small_got[z].reshape(-1)[: small.shape[0]]
    rest_of = [rest] + [across(rest, m) for m in range(1, quarters)]

    def all_rows(which):
        full = []
        for m in range(quarters):
            full += [units_mine[which][m][None], early[m, which][None], rest_of[m][:, which]]
        return jnp.concatenate(full, axis=0).reshape(-1, width)

    up_rows, down_rows = all_rows(0), all_rows(1)

    embedded_own = sinusoid(timestep, width).astype(LOW)
    shift_own = plain(embedded_own, time_weight) + time_bias
    shift_row = pick(shift_own, which)
    limit = pick(lengths, which)
    stream = stream_in.astype(F32) + shift_row
    stream_low = (jnp.concatenate(raw, axis=0).astype(F32) + shift_row).astype(LOW)
    place = (jnp.arange(LEN, dtype=jnp.int32) + sub * rows) % LEN
    mask = jnp.where(place < limit, 0.0, MASKED).astype(F32)
    mask_row, mask_column = mask[None, :], mask[:, None]
    valid = (place[:rows] < limit).astype(F32)

    pairs = local // (2 * HD)
    qv = [small_of[(0, j)][units:].reshape(2, local) for j in range(seq_dev)]
    projected, context, log_total = [], [], []
    for j in range(seq_dev):
        bias = jnp.concatenate([qv[j][0], jnp.zeros((local,), F32), qv[j][1]])
        projected.append(plain(stream_low, triples[j]) + bias)
        here = [attend(projected[j], mask_row, pair) for pair in range(pairs)]
        context.append([x[0] for x in here])
        log_total.append([x[1] for x in here])
    block = lambda x, k: x[k * rows : (k + 1) * rows]
    columns = []
    for k in range(subs):
        back = (subs - k) % subs
        for j in range(seq_dev):
            mine = jnp.concatenate([block(x, back) for x in context[j]], axis=1).astype(LOW)
            columns.append(mine if k == 0 else send(mine, back, 0))
    context_own = jnp.concatenate(columns, axis=1)

    branch = plain(context_own, out_full) + output_bias
    middle, normed_first, factor_first = norm_forward(stream + branch, first_gain, first_shift)
    middle_low = middle.astype(LOW)

    bias_all = jnp.stack([small_of[o][:units] for o in offsets])
    bias_half = lax.dynamic_slice_in_dim(bias_all, core * half_units, half_units, 1)
    bias_rel = ordered(
        bias_half.reshape(tensor, quarters, piece_units).transpose(1, 0, 2), spot
    ).reshape(-1)
    both = jnp.concatenate([middle_low, swap(middle_low, "core")], axis=0)
    active, slope = lax.optimization_barrier(
        gaussian_pair(against(both, up_rows) + bias_rel)
    )
    feed_other = plain(active[rows:], down_rows).astype(LOW)
    feed = plain(active[:rows], down_rows) + swap(feed_other, "core").astype(F32) + down_bias
    result, normed_second, factor_second = norm_forward(middle + feed, second_gain, second_shift)
    block_output = result.astype(LOW)

    to_second, grad_second_gain, grad_second_shift = norm_backward(
        cotangent.astype(F32), normed_second, factor_second, second_gain
    )
    feed_grad = to_second.astype(LOW)
    grad_down_bias = jnp.sum(feed_grad.astype(F32), axis=0)
    feed_grad_both = jnp.concatenate([feed_grad, swap(feed_grad, "core")], axis=0)

    def by_mask(total):
        shaped = total.reshape(quarters, tensor, piece_units, width)
        return {m: shaped[m] for m in range(quarters)}

    down_total = by_mask(inner(active, feed_grad_both).astype(LOW))
    before_grad = (against(feed_grad_both, down_rows) * slope.astype(F32)).astype(LOW)
    up_total = by_mask(inner(before_grad, both).astype(LOW))
    units_sum = wide(jnp.stack([up_total[0], down_total[0]]))
    for m in range(1, quarters):
        units_sum = units_sum + wide(across(jnp.stack([up_total[m], down_total[m]]), m))
    units_sum = units_sum.astype(LOW)
    grad_up_rel = jnp.sum(before_grad.astype(F32), axis=0)
    middle_other = plain(before_grad[rows:], up_rows).astype(LOW)
    middle_grad = (
        to_second + plain(before_grad[:rows], up_rows) + swap(middle_other, "core").astype(F32)
    )

    to_first, grad_first_gain, grad_first_shift = norm_backward(
        middle_grad, normed_first, factor_first, first_gain
    )
    branch_grad = to_first.astype(LOW)
    grad_output_bias = jnp.sum(branch_grad.astype(F32), axis=0)
    context_grad = against(branch_grad, out_full).astype(LOW)
    shaped = context_grad.reshape(rows, subs, seq_dev, local)
    incoming = [None] * seq_dev
    for j in reversed(range(seq_dev)):
        parts = []
        for k in range(subs):
            back = (subs - k) % subs
            mine = shaped[:, back, j]
            parts.append(mine if k == 0 else send(mine, back, 0))
        incoming[j] = jnp.concatenate(parts, axis=0).astype(F32)

    def backward(j, pair, before):
        return attend_back(
            projected[j], mask_column, context[j][pair], log_total[j][pair], incoming[j], pair, before
        )

    def together(parts):
        return jnp.concatenate([x[i] for i in range(3) for x in parts], axis=1).astype(LOW)

    grads = [None] * seq_dev
    for j in reversed(range(seq_dev)):
        grads[j] = together([backward(j, pair, []) for pair in range(pairs)])
    triple_parts = [
        inner(stream_low, grads[j]).astype(LOW).reshape(quarters, 2, part, 3 * local)
        for j in range(seq_dev)
    ]
    out_total = inner(context_own, branch_grad).astype(LOW)
    out_total = out_total.reshape(tensor, quarters, 2, out_part, width).transpose(1, 2, 0, 3, 4)
    away = [
        send(
            sum(against(block(grads[j], k), triples[j]) for j in range(seq_dev)).astype(LOW), k, 0
        )
        for k in range(1, subs)
    ]
    stream_own = to_first + sum(
        against(block(grads[j], 0), triples[j]) for j in range(seq_dev)
    )

    dp_index = spot * 2 + core
    seqs = quarters * 2 * seq_dev
    column_sums = [jnp.sum(grads[j].astype(F32), axis=0) for j in range(seq_dev)]
    shift_part = jnp.sum(to_first, axis=0) + sum(
        against(column_sums[j][None].astype(F32), triples[j].astype(F32))[0]
        for j in range(seq_dev)
    )
    hot = (jnp.arange(seqs) == dp_index * seq_dev + which).astype(F32)
    shift_rows = hot[:, None] * shift_part[None, :]
    squares = jnp.stack([jnp.sum(jnp.sum(x * x, axis=1) * valid) for x in (stream, branch, feed)])
    table = hot[:, None] * squares[None, :]
    steps_hot = (
        jnp.arange(seqs)[:, None] == dp_index * seq_dev + jnp.arange(seq_dev)[None, :]
    ).astype(F32)
    steps_all = jnp.sum(steps_hot * timestep.astype(F32)[None, :], axis=1) * (me == 0)
    up_canonical = ordered(grad_up_rel.reshape(quarters, tensor, piece_units), spot)
    up_canonical = up_canonical.transpose(1, 0, 2).reshape(tensor, half_units)
    full_up = jnp.zeros((tensor, 2, half_units), F32)
    full_qv = jnp.zeros((tensor, 2, local), F32)
    for index, (k, j) in enumerate(offsets):
        at = ((which + j) % seq_dev) * subs + (sub + k) % subs
        row = jnp.where(jnp.arange(2)[:, None] == core, up_canonical[index][None], 0.0)
        full_up = lax.dynamic_update_slice_in_dim(full_up, row[None], at, 0)
        if k == 0:
            value = column_sums[j].reshape(3, local)
            value = jnp.stack([value[0], value[2]])
            full_qv = lax.dynamic_update_slice_in_dim(full_qv, value[None], at, 0)

    vectors = [
        grad_first_gain,
        grad_first_shift,
        grad_output_bias,
        grad_down_bias,
        grad_second_gain,
        grad_second_shift,
        full_up.reshape(-1),
        shift_rows.reshape(-1),
        full_qv.reshape(-1),
        table.reshape(-1),
        steps_all,
    ]
    packed = jnp.concatenate(vectors)
    packed = jnp.pad(packed, (0, -packed.shape[0] % width)).reshape(-1, width)
    units_all, triple_all, out_all, packed, up_all = sum_all(
        plane, seq_dev, units_sum, triple_parts[1], triple_parts[0], out_total, packed, away + [stream_own]
    )
    grad_up_weight = up_all
    if up_all.ndim > 2:
        grad_up_weight = jnp.concatenate(
            [up_all[half, place] for half in range(2) for place in range(quarters)], axis=1
        )
    grad_down_weight = units_all[1].reshape(units, width).astype(F32)
    grad_output_weight = out_all.reshape(local, width).astype(F32)
    triple_all = triple_all.reshape(width, 3 * local)
    grad_triple = jnp.stack([triple_all[:, i * local : (i + 1) * local] for i in range(3)])
    grad_triple = grad_triple.astype(F32).transpose(1, 0, 2)
    input_gradient = (stream_own + sum(wide(x) for x in away)).astype(LOW)
    packed = packed.reshape(-1)
    got, at = [], 0
    for vector in vectors:
        got.append(packed[at : at + vector.shape[0]])
        at += vector.shape[0]
    full_up = pick(got[6].reshape(tensor, units), me)
    shift_grad = got[7].reshape(seqs, width)
    grad_query_value = pick(got[8].reshape(tensor, 2, local), me)
    table, steps_all = got[9].reshape(seqs, 3), got[10]
    grad_time_bias = jnp.sum(shift_grad, axis=0)
    embedded_all = sinusoid(steps_all, width).astype(LOW).astype(F32)
    grad_time_weight = lax.dot_general(
        embedded_all, shift_grad, TN, precision=lax.Precision.HIGHEST, preferred_element_type=F32
    )
    own_table = lax.dynamic_slice_in_dim(table, dp_index * seq_dev, seq_dev, 0)
    root_squares = jnp.sqrt(own_table / (lengths.astype(F32)[:, None] * width) + STAT_EPS)
    return (
        block_output,
        input_gradient,
        root_squares,
        grad_time_weight,
        grad_time_bias,
        grad_triple,
        grad_query_value,
        grad_output_weight,
        got[2],
        got[0],
        got[1],
        grad_up_weight,
        full_up,
        grad_down_weight,
        got[3],
        got[4],
        got[5],
    )


def solution(mesh):
    tensor = mesh.shape["tensor"]
    spots = mesh.shape["dp"] // 2
    plane = tuple(f"plane{i}" for i in range(spots.bit_length() - 1))
    fine = Mesh(
        mesh.devices.reshape((2,) * len(plane) + (2, tensor)), plane + ("core", "tensor")
    )
    dp = plane + ("core",)
    row = P(dp + ("tensor",), None)
    in_specs = (
        row,
        P(dp),
        P(dp),
        P(),
        P(),
        P(None, None, "tensor"),
        P(None, "tensor"),
        P("tensor", None),
        P(),
        P(),
        P(),
        P(None, "tensor"),
        P("tensor"),
        P("tensor", None),
        P(),
        P(),
        P(),
        row,
    )
    out_specs = (
        row,
        row,
        P(dp, None),
        P(),
        P(),
        P(None, None, "tensor"),
        P(None, "tensor"),
        P("tensor", None),
        P(),
        P(),
        P(),
        P(None, "tensor"),
        P("tensor"),
        P("tensor", None),
        P(),
        P(),
        P(),
    )
    return jax.shard_map(
        functools.partial(on_device, plane),
        mesh=fine,
        in_specs=in_specs,
        out_specs=out_specs,
        check_vma=False,
    )
```

```python
import functools
import math

import jax
import jax.numpy as jnp
from jax import lax
from jax.experimental import pallas as pl
from jax.experimental.pallas import tpu as pltpu
from jax.sharding import Mesh
from jax.sharding import PartitionSpec as P

HD = 64
LEN = 1024
NORM_EPS = 1e-05
STAT_EPS = 1e-06
MASKED = -1e30
LOW = jnp.bfloat16
F32 = jnp.float32
NT = (((1,), (1,)), ((), ()))
TN = (((0,), (0,)), ((), ()))


def sinusoid(steps, width):
    half = width // 2
    rates = jnp.exp(-math.log(10000.0) * jnp.arange(half).astype(F32) / half)
    angles = steps.astype(F32)[:, None] * rates[None, :]
    return jnp.concatenate([jnp.sin(angles), jnp.cos(angles)], axis=1)


def plain(left, right):
    return jnp.dot(left, right, preferred_element_type=F32)


def inner(left, right):
    return lax.dot_general(left, right, TN, preferred_element_type=F32)


def against(left, right):
    return lax.dot_general(left, right, NT, preferred_element_type=F32)


def norm_forward(total, gain, shift):
    middle = jnp.mean(total, axis=-1, keepdims=True)
    centred = total - middle
    spread = jnp.mean(centred * centred, axis=-1, keepdims=True)
    factor = lax.rsqrt(spread + NORM_EPS)
    normed = centred * factor
    return (normed * gain + shift, normed, factor)


def norm_backward(upstream, normed, factor, gain):
    pushed = upstream * gain
    first = jnp.mean(pushed, axis=-1, keepdims=True)
    second = jnp.mean(pushed * normed, axis=-1, keepdims=True)
    return (
        factor * (pushed - first - normed * second),
        jnp.sum(upstream * normed, axis=0),
        jnp.sum(upstream, axis=0),
    )


def split3(x):
    hi = x.astype(LOW)
    rest = x - hi.astype(F32)
    mid = rest.astype(LOW)
    return hi, mid, (rest - mid.astype(F32)).astype(LOW)


def extra_lanes(parts, one, count):
    lane = lax.broadcasted_iota(jnp.int32, (count, HD), 1)
    out = jnp.where(lane == len(parts), 1.0, 0.0) if one else jnp.zeros((count, HD), F32)
    for index, part in enumerate(parts):
        out = jnp.where(lane == index, jnp.broadcast_to(part.astype(F32), (count, HD)), out)
    return out.astype(LOW)


def head(x, h):
    return x[:, h * HD : (h + 1) * HD]


def attend_kernel(rows, mask_ref, q_ref, k_ref, v_ref, context_ref, log_ref):
    count = q_ref.shape[0]
    mask = mask_ref[...]
    keys = k_ref[...].astype(LOW)
    values = v_ref[...].astype(LOW)
    for start in range(0, count, rows):
        part = slice(start, start + rows)
        queries = q_ref[part].astype(LOW) * LOW(HD**-0.5)
        contexts, logs = [], []
        for h in range(2):
            scores = lax.dot_general(
                head(queries, h), head(keys, h), NT, preferred_element_type=F32
            )
            scores = scores + mask
            highest = jnp.max(scores, axis=1, keepdims=True)
            probs = jnp.exp(scores - highest)
            total = jnp.sum(probs, axis=1, keepdims=True)
            contexts.append(plain(probs.astype(LOW), head(values, h)) / total)
            logs.append(jnp.broadcast_to(highest + jnp.log(total), (rows, HD)))
        context_ref[part] = jnp.concatenate(contexts, axis=1)
        log_ref[part] = jnp.concatenate(logs, axis=1)


def attend(projected, mask_row):
    count, width = projected.shape
    local = width // 3
    pairs = local // (2 * HD)
    block = lambda which: pl.BlockSpec((count, 2 * HD), lambda p: (0, which * pairs + p))
    return pl.pallas_call(
        functools.partial(attend_kernel, 512),
        grid=(pairs,),
        in_specs=[pl.BlockSpec((1, count), lambda p: (0, 0)), block(0), block(1), block(2)],
        out_specs=[block(0)] * 2,
        out_shape=[jax.ShapeDtypeStruct((count, local), F32)] * 2,
        compiler_params=pltpu.CompilerParams(vmem_limit_bytes=40 << 20),
        cost_estimate=pl.CostEstimate(
            flops=16 * count * count * local,
            bytes_accessed=20 * count * local,
            transcendentals=count * count * local // HD,
        ),
    )(mask_row, projected, projected, projected)


def attend_back_kernel(
    rows, mask_ref, q_ref, k_ref, v_ref, context_ref, log_ref, grad_ref, dq_ref, dk_ref, dv_ref
):
    count = k_ref.shape[0]
    lane = lax.broadcasted_iota(jnp.int32, (count, HD), 1)
    three = jnp.where(lane < 3, 1.0, 0.0)
    key_extra = jnp.where(lane == 3, jnp.broadcast_to(mask_ref[...], (count, HD)), three)
    key_extra = key_extra.astype(LOW)
    value_extra = three.astype(LOW)
    queries = q_ref[...].astype(LOW) * LOW(HD**-0.5)
    keys = k_ref[...].astype(LOW)
    values = v_ref[...].astype(LOW)
    logs = log_ref[...]
    grads = grad_ref[...]
    dots = grads * context_ref[...]
    grads = grads.astype(LOW)
    kx, vx, qx, gx, dq = [], [], [], [], [None, None]
    for h in range(2):
        extra = extra_lanes(split3(-logs[:, h * HD : h * HD + 1]), True, count)
        qx.append(jnp.concatenate([head(queries, h), extra], axis=1))
        row_dot = jnp.sum(head(dots, h), axis=1, keepdims=True)
        extra = extra_lanes(split3(-row_dot), False, count)
        gx.append(jnp.concatenate([head(grads, h), extra], axis=1))
        kx.append(jnp.concatenate([head(keys, h), key_extra], axis=1))
        vx.append(jnp.concatenate([head(values, h), value_extra], axis=1))
    for start in range(0, count, rows):
        part = slice(start, start + rows)
        dk, dv = [], []
        for h in range(2):
            probs = jnp.exp(lax.dot_general(kx[h][part], qx[h], NT, preferred_element_type=F32))
            pushed = lax.dot_general(vx[h][part], gx[h], NT, preferred_element_type=F32)
            scores_grad = (probs * pushed).astype(LOW)
            dv.append(plain(probs.astype(LOW), gx[h])[:, :HD])
            dk.append(plain(scores_grad, qx[h])[:, :HD])
            more = lax.dot_general(scores_grad, kx[h][part], TN, preferred_element_type=F32)
            dq[h] = more if start == 0 else dq[h] + more
        dk_ref[part] = jnp.concatenate(dk, axis=1)
        dv_ref[part] = jnp.concatenate(dv, axis=1)
    dq_ref[...] = jnp.concatenate([x[:, :HD] for x in dq], axis=1) * HD**-0.5


def attend_back(projected, mask_column, context, log_total, grad):
    count, width = projected.shape
    local = width // 3
    pairs = local // (2 * HD)
    block = lambda which: pl.BlockSpec((count, 2 * HD), lambda p: (0, which * pairs + p))
    return pl.pallas_call(
        functools.partial(attend_back_kernel, 512),
        grid=(pairs,),
        in_specs=[pl.BlockSpec((count, 1), lambda p: (0, 0)), block(0), block(1), block(2)]
        + [block(0)] * 3,
        out_specs=[block(0)] * 3,
        out_shape=[jax.ShapeDtypeStruct((count, local), F32)] * 3,
        compiler_params=pltpu.CompilerParams(vmem_limit_bytes=50 << 20),
        cost_estimate=pl.CostEstimate(
            flops=40 * count * count * local,
            bytes_accessed=40 * count * local,
            transcendentals=count * count * local // HD,
        ),
    )(mask_column, projected, projected, projected, context, log_total, grad)


class Wires:
    def __init__(self, plane, subs, seq_dev, send_sems, recv_sems):
        self.plane, self.subs, self.seq_dev = plane, subs, seq_dev
        self.send_sems, self.recv_sems, self.sent = send_sems, recv_sems, []
        self.bits = [lax.axis_index(name) for name in plane]
        self.core = lax.axis_index("core")
        me = lax.axis_index("tensor")
        self.sub, self.which = lax.rem(me, subs), lax.div(me, subs)
        self.quarters = 2 ** len(plane)

    def spot(self, mask=0):
        total, count = 0, len(self.plane)
        for i, bit in enumerate(self.bits):
            flip = (mask >> (count - 1 - i)) & 1
            total = total + (1 - bit if flip else bit) * 2 ** (count - 1 - i)
        return total

    def at_plane(self, mask):
        count = len(self.plane)
        return {
            name: 1 - bit
            for i, (name, bit) in enumerate(zip(self.plane, self.bits))
            if (mask >> (count - 1 - i)) & 1
        }

    def at_core(self):
        return {"core": 1 - self.core}

    def at_member(self, k, j):
        return {
            "tensor": lax.rem(self.which + j + self.seq_dev, self.seq_dev) * self.subs
            + lax.rem(self.sub + k + self.subs, self.subs)
        }

    def greet(self, targets):
        barrier = pltpu.get_barrier_semaphore()
        for target in targets:
            pl.semaphore_signal(barrier, inc=1, device_id=target, device_id_type=pl.DeviceIdType.MESH)
        pl.semaphore_wait(barrier, len(targets))

    def send(self, src, dst, target):
        index = len(self.sent)
        copy = pltpu.make_async_remote_copy(
            src_ref=src,
            dst_ref=dst,
            send_sem=self.send_sems.at[index],
            recv_sem=self.recv_sems.at[index],
            device_id=target,
            device_id_type=pl.DeviceIdType.MESH,
        )
        copy.start()
        self.sent.append(copy)
        return copy

    def finish(self):
        for copy in self.sent:
            copy.wait_send()


def wide(x):
    return x.astype(F32)


def sum_kernel(
    plane, subs, seq_dev, ordering, units, later, now, output, vectors, *refs
):
    (
    units_out, triple_out, output_out, vectors_out, up_out,
    units_z, later_core, now_core, output_core, later_half, now_half, output_half,
    later_plane, now_plane, output_plane, triple_z, output_z, triple_mine, output_mine, units_away,
    vectors_core, vectors_plane, vectors_z, vectors_one, vectors_two, send_sems, recv_sems,
    ) = refs[ordering:]
    wires = Wires(plane, subs, seq_dev, send_sems, recv_sems)
    quarters, core = wires.quarters, wires.core
    spot = wires.spot()
    offsets = [(k, j) for k in range(subs) for j in range(seq_dev)]
    ahead = range(1, len(offsets))
    masks = range(1, quarters)
    wires.greet(
        [wires.at_core()]
        + [wires.at_plane(mask) for mask in masks]
        + [wires.at_member(k, j) for k, j in offsets[1:]]
    )
    core_got = []
    for source, target in ((later, later_core), (output, output_core), (now, now_core)):
        core_got.append(
            [
                wires.send(source.at[place, 1 - core], target.at[place], wires.at_core())
                for place in range(quarters)
            ]
        )
    vectors_got = wires.send(vectors, vectors_core, wires.at_core())

    inner_count = (subs - 1) * seq_dev

    def units_inside(which):
        return [
            wires.send(
                units.at[which, pl.ds(k * seq_dev, seq_dev)],
                units_z.at[which, pl.ds((k - 1) * seq_dev, seq_dev)],
                wires.at_member(k, 0),
            )
            for k in range(1, subs)
        ]

    def units_part(which, j):
        total = wide(units[which, j])
        for k in range(1, subs):
            total = total + wide(units_z[which, (k - 1) * seq_dev + j])
        return total

    def units_across(which, got):
        for copy in got:
            copy.wait_recv()
        copies = []
        for j in range(1, seq_dev):
            units_away[which, j - 1] = units_part(which, j).astype(LOW)
            copies.append(
                wires.send(
                    units_away.at[which, j - 1],
                    units_z.at[which, inner_count + j - 1],
                    wires.at_member(0, j),
                )
            )
        return copies

    units_first = units_inside(0)
    plane_got = []
    for got, source, received, half, target in (
        (core_got[0], later, later_core, later_half, later_plane),
        (core_got[1], output, output_core, output_half, output_plane),
        (core_got[2], now, now_core, now_half, now_plane),
    ):
        for copy in got:
            copy.wait_recv()
        for place in range(quarters):
            half[place] = (wide(source[place, core]) + wide(received[place])).astype(LOW)
        plane_got.append(
            [
                wires.send(half.at[wires.spot(mask)], target.at[mask - 1], wires.at_plane(mask))
                for mask in masks
            ]
        )
    vectors_got.wait_recv()
    vectors_one[...] = vectors[...] + vectors_core[...]
    vectors_got = [
        wires.send(vectors_one, vectors_plane.at[mask - 1], wires.at_plane(mask)) for mask in masks
    ]
    last, up_crossed, passed = [], [], []

    def hand_round(slot, crossed):
        for mask in masks:
            got = wires.send(slot(spot), slot(spot), wires.at_plane(mask))
            passed.append((slot, crossed, mask, got))
        crossed.append((0, wires.send(slot(spot), slot(spot), wires.at_core())))

    def hand_over(count=None):
        for _ in range(len(passed) if count is None else count):
            slot, crossed, mask, copy = passed.pop(0)
            copy.wait_recv()
            ref = slot(wires.spot(mask))
            crossed.append((mask, wires.send(ref, ref, wires.at_core())))

    def units_whole(which):
        for copy in units_got[which]:
            copy.wait_recv()
        total = units_part(which, 0)
        for j in range(1, seq_dev):
            total = total + wide(units_z[which, inner_count + j - 1])
        units_out[which, core, spot] = total.astype(LOW)
        hand_round(lambda place: units_out.at[which, core, place], last if which else up_crossed)

    units_got = [units_across(0, units_first)]
    units_second = units_inside(1)
    units_whole(0)
    units_got.append(units_across(1, units_second))
    for copy in plane_got[0]:
        copy.wait_recv()
    total = wide(later_half[spot])
    for mask in masks:
        total = total + wide(later_plane[mask - 1])
    triple_mine[...] = total.astype(LOW)
    triple_got = [wires.send(triple_mine, triple_z, wires.at_member(0, 1))]
    for copy in plane_got[1]:
        copy.wait_recv()
    total = wide(output_half[spot])
    for mask in masks:
        total = total + wide(output_plane[mask - 1])
    output_mine[...] = total.astype(LOW)
    output_got = [
        wires.send(output_mine.at[z], output_z.at[z - 1], wires.at_member(*offsets[z])) for z in ahead
    ]
    for copy in vectors_got:
        copy.wait_recv()
    total = vectors_one[...]
    for mask in masks:
        total = total + vectors_plane[mask - 1]
    vectors_two[...] = total
    vectors_got = [
        wires.send(vectors_two, vectors_z.at[z - 1], wires.at_member(*offsets[z])) for z in ahead
    ]
    units_whole(1)
    for copy in plane_got[2]:
        copy.wait_recv()
    for copy in triple_got:
        copy.wait_recv()
    total = wide(now_half[spot]) + wide(triple_z[...])
    for mask in masks:
        total = total + wide(now_plane[mask - 1])
    triple_out[spot, core] = total.astype(LOW)
    hand_round(lambda place: triple_out.at[place, core], last)
    for copy in output_got:
        copy.wait_recv()
    total = wide(output_mine[0])
    for z in ahead:
        total = total + wide(output_z[z - 1])
    output_out[spot, core] = total.astype(LOW)
    hand_round(lambda place: output_out.at[place, core], last)
    hand_over(2 * len(masks))

    def place_up(half, mask):
        place = wires.spot(mask)
        block = wide(units_out[0, half, place]).T
        wide_block = block.shape[1]
        if len(up_out.shape) == 2:
            first = pl.multiple_of((half * quarters + place) * wide_block, wide_block)
            up_out[:, pl.ds(first, wide_block)] = block
        else:
            up_out[half, place] = block

    for mask, copy in up_crossed:
        place_up(core, mask)
        copy.wait_recv()
        place_up(1 - core, mask)
    for copy in vectors_got:
        copy.wait_recv()
    total = vectors_two[...]
    for z in ahead:
        total = total + vectors_z[z - 1]
    vectors_out[...] = total
    hand_over()
    for _, copy in last:
        copy.wait_recv()
    wires.finish()


def sum_all(plane, seq_dev, units, later, now, output, vectors, before):
    tensor, quarters = lax.axis_size("tensor"), 2 ** len(plane)
    subs, masks = tensor // seq_dev, quarters - 1
    piece, share, out_share = units.shape[2:], later.shape[2:], output.shape[3:]
    up_shape = (piece[1], 2 * quarters * piece[0])
    if piece[0] % 128:
        up_shape = (2, quarters, piece[1], piece[0])
    low = lambda *shape: pltpu.VMEM(shape, LOW)
    full = lambda *shape: pltpu.VMEM(shape + vectors.shape, F32)
    copies = (
        3 * quarters + 1 + 2 * (tensor - 1) + 3 * masks + masks + 1 + 2 * (tensor - 1)
        + 4 * (masks + 1 + masks)
    )
    return pl.pallas_call(
        functools.partial(sum_kernel, plane, subs, seq_dev, len(before)),
        in_specs=[pl.BlockSpec(memory_space=pltpu.VMEM)] * 5
        + [pl.BlockSpec(memory_space=pl.ANY)] * len(before),
        out_specs=[pl.BlockSpec(memory_space=pltpu.VMEM)] * 5,
        out_shape=[
            jax.ShapeDtypeStruct((2, 2, quarters) + piece, LOW),
            jax.ShapeDtypeStruct((quarters, 2) + share, LOW),
            jax.ShapeDtypeStruct((quarters, 2) + out_share, LOW),
            jax.ShapeDtypeStruct(vectors.shape, F32),
            jax.ShapeDtypeStruct(up_shape, F32),
        ],
        scratch_shapes=[
            low(2, tensor - 1, *piece),
            low(quarters, *share),
            low(quarters, *share),
            low(quarters, tensor, *out_share),
            low(quarters, *share),
            low(quarters, *share),
            low(quarters, tensor, *out_share),
            low(masks, *share),
            low(masks, *share),
            low(masks, tensor, *out_share),
            low(*share),
            low(tensor - 1, *out_share),
            low(*share),
            low(tensor, *out_share),
            low(2, seq_dev - 1, *piece),
            full(),
            full(masks),
            full(tensor - 1),
            full(),
            full(),
            pltpu.SemaphoreType.DMA((copies,)),
            pltpu.SemaphoreType.DMA((copies,)),
        ],
        compiler_params=pltpu.CompilerParams(
            collective_id=1, has_side_effects=True, vmem_limit_bytes=48 << 20
        ),
        cost_estimate=pl.CostEstimate(flops=1 << 24, bytes_accessed=1 << 27, transcendentals=0),
    )(units, later, now, output, vectors, *before)


def gather_kernel(
    plane, subs, seq_dev, stream, triple, output, units, small,
    stream_out, triple_out, output_out, early_out, rest_out, small_out, send_sems, recv_sems,
):
    wires = Wires(plane, subs, seq_dev, send_sems, recv_sems)
    quarters, core = wires.quarters, wires.core
    offsets = [(k, j) for k in range(subs) for j in range(seq_dev)]
    ahead = range(1, len(offsets))
    masks = range(1, quarters)
    wires.greet(
        [wires.at_core()]
        + [wires.at_plane(mask) for mask in masks]
        + [wires.at_member(k, j) for k, j in offsets[1:]]
    )
    mine = 2 * wires.spot() + core
    share, out_share = triple_out.shape[1:], output_out.shape[2:]
    back = lambda z: wires.at_member(-offsets[z][0], -offsets[z][1])
    triple_got = wires.send(triple.at[mine], triple_out.at[mine], back(1))
    output_got = [wires.send(output.at[mine], output_out.at[z - 1, mine], back(z)) for z in ahead]
    small_got = [wires.send(small, small_out.at[z - 1], back(z)) for z in ahead]
    triple_got.wait_recv()
    stream_got = [wires.send(stream, stream_out.at[k - 1], wires.at_member(-k, 0)) for k in range(1, subs)]
    last, passed = [], []
    ref = triple_out.at[mine]
    for mask in masks:
        passed.append((mask, wires.send(ref, ref, wires.at_plane(mask))))
    last.append(wires.send(ref, ref, wires.at_core()))
    for copy in output_got:
        copy.wait_recv()
    early_got = wires.send(units, early_out.at[0], back(1))
    output_passed = []
    for mask in masks:
        for z in ahead:
            ref = output_out.at[z - 1, mine]
            output_passed.append((z, mask, wires.send(ref, ref, wires.at_plane(mask))))
    for z in ahead:
        ref = output_out.at[z - 1, mine]
        last.append(wires.send(ref, ref, wires.at_core()))
    for mask, copy in passed:
        copy.wait_recv()
        ref = triple_out.at[2 * wires.spot(mask) + core]
        last.append(wires.send(ref, ref, wires.at_core()))
    early_got.wait_recv()
    rest_got = [wires.send(units, rest_out.at[z - 2], back(z)) for z in ahead if z > 1]
    for mask in masks:
        last.append(wires.send(early_out.at[0], early_out.at[mask], wires.at_plane(mask)))
    for z, mask, copy in output_passed:
        copy.wait_recv()
        ref = output_out.at[z - 1, 2 * wires.spot(mask) + core]
        last.append(wires.send(ref, ref, wires.at_core()))
    for copy in small_got + stream_got + rest_got + last:
        copy.wait_recv()
    wires.finish()


def gather_all(plane, seq_dev, stream, triple, output, units, small):
    tensor, quarters = lax.axis_size("tensor"), 2 ** len(plane)
    subs, masks = tensor // seq_dev, quarters - 1
    others = tensor - 1
    copies = 2 + subs - 1 + 2 * others + 2 * quarters - 1 + 2 * others * quarters + others + masks
    return pl.pallas_call(
        functools.partial(gather_kernel, plane, subs, seq_dev),
        in_specs=[pl.BlockSpec(memory_space=pltpu.VMEM)] * 5,
        out_specs=[pl.BlockSpec(memory_space=pltpu.VMEM)] * 6,
        out_shape=[
            jax.ShapeDtypeStruct((subs - 1,) + stream.shape, LOW),
            jax.ShapeDtypeStruct(triple.shape, LOW),
            jax.ShapeDtypeStruct((others,) + output.shape, LOW),
            jax.ShapeDtypeStruct((quarters,) + units.shape, LOW),
            jax.ShapeDtypeStruct((others - 1,) + units.shape, LOW),
            jax.ShapeDtypeStruct((others,) + small.shape, F32),
        ],
        scratch_shapes=[
            pltpu.SemaphoreType.DMA((copies,)),
            pltpu.SemaphoreType.DMA((copies,)),
        ],
        compiler_params=pltpu.CompilerParams(
            collective_id=2, has_side_effects=True, vmem_limit_bytes=32 << 20
        ),
        cost_estimate=pl.CostEstimate(flops=1 << 20, bytes_accessed=1 << 27, transcendentals=0),
    )(stream, triple, output, units, small)


def gaussian_pair(value):
    cumulative = 0.5 * (1.0 + jax.scipy.special.erf(value * (1.0 / math.sqrt(2.0))))
    slope = cumulative + value * jnp.exp(-0.5 * value * value) * (1.0 / math.sqrt(2.0 * math.pi))
    return (value * cumulative).astype(LOW), slope.astype(LOW)


def on_device(
    plane,
    stream_in,
    timestep,
    lengths,
    time_weight,
    time_bias,
    triple_weight,
    query_value_bias,
    output_weight,
    output_bias,
    first_gain,
    first_shift,
    up_weight,
    up_bias,
    down_weight,
    down_bias,
    second_gain,
    second_shift,
    cotangent,
):
    rows, width = stream_in.shape
    seq_dev = timestep.shape[0]
    tensor = lax.axis_size("tensor")
    subs = tensor // seq_dev
    local = triple_weight.shape[2]
    units = up_weight.shape[1]
    half_units = units // 2
    quarters = 2 ** len(plane)
    piece_units = half_units // quarters
    me = lax.axis_index("tensor")
    core = lax.axis_index("core")
    spot = lax.axis_index(plane)
    sub = me % subs
    which = me // subs
    offsets = [(k, j) for k in range(subs) for j in range(seq_dev)]
    others = offsets[1:]

    def member(i, k, j):
        return ((i // subs + j) % seq_dev) * subs + (i % subs + k) % subs

    def fetch(x, k, j):
        return lax.ppermute(x, "tensor", [(member(i, k, j), i) for i in range(tensor)])

    def send(x, k, j):
        return lax.ppermute(x, "tensor", [(i, member(i, k, j)) for i in range(tensor)])

    def swap(x, axis):
        return lax.ppermute(x, axis, [(0, 1), (1, 0)])

    def across(x, mask):
        return lax.ppermute(x, plane, [(i, i ^ mask) for i in range(quarters)])

    def pick(x, index, axis=0):
        return lax.dynamic_index_in_dim(x, index, axis, keepdims=False)

    def tie(x, *before):
        return lax.optimization_barrier((x,) + before)[0]

    def ordered(parts, index):
        parts = jnp.stack(parts) if isinstance(parts, (list, tuple)) else parts
        return jnp.stack([pick(parts, index ^ m) for m in range(parts.shape[0])])

    triple_three = triple_weight.transpose(1, 0, 2)
    triple_own = jnp.concatenate([triple_three[i] for i in range(3)], axis=1)
    part = width // (2 * quarters)
    out_part = local // (2 * quarters)
    up_half = lax.dynamic_slice_in_dim(up_weight, core * half_units, half_units, 1).T
    down_half = lax.dynamic_slice_in_dim(down_weight, core * half_units, half_units, 0)
    units_mine = [
        ordered(x.reshape(quarters, piece_units, width), spot) for x in (up_half, down_half)
    ]
    small = jnp.concatenate([up_bias, query_value_bias.reshape(-1)])
    pad = -small.shape[0] % 1024
    raw, triple_got, out_got, early, rest, small_got = gather_all(
        plane,
        seq_dev,
        stream_in,
        triple_own.reshape(2 * quarters, part, 3 * local),
        output_weight.reshape(2 * quarters, out_part, width),
        jnp.stack([units_mine[0][0], units_mine[1][0]]),
        jnp.pad(small, (0, pad)).reshape(-1, 128),
    )
    raw = [stream_in] + [raw[k] for k in range(subs - 1)]
    triples = [triple_own, triple_got.reshape(width, 3 * local)]
    out_got = out_got.reshape(tensor - 1, local, width)
    out_full = jnp.concatenate([output_weight[None], out_got]).reshape(tensor * local, width)
    small_of = {(0, 0): small}
    for z, (k, j) in enumerate(others):
        small_of[(k, j)] = small_got[z].reshape(-1)[: small.shape[0]]
    rest_of = [rest] + [across(rest, m) for m in range(1, quarters)]

    def all_rows(which):
        full = []
        for m in range(quarters):
            full += [units_mine[which][m][None], early[m, which][None], rest_of[m][:, which]]
        return jnp.concatenate(full, axis=0).reshape(-1, width)

    up_rows, down_rows = all_rows(0), all_rows(1)

    embedded_own = sinusoid(timestep, width).astype(LOW)
    shift_own = plain(embedded_own, time_weight) + time_bias
    shift_row = pick(shift_own, which)
    limit = pick(lengths, which)
    stream = stream_in.astype(F32) + shift_row
    stream_low = (jnp.concatenate(raw, axis=0).astype(F32) + shift_row).astype(LOW)
    place = (jnp.arange(LEN, dtype=jnp.int32) + sub * rows) % LEN
    mask = jnp.where(place < limit, 0.0, MASKED).astype(F32)
    mask_row, mask_column = mask[None, :], mask[:, None]
    valid = (place[:rows] < limit).astype(F32)

    qv = [small_of[(0, j)][units:].reshape(2, local) for j in range(seq_dev)]
    projected, context, log_total = [], [], []
    for j in range(seq_dev):
        bias = jnp.concatenate([qv[j][0], jnp.zeros((local,), F32), qv[j][1]])
        projected.append(plain(stream_low, triples[j]) + bias)
        here = attend(projected[j], mask_row)
        context.append(here[0])
        log_total.append(here[1])
    block = lambda x, k: x[k * rows : (k + 1) * rows]
    columns = []
    for k in range(subs):
        back = (subs - k) % subs
        for j in range(seq_dev):
            mine = block(context[j], back).astype(LOW)
            columns.append(mine if k == 0 else send(mine, back, 0))
    context_own = jnp.concatenate(columns, axis=1)

    branch = plain(context_own, out_full) + output_bias
    middle, normed_first, factor_first = norm_forward(stream + branch, first_gain, first_shift)
    middle_low = middle.astype(LOW)

    bias_all = jnp.stack([small_of[o][:units] for o in offsets])
    bias_half = lax.dynamic_slice_in_dim(bias_all, core * half_units, half_units, 1)
    bias_rel = ordered(
        bias_half.reshape(tensor, quarters, piece_units).transpose(1, 0, 2), spot
    ).reshape(-1)
    both = jnp.concatenate([middle_low, swap(middle_low, "core")], axis=0)
    active, slope = lax.optimization_barrier(
        gaussian_pair(against(both, up_rows) + bias_rel)
    )
    feed_other = plain(active[rows:], down_rows).astype(LOW)
    feed = plain(active[:rows], down_rows) + swap(feed_other, "core").astype(F32) + down_bias
    result, normed_second, factor_second = norm_forward(middle + feed, second_gain, second_shift)
    block_output = result.astype(LOW)

    to_second, grad_second_gain, grad_second_shift = norm_backward(
        cotangent.astype(F32), normed_second, factor_second, second_gain
    )
    feed_grad = to_second.astype(LOW)
    grad_down_bias = jnp.sum(feed_grad.astype(F32), axis=0)
    feed_grad_both = jnp.concatenate([feed_grad, swap(feed_grad, "core")], axis=0)

    def by_mask(total):
        shaped = total.reshape(quarters, tensor, piece_units, width)
        return {m: shaped[m] for m in range(quarters)}

    down_total = by_mask(inner(active, feed_grad_both).astype(LOW))
    before_grad = (against(feed_grad_both, down_rows) * slope.astype(F32)).astype(LOW)
    up_total = by_mask(inner(before_grad, both).astype(LOW))
    units_sum = wide(jnp.stack([up_total[0], down_total[0]]))
    for m in range(1, quarters):
        units_sum = units_sum + wide(across(jnp.stack([up_total[m], down_total[m]]), m))
    units_sum = units_sum.astype(LOW)
    grad_up_rel = jnp.sum(before_grad.astype(F32), axis=0)
    middle_other = plain(before_grad[rows:], up_rows).astype(LOW)
    middle_grad = (
        to_second + plain(before_grad[:rows], up_rows) + swap(middle_other, "core").astype(F32)
    )

    to_first, grad_first_gain, grad_first_shift = norm_backward(
        middle_grad, normed_first, factor_first, first_gain
    )
    branch_grad = to_first.astype(LOW)
    grad_output_bias = jnp.sum(branch_grad.astype(F32), axis=0)
    context_grad = against(branch_grad, out_full).astype(LOW)
    shaped = context_grad.reshape(rows, subs, seq_dev, local)
    incoming = [None] * seq_dev
    for j in reversed(range(seq_dev)):
        parts = []
        for k in range(subs):
            back = (subs - k) % subs
            mine = shaped[:, back, j]
            parts.append(mine if k == 0 else send(mine, back, 0))
        incoming[j] = jnp.concatenate(parts, axis=0).astype(F32)

    grads = [None] * seq_dev
    for j in reversed(range(seq_dev)):
        here = attend_back(projected[j], mask_column, context[j], log_total[j], incoming[j])
        grads[j] = jnp.concatenate(here, axis=1).astype(LOW)
    triple_parts = [
        inner(stream_low, grads[j]).astype(LOW).reshape(quarters, 2, part, 3 * local)
        for j in range(seq_dev)
    ]
    out_total = inner(context_own, branch_grad).astype(LOW)
    out_total = out_total.reshape(tensor, quarters, 2, out_part, width).transpose(1, 2, 0, 3, 4)
    away = [
        send(
            sum(against(block(grads[j], k), triples[j]) for j in range(seq_dev)).astype(LOW), k, 0
        )
        for k in range(1, subs)
    ]
    stream_own = to_first + sum(
        against(block(grads[j], 0), triples[j]) for j in range(seq_dev)
    )

    dp_index = spot * 2 + core
    seqs = quarters * 2 * seq_dev
    column_sums = [jnp.sum(grads[j].astype(F32), axis=0) for j in range(seq_dev)]
    shift_part = jnp.sum(to_first, axis=0) + sum(
        against(column_sums[j][None].astype(F32), triples[j].astype(F32))[0]
        for j in range(seq_dev)
    )
    hot = (jnp.arange(seqs) == dp_index * seq_dev + which).astype(F32)
    shift_rows = hot[:, None] * shift_part[None, :]
    squares = jnp.stack([jnp.sum(jnp.sum(x * x, axis=1) * valid) for x in (stream, branch, feed)])
    table = hot[:, None] * squares[None, :]
    steps_hot = (
        jnp.arange(seqs)[:, None] == dp_index * seq_dev + jnp.arange(seq_dev)[None, :]
    ).astype(F32)
    steps_all = jnp.sum(steps_hot * timestep.astype(F32)[None, :], axis=1) * (me == 0)
    up_canonical = ordered(grad_up_rel.reshape(quarters, tensor, piece_units), spot)
    up_canonical = up_canonical.transpose(1, 0, 2).reshape(tensor, half_units)
    full_up = jnp.zeros((tensor, 2, half_units), F32)
    full_qv = jnp.zeros((tensor, 2, local), F32)
    for index, (k, j) in enumerate(offsets):
        at = ((which + j) % seq_dev) * subs + (sub + k) % subs
        row = jnp.where(jnp.arange(2)[:, None] == core, up_canonical[index][None], 0.0)
        full_up = lax.dynamic_update_slice_in_dim(full_up, row[None], at, 0)
        if k == 0:
            value = column_sums[j].reshape(3, local)
            value = jnp.stack([value[0], value[2]])
            full_qv = lax.dynamic_update_slice_in_dim(full_qv, value[None], at, 0)

    vectors = [
        grad_first_gain,
        grad_first_shift,
        grad_output_bias,
        grad_down_bias,
        grad_second_gain,
        grad_second_shift,
        full_up.reshape(-1),
        shift_rows.reshape(-1),
        full_qv.reshape(-1),
        table.reshape(-1),
        steps_all,
    ]
    packed = jnp.concatenate(vectors)
    packed = jnp.pad(packed, (0, -packed.shape[0] % width)).reshape(-1, width)
    units_all, triple_all, out_all, packed, up_all = sum_all(
        plane, seq_dev, units_sum, triple_parts[1], triple_parts[0], out_total, packed, away + [stream_own]
    )
    grad_up_weight = up_all
    if up_all.ndim > 2:
        grad_up_weight = jnp.concatenate(
            [up_all[half, place] for half in range(2) for place in range(quarters)], axis=1
        )
    grad_down_weight = units_all[1].reshape(units, width).astype(F32)
    grad_output_weight = out_all.reshape(local, width).astype(F32)
    triple_all = triple_all.reshape(width, 3 * local)
    grad_triple = jnp.stack([triple_all[:, i * local : (i + 1) * local] for i in range(3)])
    grad_triple = grad_triple.astype(F32).transpose(1, 0, 2)
    input_gradient = (stream_own + sum(wide(x) for x in away)).astype(LOW)
    packed = packed.reshape(-1)
    got, at = [], 0
    for vector in vectors:
        got.append(packed[at : at + vector.shape[0]])
        at += vector.shape[0]
    full_up = pick(got[6].reshape(tensor, units), me)
    shift_grad = got[7].reshape(seqs, width)
    grad_query_value = pick(got[8].reshape(tensor, 2, local), me)
    table, steps_all = got[9].reshape(seqs, 3), got[10]
    grad_time_bias = jnp.sum(shift_grad, axis=0)
    embedded_all = sinusoid(steps_all, width).astype(LOW).astype(F32)
    grad_time_weight = lax.dot_general(
        embedded_all, shift_grad, TN, precision=lax.Precision.HIGHEST, preferred_element_type=F32
    )
    own_table = lax.dynamic_slice_in_dim(table, dp_index * seq_dev, seq_dev, 0)
    root_squares = jnp.sqrt(own_table / (lengths.astype(F32)[:, None] * width) + STAT_EPS)
    return (
        block_output,
        input_gradient,
        root_squares,
        grad_time_weight,
        grad_time_bias,
        grad_triple,
        grad_query_value,
        grad_output_weight,
        got[2],
        got[0],
        got[1],
        grad_up_weight,
        full_up,
        grad_down_weight,
        got[3],
        got[4],
        got[5],
    )


def solution(mesh):
    tensor = mesh.shape["tensor"]
    spots = mesh.shape["dp"] // 2
    plane = tuple(f"plane{i}" for i in range(spots.bit_length() - 1))
    fine = Mesh(
        mesh.devices.reshape((2,) * len(plane) + (2, tensor)), plane + ("core", "tensor")
    )
    dp = plane + ("core",)
    row = P(dp + ("tensor",), None)
    in_specs = (
        row,
        P(dp),
        P(dp),
        P(),
        P(),
        P(None, None, "tensor"),
        P(None, "tensor"),
        P("tensor", None),
        P(),
        P(),
        P(),
        P(None, "tensor"),
        P("tensor"),
        P("tensor", None),
        P(),
        P(),
        P(),
        row,
    )
    out_specs = (
        row,
        row,
        P(dp, None),
        P(),
        P(),
        P(None, None, "tensor"),
        P(None, "tensor"),
        P("tensor", None),
        P(),
        P(),
        P(),
        P(None, "tensor"),
        P("tensor"),
        P("tensor", None),
        P(),
        P(),
        P(),
    )
    return jax.shard_map(
        functools.partial(on_device, plane),
        mesh=fine,
        in_specs=in_specs,
        out_specs=out_specs,
        check_vma=False,
    )
```

```python
import functools
import math

import jax
import jax.numpy as jnp
from jax import lax
from jax.experimental import pallas as pl
from jax.experimental.pallas import tpu as pltpu
from jax.sharding import Mesh
from jax.sharding import PartitionSpec as P

HD = 64
LEN = 1024
NORM_EPS = 1e-05
STAT_EPS = 1e-06
MASKED = -1e30
LOW = jnp.bfloat16
F32 = jnp.float32
NT = (((1,), (1,)), ((), ()))
TN = (((0,), (0,)), ((), ()))


def sinusoid(steps, width):
    half = width // 2
    rates = jnp.exp(-math.log(10000.0) * jnp.arange(half).astype(F32) / half)
    angles = steps.astype(F32)[:, None] * rates[None, :]
    return jnp.concatenate([jnp.sin(angles), jnp.cos(angles)], axis=1)


def plain(left, right):
    return jnp.dot(left, right, preferred_element_type=F32)


def inner(left, right):
    return lax.dot_general(left, right, TN, preferred_element_type=F32)


def against(left, right):
    return lax.dot_general(left, right, NT, preferred_element_type=F32)


def norm_forward(total, gain, shift):
    middle = jnp.mean(total, axis=-1, keepdims=True)
    centred = total - middle
    spread = jnp.mean(centred * centred, axis=-1, keepdims=True)
    factor = lax.rsqrt(spread + NORM_EPS)
    normed = centred * factor
    return (normed * gain + shift, normed, factor)


def norm_backward(upstream, normed, factor, gain):
    pushed = upstream * gain
    first = jnp.mean(pushed, axis=-1, keepdims=True)
    second = jnp.mean(pushed * normed, axis=-1, keepdims=True)
    return (
        factor * (pushed - first - normed * second),
        jnp.sum(upstream * normed, axis=0),
        jnp.sum(upstream, axis=0),
    )


def split3(x):
    hi = x.astype(LOW)
    rest = x - hi.astype(F32)
    mid = rest.astype(LOW)
    return hi, mid, (rest - mid.astype(F32)).astype(LOW)


def extra_lanes(parts, one, count):
    lane = lax.broadcasted_iota(jnp.int32, (count, HD), 1)
    out = jnp.where(lane == len(parts), 1.0, 0.0) if one else jnp.zeros((count, HD), F32)
    for index, part in enumerate(parts):
        out = jnp.where(lane == index, jnp.broadcast_to(part.astype(F32), (count, HD)), out)
    return out.astype(LOW)


def head(x, h):
    return x[:, h * HD : (h + 1) * HD]


def attend_kernel(rows, mask_ref, q_ref, k_ref, v_ref, context_ref, log_ref):
    count = q_ref.shape[0]
    mask = mask_ref[...]
    keys = k_ref[...].astype(LOW)
    values = v_ref[...].astype(LOW)
    for start in range(0, count, rows):
        part = slice(start, start + rows)
        queries = q_ref[part].astype(LOW) * LOW(HD**-0.5)
        contexts, logs = [], []
        for h in range(2):
            scores = lax.dot_general(
                head(queries, h), head(keys, h), NT, preferred_element_type=F32
            )
            scores = scores + mask
            highest = jnp.max(scores, axis=1, keepdims=True)
            probs = jnp.exp(scores - highest)
            total = jnp.sum(probs, axis=1, keepdims=True)
            contexts.append(plain(probs.astype(LOW), head(values, h)) / total)
            logs.append(jnp.broadcast_to(highest + jnp.log(total), (rows, HD)))
        context_ref[part] = jnp.concatenate(contexts, axis=1)
        log_ref[part] = jnp.concatenate(logs, axis=1)


def attend(projected, mask_row):
    count, width = projected.shape
    local = width // 3
    pairs = local // (2 * HD)
    block = lambda which: pl.BlockSpec((count, 2 * HD), lambda p: (0, which * pairs + p))
    return pl.pallas_call(
        functools.partial(attend_kernel, 512),
        grid=(pairs,),
        in_specs=[pl.BlockSpec((1, count), lambda p: (0, 0)), block(0), block(1), block(2)],
        out_specs=[block(0)] * 2,
        out_shape=[jax.ShapeDtypeStruct((count, local), F32)] * 2,
        compiler_params=pltpu.CompilerParams(vmem_limit_bytes=40 << 20),
        cost_estimate=pl.CostEstimate(
            flops=16 * count * count * local,
            bytes_accessed=20 * count * local,
            transcendentals=count * count * local // HD,
        ),
    )(mask_row, projected, projected, projected)


def attend_back_kernel(
    rows, mask_ref, q_ref, k_ref, v_ref, context_ref, log_ref, grad_ref, dq_ref, dk_ref, dv_ref
):
    count = k_ref.shape[0]
    lane = lax.broadcasted_iota(jnp.int32, (count, HD), 1)
    three = jnp.where(lane < 3, 1.0, 0.0)
    key_extra = jnp.where(lane == 3, jnp.broadcast_to(mask_ref[...], (count, HD)), three)
    key_extra = key_extra.astype(LOW)
    value_extra = three.astype(LOW)
    queries = q_ref[...].astype(LOW) * LOW(HD**-0.5)
    keys = k_ref[...].astype(LOW)
    values = v_ref[...].astype(LOW)
    logs = log_ref[...]
    grads = grad_ref[...]
    dots = grads * context_ref[...]
    grads = grads.astype(LOW)
    kx, vx, qx, gx, dq = [], [], [], [], [None, None]
    for h in range(2):
        extra = extra_lanes(split3(-logs[:, h * HD : h * HD + 1]), True, count)
        qx.append(jnp.concatenate([head(queries, h), extra], axis=1))
        row_dot = jnp.sum(head(dots, h), axis=1, keepdims=True)
        extra = extra_lanes(split3(-row_dot), False, count)
        gx.append(jnp.concatenate([head(grads, h), extra], axis=1))
        kx.append(jnp.concatenate([head(keys, h), key_extra], axis=1))
        vx.append(jnp.concatenate([head(values, h), value_extra], axis=1))
    for start in range(0, count, rows):
        part = slice(start, start + rows)
        dk, dv = [], []
        for h in range(2):
            probs = jnp.exp(lax.dot_general(kx[h][part], qx[h], NT, preferred_element_type=F32))
            pushed = lax.dot_general(vx[h][part], gx[h], NT, preferred_element_type=F32)
            scores_grad = (probs * pushed).astype(LOW)
            dv.append(plain(probs.astype(LOW), gx[h])[:, :HD])
            dk.append(plain(scores_grad, qx[h])[:, :HD])
            more = lax.dot_general(scores_grad, kx[h][part], TN, preferred_element_type=F32)
            dq[h] = more if start == 0 else dq[h] + more
        dk_ref[part] = jnp.concatenate(dk, axis=1)
        dv_ref[part] = jnp.concatenate(dv, axis=1)
    dq_ref[...] = jnp.concatenate([x[:, :HD] for x in dq], axis=1) * HD**-0.5


def attend_back(projected, mask_column, context, log_total, grad):
    count, width = projected.shape
    local = width // 3
    pairs = local // (2 * HD)
    block = lambda which: pl.BlockSpec((count, 2 * HD), lambda p: (0, which * pairs + p))
    return pl.pallas_call(
        functools.partial(attend_back_kernel, 512),
        grid=(pairs,),
        in_specs=[pl.BlockSpec((count, 1), lambda p: (0, 0)), block(0), block(1), block(2)]
        + [block(0)] * 3,
        out_specs=[block(0)] * 3,
        out_shape=[jax.ShapeDtypeStruct((count, local), F32)] * 3,
        compiler_params=pltpu.CompilerParams(vmem_limit_bytes=50 << 20),
        cost_estimate=pl.CostEstimate(
            flops=40 * count * count * local,
            bytes_accessed=40 * count * local,
            transcendentals=count * count * local // HD,
        ),
    )(mask_column, projected, projected, projected, context, log_total, grad)


class Wires:
    def __init__(self, plane, subs, seq_dev, send_sems, recv_sems):
        self.plane, self.subs, self.seq_dev = plane, subs, seq_dev
        self.send_sems, self.recv_sems, self.sent = send_sems, recv_sems, []
        self.bits = [lax.axis_index(name) for name in plane]
        self.core = lax.axis_index("core")
        me = lax.axis_index("tensor")
        self.sub, self.which = lax.rem(me, subs), lax.div(me, subs)
        self.quarters = 2 ** len(plane)

    def spot(self, mask=0):
        total, count = 0, len(self.plane)
        for i, bit in enumerate(self.bits):
            flip = (mask >> (count - 1 - i)) & 1
            total = total + (1 - bit if flip else bit) * 2 ** (count - 1 - i)
        return total

    def at_plane(self, mask):
        count = len(self.plane)
        return {
            name: 1 - bit
            for i, (name, bit) in enumerate(zip(self.plane, self.bits))
            if (mask >> (count - 1 - i)) & 1
        }

    def at_core(self):
        return {"core": 1 - self.core}

    def at_member(self, k, j):
        return {
            "tensor": lax.rem(self.which + j + self.seq_dev, self.seq_dev) * self.subs
            + lax.rem(self.sub + k + self.subs, self.subs)
        }

    def greet(self, targets):
        barrier = pltpu.get_barrier_semaphore()
        for target in targets:
            pl.semaphore_signal(barrier, inc=1, device_id=target, device_id_type=pl.DeviceIdType.MESH)
        pl.semaphore_wait(barrier, len(targets))

    def send(self, src, dst, target):
        index = len(self.sent)
        copy = pltpu.make_async_remote_copy(
            src_ref=src,
            dst_ref=dst,
            send_sem=self.send_sems.at[index],
            recv_sem=self.recv_sems.at[index],
            device_id=target,
            device_id_type=pl.DeviceIdType.MESH,
        )
        copy.start()
        self.sent.append(copy)
        return copy

    def finish(self):
        for copy in self.sent:
            copy.wait_send()


def wide(x):
    return x.astype(F32)


def sum_kernel(
    plane, subs, seq_dev, ordering, units, later, now, output, vectors, *refs
):
    (
    units_out, triple_out, output_out, vectors_out, up_out,
    units_z, later_core, now_core, output_core, later_half, now_half, output_half,
    later_plane, now_plane, output_plane, triple_z, output_z, triple_mine, output_mine, units_away,
    vectors_core, vectors_plane, vectors_z, vectors_one, vectors_two, send_sems, recv_sems,
    ) = refs[ordering:]
    wires = Wires(plane, subs, seq_dev, send_sems, recv_sems)
    quarters, core = wires.quarters, wires.core
    spot = wires.spot()
    offsets = [(k, j) for k in range(subs) for j in range(seq_dev)]
    ahead = range(1, len(offsets))
    masks = range(1, quarters)
    wires.greet(
        [wires.at_core()]
        + [wires.at_plane(mask) for mask in masks]
        + [wires.at_member(k, j) for k, j in offsets[1:]]
    )
    core_got = []
    for source, target in ((later, later_core), (output, output_core), (now, now_core)):
        core_got.append(
            [
                wires.send(source.at[place, 1 - core], target.at[place], wires.at_core())
                for place in range(quarters)
            ]
        )
    vectors_got = wires.send(vectors, vectors_core, wires.at_core())

    inner_count = (subs - 1) * seq_dev

    def units_inside(which):
        return [
            wires.send(
                units.at[which, pl.ds(k * seq_dev, seq_dev)],
                units_z.at[which, pl.ds((k - 1) * seq_dev, seq_dev)],
                wires.at_member(k, 0),
            )
            for k in range(1, subs)
        ]

    def units_part(which, j):
        total = wide(units[which, j])
        for k in range(1, subs):
            total = total + wide(units_z[which, (k - 1) * seq_dev + j])
        return total

    def units_across(which, got):
        for copy in got:
            copy.wait_recv()
        copies = []
        for j in range(1, seq_dev):
            units_away[which, j - 1] = units_part(which, j).astype(LOW)
            copies.append(
                wires.send(
                    units_away.at[which, j - 1],
                    units_z.at[which, inner_count + j - 1],
                    wires.at_member(0, j),
                )
            )
        return copies

    units_first = units_inside(0)
    plane_got = []
    for got, source, received, half, target in (
        (core_got[0], later, later_core, later_half, later_plane),
        (core_got[1], output, output_core, output_half, output_plane),
        (core_got[2], now, now_core, now_half, now_plane),
    ):
        for copy in got:
            copy.wait_recv()
        for place in range(quarters):
            half[place] = (wide(source[place, core]) + wide(received[place])).astype(LOW)
        plane_got.append(
            [
                wires.send(half.at[wires.spot(mask)], target.at[mask - 1], wires.at_plane(mask))
                for mask in masks
            ]
        )
    vectors_got.wait_recv()
    vectors_one[...] = vectors[...] + vectors_core[...]
    vectors_got = [
        wires.send(vectors_one, vectors_plane.at[mask - 1], wires.at_plane(mask)) for mask in masks
    ]
    last, up_crossed, passed = [], [], []

    up_order = [1 << i for i in range(len(plane))]

    def spread(slot, crossed, mask, order):
        ref = slot(wires.spot(mask))
        for i, bit in enumerate(order):
            got = wires.send(ref, ref, wires.at_plane(bit))
            passed.append((slot, crossed, mask | bit, order[i + 1 :], got))
        crossed.append((mask, wires.send(ref, ref, wires.at_core())))

    def hand_over(count=None):
        while passed and count != 0:
            slot, crossed, mask, order, copy = passed.pop(0)
            copy.wait_recv()
            spread(slot, crossed, mask, order)
            count = None if count is None else count - 1

    def units_whole(which):
        for copy in units_got[which]:
            copy.wait_recv()
        total = units_part(which, 0)
        for j in range(1, seq_dev):
            total = total + wide(units_z[which, inner_count + j - 1])
        units_out[which, core, spot] = total.astype(LOW)
        spread(
            lambda place: units_out.at[which, core, place],
            last if which else up_crossed,
            0,
            up_order[::-1] if which else up_order,
        )

    units_got = [units_across(0, units_first)]
    units_second = units_inside(1)
    units_whole(0)
    units_got.append(units_across(1, units_second))
    for copy in plane_got[0]:
        copy.wait_recv()
    total = wide(later_half[spot])
    for mask in masks:
        total = total + wide(later_plane[mask - 1])
    triple_mine[...] = total.astype(LOW)
    triple_got = [wires.send(triple_mine, triple_z, wires.at_member(0, 1))]
    for copy in plane_got[1]:
        copy.wait_recv()
    total = wide(output_half[spot])
    for mask in masks:
        total = total + wide(output_plane[mask - 1])
    output_mine[...] = total.astype(LOW)
    output_got = [
        wires.send(output_mine.at[z], output_z.at[z - 1], wires.at_member(*offsets[z])) for z in ahead
    ]
    for copy in vectors_got:
        copy.wait_recv()
    total = vectors_one[...]
    for mask in masks:
        total = total + vectors_plane[mask - 1]
    vectors_two[...] = total
    vectors_got = [
        wires.send(vectors_two, vectors_z.at[z - 1], wires.at_member(*offsets[z])) for z in ahead
    ]
    hand_over(len(plane))
    units_whole(1)
    for copy in plane_got[2]:
        copy.wait_recv()
    for copy in triple_got:
        copy.wait_recv()
    total = wide(now_half[spot]) + wide(triple_z[...])
    for mask in masks:
        total = total + wide(now_plane[mask - 1])
    triple_out[spot, core] = total.astype(LOW)
    spread(lambda place: triple_out.at[place, core], last, 0, up_order)
    for copy in output_got:
        copy.wait_recv()
    total = wide(output_mine[0])
    for z in ahead:
        total = total + wide(output_z[z - 1])
    output_out[spot, core] = total.astype(LOW)
    spread(lambda place: output_out.at[place, core], last, 0, up_order[::-1])
    hand_over()

    def place_up(half, mask):
        place = wires.spot(mask)
        block = wide(units_out[0, half, place]).T
        wide_block = block.shape[1]
        if len(up_out.shape) == 2:
            first = pl.multiple_of((half * quarters + place) * wide_block, wide_block)
            up_out[:, pl.ds(first, wide_block)] = block
        else:
            up_out[half, place] = block

    for mask, copy in up_crossed:
        place_up(core, mask)
        copy.wait_recv()
        place_up(1 - core, mask)
    for copy in vectors_got:
        copy.wait_recv()
    total = vectors_two[...]
    for z in ahead:
        total = total + vectors_z[z - 1]
    vectors_out[...] = total
    hand_over()
    for _, copy in last:
        copy.wait_recv()
    wires.finish()


def sum_all(plane, seq_dev, units, later, now, output, vectors, before):
    tensor, quarters = lax.axis_size("tensor"), 2 ** len(plane)
    subs, masks = tensor // seq_dev, quarters - 1
    piece, share, out_share = units.shape[2:], later.shape[2:], output.shape[3:]
    up_shape = (piece[1], 2 * quarters * piece[0])
    if piece[0] % 128:
        up_shape = (2, quarters, piece[1], piece[0])
    low = lambda *shape: pltpu.VMEM(shape, LOW)
    full = lambda *shape: pltpu.VMEM(shape + vectors.shape, F32)
    copies = (
        3 * quarters + 1 + 2 * (tensor - 1) + 3 * masks + masks + 1 + 2 * (tensor - 1)
        + 4 * (masks + 1 + masks)
    )
    return pl.pallas_call(
        functools.partial(sum_kernel, plane, subs, seq_dev, len(before)),
        in_specs=[pl.BlockSpec(memory_space=pltpu.VMEM)] * 5
        + [pl.BlockSpec(memory_space=pl.ANY)] * len(before),
        out_specs=[pl.BlockSpec(memory_space=pltpu.VMEM)] * 5,
        out_shape=[
            jax.ShapeDtypeStruct((2, 2, quarters) + piece, LOW),
            jax.ShapeDtypeStruct((quarters, 2) + share, LOW),
            jax.ShapeDtypeStruct((quarters, 2) + out_share, LOW),
            jax.ShapeDtypeStruct(vectors.shape, F32),
            jax.ShapeDtypeStruct(up_shape, F32),
        ],
        scratch_shapes=[
            low(2, tensor - 1, *piece),
            low(quarters, *share),
            low(quarters, *share),
            low(quarters, tensor, *out_share),
            low(quarters, *share),
            low(quarters, *share),
            low(quarters, tensor, *out_share),
            low(masks, *share),
            low(masks, *share),
            low(masks, tensor, *out_share),
            low(*share),
            low(tensor - 1, *out_share),
            low(*share),
            low(tensor, *out_share),
            low(2, seq_dev - 1, *piece),
            full(),
            full(masks),
            full(tensor - 1),
            full(),
            full(),
            pltpu.SemaphoreType.DMA((copies,)),
            pltpu.SemaphoreType.DMA((copies,)),
        ],
        compiler_params=pltpu.CompilerParams(
            collective_id=1, has_side_effects=True, vmem_limit_bytes=48 << 20
        ),
        cost_estimate=pl.CostEstimate(flops=1 << 24, bytes_accessed=1 << 27, transcendentals=0),
    )(units, later, now, output, vectors, *before)


def gather_kernel(
    plane, subs, seq_dev, stream, triple, output, units, small,
    stream_out, triple_out, output_out, early_out, rest_out, small_out, send_sems, recv_sems,
):
    wires = Wires(plane, subs, seq_dev, send_sems, recv_sems)
    quarters, core = wires.quarters, wires.core
    offsets = [(k, j) for k in range(subs) for j in range(seq_dev)]
    ahead = range(1, len(offsets))
    masks = range(1, quarters)
    wires.greet(
        [wires.at_core()]
        + [wires.at_plane(mask) for mask in masks]
        + [wires.at_member(k, j) for k, j in offsets[1:]]
    )
    mine = 2 * wires.spot() + core
    share, out_share = triple_out.shape[1:], output_out.shape[2:]
    back = lambda z: wires.at_member(-offsets[z][0], -offsets[z][1])
    triple_got = wires.send(triple.at[mine], triple_out.at[mine], back(1))
    output_got = [wires.send(output.at[mine], output_out.at[z - 1, mine], back(z)) for z in ahead]
    small_got = [wires.send(small, small_out.at[z - 1], back(z)) for z in ahead]
    triple_got.wait_recv()
    stream_got = [wires.send(stream, stream_out.at[k - 1], wires.at_member(-k, 0)) for k in range(1, subs)]
    last, passed = [], []
    ref = triple_out.at[mine]
    for mask in masks:
        passed.append((mask, wires.send(ref, ref, wires.at_plane(mask))))
    last.append(wires.send(ref, ref, wires.at_core()))
    for copy in output_got:
        copy.wait_recv()
    early_got = wires.send(units, early_out.at[0], back(1))
    output_passed = []
    for mask in masks:
        for z in ahead:
            ref = output_out.at[z - 1, mine]
            output_passed.append((z, mask, wires.send(ref, ref, wires.at_plane(mask))))
    for z in ahead:
        ref = output_out.at[z - 1, mine]
        last.append(wires.send(ref, ref, wires.at_core()))
    for mask, copy in passed:
        copy.wait_recv()
        ref = triple_out.at[2 * wires.spot(mask) + core]
        last.append(wires.send(ref, ref, wires.at_core()))
    early_got.wait_recv()
    rest_got = [wires.send(units, rest_out.at[z - 2], back(z)) for z in ahead if z > 1]
    for mask in masks:
        last.append(wires.send(early_out.at[0], early_out.at[mask], wires.at_plane(mask)))
    for z, mask, copy in output_passed:
        copy.wait_recv()
        ref = output_out.at[z - 1, 2 * wires.spot(mask) + core]
        last.append(wires.send(ref, ref, wires.at_core()))
    for copy in small_got + stream_got + rest_got + last:
        copy.wait_recv()
    wires.finish()


def gather_all(plane, seq_dev, stream, triple, output, units, small):
    tensor, quarters = lax.axis_size("tensor"), 2 ** len(plane)
    subs, masks = tensor // seq_dev, quarters - 1
    others = tensor - 1
    copies = 2 + subs - 1 + 2 * others + 2 * quarters - 1 + 2 * others * quarters + others + masks
    return pl.pallas_call(
        functools.partial(gather_kernel, plane, subs, seq_dev),
        in_specs=[pl.BlockSpec(memory_space=pltpu.VMEM)] * 5,
        out_specs=[pl.BlockSpec(memory_space=pltpu.VMEM)] * 6,
        out_shape=[
            jax.ShapeDtypeStruct((subs - 1,) + stream.shape, LOW),
            jax.ShapeDtypeStruct(triple.shape, LOW),
            jax.ShapeDtypeStruct((others,) + output.shape, LOW),
            jax.ShapeDtypeStruct((quarters,) + units.shape, LOW),
            jax.ShapeDtypeStruct((others - 1,) + units.shape, LOW),
            jax.ShapeDtypeStruct((others,) + small.shape, F32),
        ],
        scratch_shapes=[
            pltpu.SemaphoreType.DMA((copies,)),
            pltpu.SemaphoreType.DMA((copies,)),
        ],
        compiler_params=pltpu.CompilerParams(
            collective_id=2, has_side_effects=True, vmem_limit_bytes=32 << 20
        ),
        cost_estimate=pl.CostEstimate(flops=1 << 20, bytes_accessed=1 << 27, transcendentals=0),
    )(stream, triple, output, units, small)


def gaussian_pair(value):
    cumulative = 0.5 * (1.0 + jax.scipy.special.erf(value * (1.0 / math.sqrt(2.0))))
    slope = cumulative + value * jnp.exp(-0.5 * value * value) * (1.0 / math.sqrt(2.0 * math.pi))
    return (value * cumulative).astype(LOW), slope.astype(LOW)


def on_device(
    plane,
    stream_in,
    timestep,
    lengths,
    time_weight,
    time_bias,
    triple_weight,
    query_value_bias,
    output_weight,
    output_bias,
    first_gain,
    first_shift,
    up_weight,
    up_bias,
    down_weight,
    down_bias,
    second_gain,
    second_shift,
    cotangent,
):
    rows, width = stream_in.shape
    seq_dev = timestep.shape[0]
    tensor = lax.axis_size("tensor")
    subs = tensor // seq_dev
    local = triple_weight.shape[2]
    units = up_weight.shape[1]
    half_units = units // 2
    quarters = 2 ** len(plane)
    piece_units = half_units // quarters
    me = lax.axis_index("tensor")
    core = lax.axis_index("core")
    spot = lax.axis_index(plane)
    sub = me % subs
    which = me // subs
    offsets = [(k, j) for k in range(subs) for j in range(seq_dev)]
    others = offsets[1:]

    def member(i, k, j):
        return ((i // subs + j) % seq_dev) * subs + (i % subs + k) % subs

    def fetch(x, k, j):
        return lax.ppermute(x, "tensor", [(member(i, k, j), i) for i in range(tensor)])

    def send(x, k, j):
        return lax.ppermute(x, "tensor", [(i, member(i, k, j)) for i in range(tensor)])

    def swap(x, axis):
        return lax.ppermute(x, axis, [(0, 1), (1, 0)])

    def across(x, mask):
        return lax.ppermute(x, plane, [(i, i ^ mask) for i in range(quarters)])

    def pick(x, index, axis=0):
        return lax.dynamic_index_in_dim(x, index, axis, keepdims=False)

    def tie(x, *before):
        return lax.optimization_barrier((x,) + before)[0]

    def ordered(parts, index):
        parts = jnp.stack(parts) if isinstance(parts, (list, tuple)) else parts
        return jnp.stack([pick(parts, index ^ m) for m in range(parts.shape[0])])

    triple_three = triple_weight.transpose(1, 0, 2)
    triple_own = jnp.concatenate([triple_three[i] for i in range(3)], axis=1)
    part = width // (2 * quarters)
    out_part = local // (2 * quarters)
    up_half = lax.dynamic_slice_in_dim(up_weight, core * half_units, half_units, 1).T
    down_half = lax.dynamic_slice_in_dim(down_weight, core * half_units, half_units, 0)
    units_mine = [
        ordered(x.reshape(quarters, piece_units, width), spot) for x in (up_half, down_half)
    ]
    small = jnp.concatenate([up_bias, query_value_bias.reshape(-1)])
    pad = -small.shape[0] % 1024
    raw, triple_got, out_got, early, rest, small_got = gather_all(
        plane,
        seq_dev,
        stream_in,
        triple_own.reshape(2 * quarters, part, 3 * local),
        output_weight.reshape(2 * quarters, out_part, width),
        jnp.stack([units_mine[0][0], units_mine[1][0]]),
        jnp.pad(small, (0, pad)).reshape(-1, 128),
    )
    raw = [stream_in] + [raw[k] for k in range(subs - 1)]
    triples = [triple_own, triple_got.reshape(width, 3 * local)]
    out_got = out_got.reshape(tensor - 1, local, width)
    out_full = jnp.concatenate([output_weight[None], out_got]).reshape(tensor * local, width)
    small_of = {(0, 0): small}
    for z, (k, j) in enumerate(others):
        small_of[(k, j)] = small_got[z].reshape(-1)[: small.shape[0]]
    rest_of = [rest] + [across(rest, m) for m in range(1, quarters)]

    def all_rows(which):
        full = []
        for m in range(quarters):
            full += [units_mine[which][m][None], early[m, which][None], rest_of[m][:, which]]
        return jnp.concatenate(full, axis=0).reshape(-1, width)

    up_rows, down_rows = all_rows(0), all_rows(1)

    embedded_own = sinusoid(timestep, width).astype(LOW)
    shift_own = plain(embedded_own, time_weight) + time_bias
    shift_row = pick(shift_own, which)
    limit = pick(lengths, which)
    stream = stream_in.astype(F32) + shift_row
    stream_low = (jnp.concatenate(raw, axis=0).astype(F32) + shift_row).astype(LOW)
    place = (jnp.arange(LEN, dtype=jnp.int32) + sub * rows) % LEN
    mask = jnp.where(place < limit, 0.0, MASKED).astype(F32)
    mask_row, mask_column = mask[None, :], mask[:, None]
    valid = (place[:rows] < limit).astype(F32)

    qv = [small_of[(0, j)][units:].reshape(2, local) for j in range(seq_dev)]
    projected, context, log_total = [], [], []
    for j in range(seq_dev):
        bias = jnp.concatenate([qv[j][0], jnp.zeros((local,), F32), qv[j][1]])
        projected.append(plain(stream_low, triples[j]) + bias)
        here = attend(projected[j], mask_row)
        context.append(here[0])
        log_total.append(here[1])
    block = lambda x, k: x[k * rows : (k + 1) * rows]
    columns = []
    for k in range(subs):
        back = (subs - k) % subs
        for j in range(seq_dev):
            mine = block(context[j], back).astype(LOW)
            columns.append(mine if k == 0 else send(mine, back, 0))
    context_own = jnp.concatenate(columns, axis=1)

    branch = plain(context_own, out_full) + output_bias
    middle, normed_first, factor_first = norm_forward(stream + branch, first_gain, first_shift)
    middle_low = middle.astype(LOW)

    bias_all = jnp.stack([small_of[o][:units] for o in offsets])
    bias_half = lax.dynamic_slice_in_dim(bias_all, core * half_units, half_units, 1)
    bias_rel = ordered(
        bias_half.reshape(tensor, quarters, piece_units).transpose(1, 0, 2), spot
    ).reshape(-1)
    both = jnp.concatenate([middle_low, swap(middle_low, "core")], axis=0)
    active, slope = lax.optimization_barrier(
        gaussian_pair(against(both, up_rows) + bias_rel)
    )
    feed_other = plain(active[rows:], down_rows).astype(LOW)
    feed = plain(active[:rows], down_rows) + swap(feed_other, "core").astype(F32) + down_bias
    result, normed_second, factor_second = norm_forward(middle + feed, second_gain, second_shift)
    block_output = result.astype(LOW)

    to_second, grad_second_gain, grad_second_shift = norm_backward(
        cotangent.astype(F32), normed_second, factor_second, second_gain
    )
    feed_grad = to_second.astype(LOW)
    grad_down_bias = jnp.sum(feed_grad.astype(F32), axis=0)
    feed_grad_both = jnp.concatenate([feed_grad, swap(feed_grad, "core")], axis=0)

    def by_mask(total):
        shaped = total.reshape(quarters, tensor, piece_units, width)
        return {m: shaped[m] for m in range(quarters)}

    down_total = by_mask(inner(active, feed_grad_both).astype(LOW))
    before_grad = (against(feed_grad_both, down_rows) * slope.astype(F32)).astype(LOW)
    up_total = by_mask(inner(before_grad, both).astype(LOW))
    units_sum = wide(jnp.stack([up_total[0], down_total[0]]))
    for m in range(1, quarters):
        units_sum = units_sum + wide(across(jnp.stack([up_total[m], down_total[m]]), m))
    units_sum = units_sum.astype(LOW)
    grad_up_rel = jnp.sum(before_grad.astype(F32), axis=0)
    middle_other = plain(before_grad[rows:], up_rows).astype(LOW)
    middle_grad = (
        to_second + plain(before_grad[:rows], up_rows) + swap(middle_other, "core").astype(F32)
    )

    to_first, grad_first_gain, grad_first_shift = norm_backward(
        middle_grad, normed_first, factor_first, first_gain
    )
    branch_grad = to_first.astype(LOW)
    grad_output_bias = jnp.sum(branch_grad.astype(F32), axis=0)
    context_grad = against(branch_grad, out_full).astype(LOW)
    shaped = context_grad.reshape(rows, subs, seq_dev, local)
    incoming = [None] * seq_dev
    for j in reversed(range(seq_dev)):
        parts = []
        for k in range(subs):
            back = (subs - k) % subs
            mine = shaped[:, back, j]
            parts.append(mine if k == 0 else send(mine, back, 0))
        incoming[j] = jnp.concatenate(parts, axis=0).astype(F32)

    grads = [None] * seq_dev
    for j in reversed(range(seq_dev)):
        here = attend_back(projected[j], mask_column, context[j], log_total[j], incoming[j])
        grads[j] = jnp.concatenate(here, axis=1).astype(LOW)
    triple_parts = [
        inner(stream_low, grads[j]).astype(LOW).reshape(quarters, 2, part, 3 * local)
        for j in range(seq_dev)
    ]
    out_total = inner(context_own, branch_grad).astype(LOW)
    out_total = out_total.reshape(tensor, quarters, 2, out_part, width).transpose(1, 2, 0, 3, 4)
    away = [
        send(
            sum(against(block(grads[j], k), triples[j]) for j in range(seq_dev)).astype(LOW), k, 0
        )
        for k in range(1, subs)
    ]
    stream_own = to_first + sum(
        against(block(grads[j], 0), triples[j]) for j in range(seq_dev)
    )

    dp_index = spot * 2 + core
    seqs = quarters * 2 * seq_dev
    column_sums = [jnp.sum(grads[j].astype(F32), axis=0) for j in range(seq_dev)]
    shift_part = jnp.sum(to_first, axis=0) + sum(
        against(column_sums[j][None].astype(F32), triples[j].astype(F32))[0]
        for j in range(seq_dev)
    )
    hot = (jnp.arange(seqs) == dp_index * seq_dev + which).astype(F32)
    shift_rows = hot[:, None] * shift_part[None, :]
    squares = jnp.stack([jnp.sum(jnp.sum(x * x, axis=1) * valid) for x in (stream, branch, feed)])
    table = hot[:, None] * squares[None, :]
    steps_hot = (
        jnp.arange(seqs)[:, None] == dp_index * seq_dev + jnp.arange(seq_dev)[None, :]
    ).astype(F32)
    steps_all = jnp.sum(steps_hot * timestep.astype(F32)[None, :], axis=1) * (me == 0)
    up_canonical = ordered(grad_up_rel.reshape(quarters, tensor, piece_units), spot)
    up_canonical = up_canonical.transpose(1, 0, 2).reshape(tensor, half_units)
    full_up = jnp.zeros((tensor, 2, half_units), F32)
    full_qv = jnp.zeros((tensor, 2, local), F32)
    for index, (k, j) in enumerate(offsets):
        at = ((which + j) % seq_dev) * subs + (sub + k) % subs
        row = jnp.where(jnp.arange(2)[:, None] == core, up_canonical[index][None], 0.0)
        full_up = lax.dynamic_update_slice_in_dim(full_up, row[None], at, 0)
        if k == 0:
            value = column_sums[j].reshape(3, local)
            value = jnp.stack([value[0], value[2]])
            full_qv = lax.dynamic_update_slice_in_dim(full_qv, value[None], at, 0)

    vectors = [
        grad_first_gain,
        grad_first_shift,
        grad_output_bias,
        grad_down_bias,
        grad_second_gain,
        grad_second_shift,
        full_up.reshape(-1),
        shift_rows.reshape(-1),
        full_qv.reshape(-1),
        table.reshape(-1),
        steps_all,
    ]
    packed = jnp.concatenate(vectors)
    packed = jnp.pad(packed, (0, -packed.shape[0] % width)).reshape(-1, width)
    units_all, triple_all, out_all, packed, up_all = sum_all(
        plane, seq_dev, units_sum, triple_parts[1], triple_parts[0], out_total, packed, away + [stream_own]
    )
    grad_up_weight = up_all
    if up_all.ndim > 2:
        grad_up_weight = jnp.concatenate(
            [up_all[half, place] for half in range(2) for place in range(quarters)], axis=1
        )
    grad_down_weight = units_all[1].reshape(units, width).astype(F32)
    grad_output_weight = out_all.reshape(local, width).astype(F32)
    triple_all = triple_all.reshape(width, 3 * local)
    grad_triple = jnp.stack([triple_all[:, i * local : (i + 1) * local] for i in range(3)])
    grad_triple = grad_triple.astype(F32).transpose(1, 0, 2)
    input_gradient = (stream_own + sum(wide(x) for x in away)).astype(LOW)
    packed = packed.reshape(-1)
    got, at = [], 0
    for vector in vectors:
        got.append(packed[at : at + vector.shape[0]])
        at += vector.shape[0]
    full_up = pick(got[6].reshape(tensor, units), me)
    shift_grad = got[7].reshape(seqs, width)
    grad_query_value = pick(got[8].reshape(tensor, 2, local), me)
    table, steps_all = got[9].reshape(seqs, 3), got[10]
    grad_time_bias = jnp.sum(shift_grad, axis=0)
    embedded_all = sinusoid(steps_all, width).astype(LOW).astype(F32)
    grad_time_weight = lax.dot_general(
        embedded_all, shift_grad, TN, precision=lax.Precision.HIGHEST, preferred_element_type=F32
    )
    own_table = lax.dynamic_slice_in_dim(table, dp_index * seq_dev, seq_dev, 0)
    root_squares = jnp.sqrt(own_table / (lengths.astype(F32)[:, None] * width) + STAT_EPS)
    return (
        block_output,
        input_gradient,
        root_squares,
        grad_time_weight,
        grad_time_bias,
        grad_triple,
        grad_query_value,
        grad_output_weight,
        got[2],
        got[0],
        got[1],
        grad_up_weight,
        full_up,
        grad_down_weight,
        got[3],
        got[4],
        got[5],
    )


def solution(mesh):
    tensor = mesh.shape["tensor"]
    spots = mesh.shape["dp"] // 2
    plane = tuple(f"plane{i}" for i in range(spots.bit_length() - 1))
    fine = Mesh(
        mesh.devices.reshape((2,) * len(plane) + (2, tensor)), plane + ("core", "tensor")
    )
    dp = plane + ("core",)
    row = P(dp + ("tensor",), None)
    in_specs = (
        row,
        P(dp),
        P(dp),
        P(),
        P(),
        P(None, None, "tensor"),
        P(None, "tensor"),
        P("tensor", None),
        P(),
        P(),
        P(),
        P(None, "tensor"),
        P("tensor"),
        P("tensor", None),
        P(),
        P(),
        P(),
        row,
    )
    out_specs = (
        row,
        row,
        P(dp, None),
        P(),
        P(),
        P(None, None, "tensor"),
        P(None, "tensor"),
        P("tensor", None),
        P(),
        P(),
        P(),
        P(None, "tensor"),
        P("tensor"),
        P("tensor", None),
        P(),
        P(),
        P(),
    )
    return jax.shard_map(
        functools.partial(on_device, plane),
        mesh=fine,
        in_specs=in_specs,
        out_specs=out_specs,
        check_vma=False,
    )
```
